128 devices in a mesh: dp: 4 (over x), expert: 32 (over z, y, core).
Axes of the slice: x: 4, y: 4, z: 4, core: 2. Of those that a mesh axis runs over, the one named last changes fastest.
Arguments:
- latent_rows: bfloat16 [24576, 576], P(('dp', 'expert')), may hold values from -6 to 6
- new_rows: bfloat16 [4, 96, 576], P('dp'), may hold values from -6 to 6
- kv_gain: float32 [512], replicated, may hold values from 0.5 to 1.5
- lengths: int32 [384], replicated, may hold values from 32 to 96, as said below
- owners: int32 [384], replicated, may hold values from 0 to 3, as said below
- queries: bfloat16 [4, 96, 64, 576], P('dp'), may hold values from -300 to 300
- w_uv: bfloat16 [64, 512, 128], P('expert'), may hold values from -0.25 to 0.25
- w_out: bfloat16 [8192, 7168], P('expert'), may hold values from -0.0625 to 0.0625
- resid: bfloat16 [4, 96, 7168], P('dp', 'expert'), may hold values from -6 to 6
- moe_gain: float32 [7168], replicated, may hold values from 0.5 to 1.5
- route_ids: int32 [4, 96, 8], P('dp', 'expert'), may hold values from 0 to 31, all different within a row; in each aligned block of 3 rows (0 to 2, 3 to 5, ..., all dimensions but the last counted through in order) at most 2 rows name the same one
- route_weights: float32 [4, 96, 8], P('dp', 'expert'), may hold values from 0.1 to 0.6
- w_gate: bfloat16 [32, 7168, 1024], P('expert', None, 'dp'), may hold values from -0.0625 to 0.0625
- w_up: bfloat16 [32, 7168, 1024], P('expert', None, 'dp'), may hold values from -0.0625 to 0.0625
- w_down: bfloat16 [32, 1024, 7168], P('expert', 'dp'), may hold values from -0.1875 to 0.1875
Outputs:
- decode_cache: bfloat16 [4, 32, 192, 576], P('dp', 'expert')
- decoded: bfloat16 [4, 96, 7168], P('dp', 'expert')
The draws below stay inside these ranges and needn't reach their ends.
Inputs may be any that keep to these rules, and one draw needn't show every extreme that they name: `lengths`: every length is a positive multiple of 32; together they cover the 24576 prefill rows. `owners`: each group owns exactly 96 requests, of 6144 rows together. `route_ids`: among the 3 tokens of one device, no expert is named by more than 2 tokens.
All inputs are finite; a program needn't handle non-finite values.
Results may differ from the reference program's by a relative error of at most 0.018.
Values may be sent and summed in bfloat16 or wider, within the bound.
No kernel may reach another device: no remote copies, remote signals or barrier semaphores. Data moves between devices by JAX's collectives and lax.ppermute only.
A program may use at most 128 MiB of HBM per device.

```python
import math
import jax
import jax.numpy as jnp
import numpy as np
from jax import lax

D = 7168
LAT = 512
VDIM = 128
TOPK = 8
H = 64
FFX = 1024
PRE_DEV = 192
T_DEV = 3
CW = 576
REQ_G = 96
NREQ = 384
ROWS = 24576
MOSTU = 3
EXPERTS = 32
CAP = 2
N_DP = 4
N_EXPERT = 32


def request_layout(key):
    key_spread, key_order = jax.random.split(key)
    average = PRE_DEV // REQ_G
    half_count = REQ_G // 2
    spread = jax.random.randint(key_spread, (N_DP, half_count), 0, average, dtype=jnp.int32)
    spread = spread.at[:, 0].set(average - 1)
    unit_len = jnp.concatenate([average + spread, average - spread], axis=1).reshape(NREQ)
    group_ids = jnp.repeat(jnp.arange(N_DP, dtype=jnp.int32), REQ_G)
    shuffle = jax.random.permutation(key_order, NREQ)
    return ((unit_len[shuffle] * N_EXPERT).astype(jnp.int32), group_ids[shuffle].astype(jnp.int32))


def draw_lengths(key, part):
    return request_layout(key)[0]


def draw_owners(key, part):
    return request_layout(key)[1]


def draw_queries(key, part):
    key = jax.random.fold_in(key, 7)
    key_base = jax.random.fold_in(key, 0)
    values = jax.random.normal(key_base, (N_DP, REQ_G, H, CW), jnp.float32)
    return jnp.clip(values, -300.0, 300.0).astype(jnp.bfloat16)


def shard_levels(rng, shape, shards, least, high):
    loudness = 1.0
    for dim, shards_of in shards:
        steps = jax.random.uniform(jax.random.fold_in(jax.random.fold_in(rng, 6), dim), (shards_of,), jnp.float32, least / len(shards), high / len(shards))
        loudness = loudness * jnp.repeat(jnp.exp(steps), shape[dim] // shards_of).reshape((-1,) + (1,) * (len(shape) - 1 - dim))
    return loudness


def deal_out(stream_key, own, number, rows, number_of, top, limit, skew):
    order = jax.random.permutation(stream_key, number_of)
    crowded, common = portions_of(number_of, rows * top, limit, skew, True), portions_of(number_of, rows * top, limit, skew, False)
    places = jnp.arange(number_of)

    def named(sizes, offset_by):
        used = int((sizes > 0).sum())
        fixed = max(1, used // 4)
        passed = fixed + (places - fixed + offset_by * (used - fixed)) % max(1, number_of - fixed)
        return jnp.zeros((number_of,), jnp.int32).at[order[jnp.where(places < fixed, places, passed)]].set(jnp.asarray(sizes, jnp.int32))

    sizes = jnp.where(number % 4 == 0, named(crowded, number // 4), named(common, number - number // 4 - 1))
    mixed = jax.random.permutation(jax.random.fold_in(own, 3), number_of)
    giver, taker = mixed[0:number_of // 2 * 2:2], mixed[1:number_of // 2 * 2:2]
    room = jnp.minimum(sizes[giver] - 1, limit - sizes[taker]) // 2
    room = jnp.where((giver == order[0]) | (taker == order[0]) | (sizes[taker] == 0), 0, jnp.maximum(room, 0))
    passed = jax.random.randint(jax.random.fold_in(own, 4), (number_of // 2,), 0, 1 << 20) % (room + 1)
    sizes = sizes.at[giver].add(-passed).at[taker].add(passed)
    labels = jnp.searchsorted(jnp.cumsum(sizes), jnp.arange(rows * top), side="right").astype(jnp.int32)
    listing = labels.reshape(top, rows).T
    listing = listing[jax.random.permutation(jax.random.fold_in(own, 1), rows)]
    offset_by = jax.random.randint(jax.random.fold_in(own, 2), (rows, 1), 0, top)
    return jnp.take_along_axis(listing, (jnp.arange(top)[None, :] + offset_by) % top, axis=1)


def portions_of(number_of, total, limit, slope, full):
    portions = [(1 << 20) // math.isqrt(rank ** slope) + 1 for rank in range(1, number_of + 1)]
    largest = limit if full else min(limit, max(-(-total // number_of), total * portions[0] // sum(portions)))
    least = 1 if total - largest >= number_of - 1 else 0
    counts, rest = [largest] + [least] * (number_of - 1), total - largest - least * (number_of - 1)
    while rest > 0:
        candidates = [i for i in range(1, number_of) if counts[i] < largest] or [i for i in range(1, number_of) if counts[i] < limit]
        pool, budget = sum([portions[i] for i in candidates]), rest
        for i in candidates:
            more = min(limit - counts[i], max(1, budget * portions[i] // pool), rest)
            counts[i] = counts[i] + more
            rest = rest - more
    return np.array(counts)


def bell_draw(own_key, extent, scale, reach, cuts=(), kind=jnp.bfloat16):
    drawn = scale * jax.random.normal(own_key, extent, jnp.float32)
    if cuts:
        drawn = drawn * shard_levels(own_key, extent, cuts, -0.22, 0.18)
    return jnp.clip(drawn, -reach, reach).astype(kind)


def setup_inputs(seed: int = 0) -> dict:
    seeds = jax.random.split(jax.random.key(seed), 16)
    latent_rows = bell_draw(seeds[0], (ROWS, CW), 1.0, 6.0, ((0, 128),))
    new_rows = bell_draw(seeds[1], (N_DP, REQ_G, CW), 1.0, 6.0, ((0, 4),))
    kv_gain = jnp.clip(1.0 + 0.1 * jax.random.normal(seeds[2], (LAT,), jnp.float32), 0.5, 1.5)
    lengths = draw_lengths(jax.random.fold_in(seeds[15], 71), 0)
    owners = draw_owners(jax.random.fold_in(seeds[15], 71), 0)
    queries = draw_queries(jax.random.fold_in(seeds[15], 71), 0)
    w_uv = bell_draw(seeds[6], (H, LAT, VDIM), LAT ** -0.5, 0.25, ((0, 32),))
    w_out = bell_draw(seeds[7], (H * VDIM, D), (H * VDIM) ** -0.5, 0.0625, ((0, 32),))
    resid = bell_draw(seeds[8], (N_DP, REQ_G, D), 1.0, 6.0, ((0, 4), (1, 32)))
    moe_gain = jnp.clip(1.0 + 0.1 * jax.random.normal(seeds[9], (D,), jnp.float32), 0.5, 1.5)
    route_ids_keys = jax.random.split(jax.random.fold_in(seeds[10], 1), N_DP * REQ_G // T_DEV)
    route_ids_turns = jax.random.permutation(jax.random.fold_in(seeds[10], 3), N_DP * REQ_G // T_DEV)
    route_ids = jax.vmap(lambda own, number: deal_out(jax.random.fold_in(seeds[10], 2), own, number, T_DEV, EXPERTS, TOPK, CAP, 2))(route_ids_keys, route_ids_turns).reshape((N_DP, REQ_G, TOPK))
    route_weights = jnp.clip(0.1 + 0.5 * jax.random.uniform(seeds[11], (N_DP, REQ_G, TOPK), jnp.float32) ** shard_levels(seeds[11], (N_DP, REQ_G, TOPK), ((0, 4), (1, 32)), -0.2, 0.2), 0.1, 0.6)
    w_gate = bell_draw(seeds[12], (EXPERTS, D, FFX), D ** -0.5, 0.0625, ((0, 32), (2, 4)))
    w_up = bell_draw(seeds[13], (EXPERTS, D, FFX), D ** -0.5, 0.0625, ((0, 32), (2, 4)))
    w_down = bell_draw(seeds[14], (EXPERTS, FFX, D), FFX ** -0.5, 0.1875, ((0, 32), (1, 4)))
    return {"latent_rows": latent_rows, "new_rows": new_rows, "kv_gain": kv_gain, "lengths": lengths, "owners": owners, "queries": queries, "w_uv": w_uv, "w_out": w_out, "resid": resid, "moe_gain": moe_gain, "route_ids": route_ids, "route_weights": route_weights, "w_gate": w_gate, "w_up": w_up, "w_down": w_down}


eps = 1e-06
theta = 10000.0
score_scale = 192.0 ** (-0.5)

def request_tables(lengths, owners):
    unit_len = (lengths // N_EXPERT).astype(jnp.int32)
    unit_end = jnp.cumsum(unit_len).astype(jnp.int32)
    unit_start = (unit_end - unit_len).astype(jnp.int32)
    request_order = jnp.arange(lengths.shape[0], dtype=jnp.int32)
    earlier = (owners[None, :] == owners[:, None]) & (request_order[None, :] < request_order[:, None])
    group_start = lax.optimization_barrier(jnp.sum(jnp.where(earlier, unit_len[None, :], 0), axis=1)).astype(jnp.int32)
    return (unit_len, unit_start, unit_end, group_start)

def cache_rows(raw_rows, positions, kv_gain):
    raw_rows = raw_rows.astype(jnp.float32)
    latent = raw_rows[:, :LAT]
    rotary = raw_rows[:, LAT:]
    inverse = lax.rsqrt(lax.optimization_barrier(jnp.mean(latent * latent, axis=1, keepdims=True)) + eps)
    latent = latent * inverse * kv_gain[None, :]
    half_width = rotary.shape[1] // 2
    frequency = theta ** (-jnp.arange(half_width, dtype=jnp.float32) / half_width)
    angles = positions.astype(jnp.float32)[:, None] * frequency[None, :]
    cosine = jnp.cos(angles)
    sine_part = jnp.sin(angles)
    lower_half = rotary[:, :half_width]
    upper_half = rotary[:, half_width:]
    rotated = jnp.concatenate([lower_half * cosine - upper_half * sine_part, upper_half * cosine + lower_half * sine_part], axis=1)
    return jnp.concatenate([latent, rotated], axis=1).astype(jnp.bfloat16)

def reference(latent_rows, new_rows, kv_gain, lengths, owners, queries, w_uv, w_out, resid, moe_gain, route_ids, route_weights, w_gate, w_up, w_down):
    unit_len, unit_start, unit_end, group_start = request_tables(lengths, owners)
    all_units = jnp.arange(N_DP * PRE_DEV, dtype=jnp.int32)
    unit_req = lax.optimization_barrier(jnp.sum((all_units[:, None] >= unit_end[None, :]).astype(jnp.int32), axis=1)).astype(jnp.int32)
    all_rows = jnp.arange(ROWS, dtype=jnp.int32)
    row_req = unit_req[all_rows // N_EXPERT]
    positions = (all_rows - unit_start[row_req] * N_EXPERT).astype(jnp.int32)
    processed = cache_rows(latent_rows, positions, kv_gain)
    unit_rows = processed.reshape(N_DP * PRE_DEV, N_EXPERT, CW)
    unit_group = owners[unit_req]
    unit_order = jnp.stack([jnp.nonzero(unit_group == group_id, size=PRE_DEV)[0].astype(jnp.int32) for group_id in range(N_DP)])
    grouped = unit_rows[unit_order]
    decode_cache = jnp.transpose(grouped, (0, 2, 1, 3))
    sequence = grouped.reshape(N_DP, PRE_DEV * N_EXPERT, CW)
    window_rows = MOSTU * N_EXPERT
    padded = jnp.concatenate([sequence, jnp.zeros((N_DP, window_rows, CW), jnp.bfloat16)], axis=1)
    members = jnp.stack([jnp.nonzero(owners == group_id, size=REQ_G)[0].astype(jnp.int32) for group_id in range(N_DP)])
    new_keys = cache_rows(new_rows.reshape(NREQ, CW), lengths[members].reshape(NREQ), kv_gain)
    first_rows = (group_start[members] * N_EXPERT).reshape(NREQ).astype(jnp.int32)
    live_rows = (unit_len[members] * N_EXPERT).reshape(NREQ).astype(jnp.int32)
    group_of = jnp.repeat(jnp.arange(N_DP, dtype=jnp.int32), REQ_G)
    flat_queries = queries.reshape(NREQ, H, CW)

    def attend(request_item):
        group_id, first_row, live_count, query_rows, new_key = request_item
        window = lax.dynamic_slice_in_dim(padded[group_id], first_row, window_rows, 0)
        key_rows = jnp.concatenate([window, new_key[None, :]], axis=0).astype(jnp.float32)
        alive_mask = jnp.concatenate([jnp.arange(window_rows, dtype=jnp.int32) < live_count, jnp.ones((1,), dtype=bool)])
        scores = jnp.dot(query_rows.astype(jnp.float32), key_rows.T, precision=lax.Precision.HIGHEST) * score_scale
        highest = lax.optimization_barrier(jnp.max(jnp.where(alive_mask[None, :], scores, -jnp.inf), axis=1, keepdims=True))
        weights = jnp.where(alive_mask[None, :], jnp.exp(scores - highest), 0.0)
        mixture = jnp.dot(weights, key_rows[:, :LAT], precision=lax.Precision.HIGHEST) / lax.optimization_barrier(jnp.sum(weights, axis=1, keepdims=True))
        return mixture.astype(jnp.bfloat16)
    attended = lax.map(attend, (group_of, first_rows, live_rows, flat_queries, new_keys))
    projected = jnp.einsum('rhl,hlv->rhv', attended.astype(jnp.float32), w_uv.astype(jnp.float32)).astype(jnp.bfloat16)
    attention_out = jnp.dot(projected.reshape(NREQ, H * VDIM), w_out, preferred_element_type=jnp.float32)
    residual = resid.reshape(NREQ, D).astype(jnp.float32) + attention_out
    normed = (residual * lax.rsqrt(lax.optimization_barrier(jnp.mean(residual * residual, axis=1, keepdims=True)) + eps) * moe_gain[None, :]).astype(jnp.bfloat16)
    expert_ids = jnp.arange(EXPERTS, dtype=jnp.int32)
    flat_ids = route_ids.reshape(NREQ, TOPK)
    flat_weights = route_weights.reshape(NREQ, TOPK)
    combine_weights = lax.optimization_barrier(jnp.sum(jnp.where(flat_ids[:, :, None] == expert_ids[None, None, :], flat_weights[:, :, None], 0.0), axis=1))

    def one_expert(running, expert):
        gate_in, up_in, down_in, share_col = expert
        gate_out = jnp.dot(normed, gate_in, preferred_element_type=jnp.float32)
        up_out = jnp.dot(normed, up_in, preferred_element_type=jnp.float32)
        hidden = (jax.nn.silu(gate_out) * up_out).astype(jnp.bfloat16)
        output = jnp.dot(hidden, down_in, preferred_element_type=jnp.float32)
        return (running + share_col[:, None] * output, None)
    moe_sum, _ = lax.scan(one_expert, jnp.zeros((NREQ, D), jnp.float32), (w_gate, w_up, w_down, combine_weights.T))
    decoded = (residual + moe_sum).astype(jnp.bfloat16).reshape(N_DP, REQ_G, D)
    return (decode_cache, decoded)
```

```python
import jax
import jax.numpy as jnp
from jax import lax
from jax.sharding import PartitionSpec as P

LAT = 512
UNIT = 32

eps = 1e-06
theta = 10000.0
score_scale = 192.0 ** (-0.5)
BF = jnp.bfloat16
F32 = jnp.float32


def norm_rotate(raw_rows, positions, kv_gain):
    raw_rows = raw_rows.astype(F32)
    latent = raw_rows[:, :LAT]
    rotary = raw_rows[:, LAT:]
    inverse = lax.rsqrt(jnp.mean(latent * latent, axis=1, keepdims=True) + eps)
    latent = latent * inverse * kv_gain[None, :]
    half_width = rotary.shape[1] // 2
    frequency = theta ** (-jnp.arange(half_width, dtype=F32) / half_width)
    angles = positions.astype(F32)[:, None] * frequency[None, :]
    cosine = jnp.cos(angles)
    sine_part = jnp.sin(angles)
    lower_half = rotary[:, :half_width]
    upper_half = rotary[:, half_width:]
    rotated = jnp.concatenate(
        [
            lower_half * cosine - upper_half * sine_part,
            upper_half * cosine + lower_half * sine_part,
        ],
        axis=1,
    )
    return jnp.concatenate([latent, rotated], axis=1).astype(BF)


def shift(x, step, size, axis):
    return lax.ppermute(x, axis, [((i + step) % size, i) for i in range(size)])


def shards(
    latent_rows,
    new_rows,
    kv_gain,
    lengths,
    owners,
    queries,
    w_uv,
    w_out,
    resid,
    moe_gain,
    route_ids,
    route_weights,
    w_gate,
    w_up,
    w_down,
):
    dp_count = lax.axis_size("dp")
    columns = lax.axis_size("expert")
    group = lax.axis_index("dp")
    column = lax.axis_index("expert")
    pre_rows, width = latent_rows.shape
    local_units = pre_rows // UNIT
    block_units = columns * local_units

    by_row = latent_rows.reshape(local_units, UNIT, width).transpose(1, 0, 2)
    dealt = lax.all_to_all(by_row, "expert", split_axis=0, concat_axis=0, tiled=True)
    dealt = dealt.reshape(block_units, width)
    blocks = jnp.concatenate(
        [dealt] + [shift(dealt, k, dp_count, "dp") for k in range(1, dp_count)], axis=0
    )

    requests = lengths.shape[0]
    request_total = queries.shape[1]
    unit_len = lengths // UNIT
    order = jnp.arange(requests, dtype=jnp.int32)
    before = order[None, :] < order[:, None]
    unit_start = jnp.sum(jnp.where(before, unit_len[None, :], 0), axis=1)
    own = owners == group
    own_before = before & own[None, :]
    group_start = jnp.sum(jnp.where(own_before, unit_len[None, :], 0), axis=1)
    group_rank = jnp.sum(own_before.astype(jnp.int32), axis=1)
    slots = jnp.arange(pre_rows, dtype=jnp.int32)
    offset = slots[:, None] - group_start[None, :]
    covers = own[None, :] & (offset >= 0) & (offset < unit_len[None, :])
    slot_offset = jnp.sum(jnp.where(covers, offset, 0), axis=1)
    slot_unit = jnp.sum(jnp.where(covers, offset + unit_start[None, :], 0), axis=1)
    relative = (slot_unit // block_units - group + dp_count) % dp_count
    slot_place = relative * block_units + slot_unit % block_units
    members = jnp.arange(request_total, dtype=jnp.int32)
    is_member = own[None, :] & (group_rank[None, :] == members[:, None])
    first_unit = jnp.sum(jnp.where(is_member, group_start[None, :], 0), axis=1)
    unit_count = jnp.sum(jnp.where(is_member, unit_len[None, :], 0), axis=1)

    places = jnp.arange(dp_count * block_units, dtype=jnp.int32)
    pick = (slot_place[:, None] == places[None, :]).astype(BF)
    raw_cache = jnp.dot(pick, blocks, preferred_element_type=F32)
    cache_local = norm_rotate(raw_cache, slot_offset * UNIT + column, kv_gain)

    window = 2 * pre_rows // request_total - 1
    share = request_total // columns
    steps = jnp.arange(window, dtype=jnp.int32)
    wanted = (first_unit[:, None] + steps[None, :]).reshape(-1)
    take = (wanted[:, None] == slots[None, :]).astype(BF)
    outgoing = jnp.dot(take, cache_local, preferred_element_type=F32).astype(BF)
    keys = lax.all_to_all(
        outgoing.reshape(columns, share * window, width),
        "expert",
        split_axis=0,
        concat_axis=0,
        tiled=True,
    )
    keys = keys.reshape(UNIT, share, window, width).transpose(1, 2, 0, 3)
    keys = keys.reshape(share, window * UNIT, width)
    own_first = column * share
    own_queries = lax.dynamic_slice_in_dim(queries[0], own_first, share, 0)
    own_counts = lax.dynamic_slice_in_dim(unit_count, own_first, share, 0)
    own_new = lax.dynamic_slice_in_dim(new_rows[0], own_first, share, 0)
    new_keys = norm_rotate(own_new, own_counts * UNIT, kv_gain)
    scores = (
        jnp.einsum("jhc,jkc->jhk", own_queries, keys, preferred_element_type=F32) * score_scale
    )
    live = (jnp.arange(window * UNIT, dtype=jnp.int32) // UNIT)[None, :] < own_counts[:, None]
    self_score = (
        jnp.einsum("jhc,jc->jh", own_queries, new_keys, preferred_element_type=F32) * score_scale
    )
    scores = jnp.where(live[:, None, :], scores, -jnp.inf)
    highest = jnp.maximum(jnp.max(scores, axis=2), self_score)
    weights = jnp.exp(scores - highest[:, :, None])
    self_weight = jnp.exp(self_score - highest)
    total = jnp.sum(weights, axis=2) + self_weight
    mixture = (
        jnp.einsum(
            "jhk,jkl->jhl", weights.astype(BF), keys[:, :, :LAT], preferred_element_type=F32
        )
        + self_weight[:, :, None] * new_keys[:, None, :LAT].astype(F32)
    )
    attended = (mixture / total[:, :, None]).astype(BF)

    head_share = w_uv.shape[0]
    by_head = attended.reshape(share, columns, head_share, LAT).transpose(1, 0, 2, 3)
    by_head = lax.all_to_all(by_head, "expert", split_axis=0, concat_axis=0, tiled=True)
    by_head = by_head.reshape(request_total, head_share, LAT)
    projected = jnp.einsum("jhl,hlv->jhv", by_head, w_uv, preferred_element_type=F32).astype(BF)
    partial_sums = jnp.dot(
        projected.reshape(request_total, -1), w_out, preferred_element_type=F32
    ).astype(BF)

    model_width = w_out.shape[1]
    chips = columns // 2
    core = column % 2
    by_core = partial_sums.reshape(chips, 2, share, model_width)
    mine = lax.dynamic_index_in_dim(by_core, core, 1, keepdims=False)
    other = lax.dynamic_index_in_dim(by_core, 1 - core, 1, keepdims=False)
    other = lax.ppermute(other, "expert", [(i, i ^ 1) for i in range(columns)])
    pair_sums = (mine.astype(F32) + other.astype(F32)).astype(BF)
    chip_sums = lax.all_to_all(
        pair_sums,
        "expert",
        split_axis=0,
        concat_axis=0,
        tiled=True,
        axis_index_groups=[[2 * i + c for i in range(chips)] for c in range(2)],
    )
    attention_out = jnp.sum(chip_sums.astype(F32), axis=0)
    residual = resid[0].astype(F32) + attention_out
    normed = (
        residual
        * lax.rsqrt(jnp.mean(residual * residual, axis=1, keepdims=True) + eps)
        * moe_gain[None, :]
    ).astype(BF)

    piece = model_width // dp_count
    gates, ups, downs = [], [], []
    for k in range(dp_count):
        to = (group - k + dp_count) % dp_count * piece
        parts = (
            lax.dynamic_slice_in_dim(w_gate[0], to, piece, 0),
            lax.dynamic_slice_in_dim(w_up[0], to, piece, 0),
            lax.dynamic_slice_in_dim(w_down[0], to, piece, 1),
        )
        if k:
            parts = tuple(shift(part, k, dp_count, "dp") for part in parts)
        for held, part in zip((gates, ups, downs), parts):
            held.append(part)

    tokens = resid.shape[1]
    capacity = 2
    expert_ids = jnp.arange(columns, dtype=jnp.int32)
    matches = route_ids[0][:, :, None] == expert_ids[None, None, :]
    combine_weights = jnp.sum(jnp.where(matches, route_weights[0][:, :, None], 0.0), axis=1)
    routed = jnp.any(matches, axis=1)
    token_order = jnp.arange(tokens, dtype=jnp.int32)
    earlier = token_order[None, :] < token_order[:, None]
    slot_rank = jnp.sum(
        jnp.where(earlier[:, :, None], routed.astype(jnp.int32)[None, :, :], 0), axis=1
    )
    slot_ids = jnp.arange(capacity, dtype=jnp.int32)
    slot_table = routed.T[:, None, :] & (slot_rank.T[:, None, :] == slot_ids[None, :, None])
    outgoing_tokens = jnp.einsum(
        "xct,tfd->fxcd",
        slot_table.astype(BF),
        normed.reshape(tokens, dp_count, piece),
        preferred_element_type=F32,
    ).astype(BF)
    arrived = lax.all_to_all(
        outgoing_tokens.reshape(dp_count * columns, capacity, piece),
        ("dp", "expert"),
        split_axis=0,
        concat_axis=0,
        tiled=True,
    )
    rows = arrived.reshape(dp_count * columns * capacity, piece)

    sums = None
    for k in range(dp_count):
        pair = jnp.concatenate(
            [
                jnp.dot(rows, gates[k], preferred_element_type=F32),
                jnp.dot(rows, ups[k], preferred_element_type=F32),
            ],
            axis=1,
        )
        if k:
            pair = shift(pair.astype(BF), dp_count - k, dp_count, "dp").astype(F32)
        sums = pair if sums is None else sums + pair
    half = sums.shape[1] // 2
    hidden = (jax.nn.silu(sums[:, :half]) * sums[:, half:]).astype(BF)
    out = None
    for k in range(dp_count):
        block = shift(hidden, k, dp_count, "dp") if k else hidden
        term = jnp.dot(block, downs[k], preferred_element_type=F32)
        out = term if out is None else out + term
    returned = lax.all_to_all(
        out.astype(BF).reshape(dp_count * columns, capacity, piece),
        ("dp", "expert"),
        split_axis=0,
        concat_axis=0,
        tiled=True,
    )
    slot_weights = jnp.where(slot_table, combine_weights.T[:, None, :], 0.0)
    moe_sum = jnp.einsum(
        "xct,fxcd->tfd",
        slot_weights,
        returned.reshape(dp_count, columns, capacity, piece).astype(F32),
        precision=lax.Precision.HIGHEST,
    ).reshape(tokens, model_width)
    decoded = (residual + moe_sum).astype(BF)
    return (cache_local[None, None], decoded[None])


def solution(mesh):
    return jax.shard_map(
        shards,
        mesh=mesh,
        in_specs=(
            P(("dp", "expert"), None),
            P("dp", None, None),
            P(),
            P(),
            P(),
            P("dp", None, None, None),
            P("expert", None, None),
            P("expert", None),
            P("dp", "expert", None),
            P(),
            P("dp", "expert", None),
            P("dp", "expert", None),
            P("expert", None, "dp"),
            P("expert", None, "dp"),
            P("expert", "dp", None),
        ),
        out_specs=(P("dp", "expert", None, None), P("dp", "expert", None)),
        check_vma=False,
    )
```

```python
import jax
import jax.numpy as jnp
from jax import lax
from jax.experimental import pallas as pl
from jax.experimental.pallas import tpu as pltpu
from jax.sharding import PartitionSpec as P

LAT = 512
UNIT = 32
MOST = 3
SLOTS = 10

eps = 1e-06
theta = 10000.0
score_scale = 192.0 ** (-0.5)
BF = jnp.bfloat16
F32 = jnp.float32
I32 = jnp.int32


def turn(positions, half_width):
    frequency = theta ** (-jnp.arange(half_width, dtype=F32) / half_width)
    angles = positions.astype(F32)[:, None] * frequency[None, :]
    return jnp.cos(angles), jnp.sin(angles)


def norm_rotate(raw_rows, cosine, sine, kv_gain):
    raw_rows = raw_rows.astype(F32)
    latent = raw_rows[:, :LAT]
    half_width = cosine.shape[1]
    inverse = lax.rsqrt(jnp.mean(latent * latent, axis=1, keepdims=True) + eps)
    latent = latent * inverse * kv_gain
    lower = raw_rows[:, LAT : LAT + half_width]
    upper = raw_rows[:, LAT + half_width :]
    return jnp.concatenate(
        [latent, lower * cosine - upper * sine, upper * cosine + lower * sine], axis=1
    ).astype(BF)


def shift(x, step, size, axis):
    return lax.ppermute(x, axis, [((i + step) % size, i) for i in range(size)])


def attend_kernel(
    place_ref,
    count_ref,
    member_ref,
    number_ref,
    *refs,
    blocks,
    most_slots,
    sent_slots,
):
    rows_in = refs[:blocks]
    extra_in = refs[blocks : 2 * blocks]
    cos_ref, sin_ref, gain_ref, new_ref, query_ref, out_ref, keys, query, sems = refs[2 * blocks :]
    number = number_ref[0]

    def fetch(slot):
        return pltpu.make_async_copy(
            query_ref.at[member_ref[slot]], query.at[slot], sems.at[slot]
        )

    @pl.loop(0, number)
    def _(slot):
        fetch(slot).start()

    gain = gain_ref[...]
    start = 0
    for block in range(blocks):
        for ref in (rows_in[block], extra_in[block]):
            size = ref.shape[0]
            span = slice(start, start + size)
            keys[span, :] = norm_rotate(ref[...], cos_ref[span, :], sin_ref[span, :], gain)
            start += size

    @pl.loop(number, sent_slots)
    def _(slot):
        out_ref[slot] = jnp.zeros(out_ref.shape[1:], BF)

    heads = out_ref.shape[1]
    window = MOST * UNIT
    lanes = window + UNIT
    lane = lax.broadcasted_iota(I32, (heads, lanes), 1)

    @pl.loop(0, number)
    def _(slot):
        fetch(slot).wait()
        place = pl.multiple_of(place_ref[slot], UNIT)
        own = keys[pl.ds(place, window), :]
        new = jnp.broadcast_to(
            new_ref[pl.ds(member_ref[slot], 1), :].astype(BF), (UNIT, own.shape[1])
        )
        held = jnp.concatenate([own, new], axis=0)
        scores = (
            lax.dot_general(
                query[slot], held, (((1,), (1,)), ((), ())), preferred_element_type=F32
            )
            * score_scale
        )
        live = (lane < count_ref[slot] * UNIT) | (lane == window)
        scores = jnp.where(live, scores, -jnp.inf)
        weights = jnp.exp(scores - jnp.max(scores, axis=1, keepdims=True))
        total = jnp.sum(weights, axis=1, keepdims=True)
        mixture = jnp.dot(weights.astype(BF), held[:, :LAT], preferred_element_type=F32)
        out_ref[slot] = (mixture / total).astype(BF)


def attend(tables, rows, extras, cosine, sine, gain, new_keys, queries, most_slots):
    heads = queries.shape[1]
    blocks = len(rows)
    total_rows = cosine.shape[0]
    whole = pl.BlockSpec(memory_space=pltpu.VMEM)
    scalar = pl.BlockSpec(memory_space=pltpu.SMEM)

    def body(*refs):
        attend_kernel(*refs, blocks=blocks, most_slots=most_slots, sent_slots=SLOTS)

    return pl.pallas_call(
        body,
        out_shape=jax.ShapeDtypeStruct((most_slots, heads, LAT), BF),
        in_specs=[scalar] * 4
        + [whole] * (2 * blocks + 4)
        + [pl.BlockSpec(memory_space=pl.ANY)],
        out_specs=whole,
        scratch_shapes=[
            pltpu.VMEM((total_rows, queries.shape[2]), BF),
            pltpu.VMEM((most_slots,) + queries.shape[1:], BF),
            pltpu.SemaphoreType.DMA((most_slots,)),
        ],
        compiler_params=pltpu.CompilerParams(vmem_limit_bytes=32 * 1024 * 1024),
        cost_estimate=pl.CostEstimate(
            flops=10**8, bytes_accessed=4 * 10**6, transcendentals=10**5
        ),
        name="attend",
    )(*tables, *rows, *extras, cosine, sine, gain, new_keys, queries)


def shards(
    latent_rows,
    new_rows,
    kv_gain,
    lengths,
    owners,
    queries,
    w_uv,
    w_out,
    resid,
    moe_gain,
    route_ids,
    route_weights,
    w_gate,
    w_up,
    w_down,
):
    dp_count = lax.axis_size("dp")
    columns = lax.axis_size("expert")
    devices = dp_count * columns
    group = lax.axis_index("dp")
    column = lax.axis_index("expert")
    core = column % 2
    pre_rows, width = latent_rows.shape
    half_rope = (width - LAT) // 2
    local_units = pre_rows // UNIT
    block_units = columns * local_units
    gain = kv_gain[None, :]

    border = (MOST - 1) * UNIT
    next_rows = lax.ppermute(
        latent_rows[:border],
        ("dp", "expert"),
        [((i + 1) % devices, i) for i in range(devices)],
    )
    rows = [latent_rows] + [shift(latent_rows, k, dp_count, "dp") for k in range(1, dp_count)]
    extras = [next_rows] + [shift(next_rows, k, dp_count, "dp") for k in range(1, dp_count)]

    by_row = latent_rows.reshape(local_units, UNIT, width).transpose(1, 0, 2)
    dealt = lax.all_to_all(by_row, "expert", split_axis=0, concat_axis=0, tiled=True)
    dealt = dealt.reshape(block_units, width)

    requests = lengths.shape[0]
    request_total = queries.shape[1]
    unit_len = lengths // UNIT
    order = jnp.arange(requests, dtype=I32)
    before = order[None, :] < order[:, None]
    unit_start = jnp.sum(jnp.where(before, unit_len[None, :], 0), axis=1)
    home = owners * columns + unit_start // local_units % columns
    home_rank = jnp.sum((before & (home[None, :] == home[:, None])).astype(I32), axis=1)
    own = owners == group
    own_before = before & own[None, :]
    group_start = jnp.sum(jnp.where(own_before, unit_len[None, :], 0), axis=1)
    group_rank = jnp.sum(own_before.astype(I32), axis=1)

    most_slots = dp_count * local_units
    slot_order = jnp.arange(most_slots, dtype=I32)
    here = home == group * columns + column
    is_slot = here[None, :] & (home_rank[None, :] == slot_order[:, None])
    start_block = (unit_start // block_units - group + dp_count) % dp_count
    start_place = start_block * (pre_rows + border) + unit_start % local_units * UNIT
    slot_place = jnp.sum(jnp.where(is_slot, start_place[None, :], 0), axis=1)
    slot_count = jnp.sum(jnp.where(is_slot, unit_len[None, :], 0), axis=1)
    slot_member = jnp.sum(jnp.where(is_slot, group_rank[None, :], 0), axis=1)
    slot_number = jnp.sum(here.astype(I32), keepdims=True)

    near_units = local_units + MOST - 1
    near = jnp.arange(near_units * dp_count, dtype=I32)
    near_block = (group + near // near_units) % dp_count
    near_unit = near_block * block_units + column * local_units + near % near_units
    near_start = jnp.max(
        jnp.where(unit_start[None, :] <= near_unit[:, None], unit_start[None, :], 0), axis=1
    )
    near_position = ((near_unit - near_start) * UNIT)[:, None] + jnp.arange(UNIT, dtype=I32)
    cosine, sine = turn(near_position.reshape(-1), half_rope)
    members = jnp.arange(request_total, dtype=I32)
    is_member = own[None, :] & (group_rank[None, :] == members[:, None])
    member_length = jnp.sum(jnp.where(is_member, lengths[None, :], 0), axis=1)
    new_keys = norm_rotate(new_rows[0], *turn(member_length, half_rope), gain).astype(F32)

    attended = attend(
        (slot_place, slot_count, slot_member, slot_number),
        rows,
        extras,
        cosine,
        sine,
        gain,
        new_keys,
        queries[0],
        most_slots,
    )

    model_width = w_out.shape[1]
    piece = model_width // dp_count
    halves = (0, 1, 1, 0)
    quarters = (0, 2, 3, 1)

    def pair_perm(partner):
        perm = []
        for f in range(dp_count):
            for x in range(columns):
                g = (f - x % 2) % dp_count
                perm.append((f * columns + x, (partner(g) + x % 2) % dp_count * columns + x))
        return perm

    weight_perm = pair_perm(lambda g: g ^ 1)
    token_perm = pair_perm(lambda g: dp_count - 1 - g)
    place = (group - core + dp_count) % dp_count
    quarter_of = jnp.array(quarters, I32)
    my_quarter = quarter_of[place]
    their_quarter = quarter_of[place ^ 1]

    def width_half(first):
        def side(q):
            return jnp.concatenate(
                [
                    lax.dynamic_slice_in_dim(w_gate[0], q * piece, piece, 0),
                    lax.dynamic_slice_in_dim(w_up[0], q * piece, piece, 0),
                ],
                axis=1,
            )

        return jnp.stack([side(first), side(first ^ 1)])

    to_partner, attended = lax.optimization_barrier((width_half(their_quarter), attended))
    from_partner = lax.ppermute(to_partner, ("dp", "expert"), weight_perm)
    dealt, attended = lax.optimization_barrier((dealt, attended))

    blocks = jnp.concatenate(
        [dealt] + [shift(dealt, k, dp_count, "dp") for k in range(1, dp_count)], axis=0
    )
    slots = jnp.arange(pre_rows, dtype=I32)
    offset = slots[:, None] - group_start[None, :]
    covers = own[None, :] & (offset >= 0) & (offset < unit_len[None, :])
    slot_offset = jnp.sum(jnp.where(covers, offset, 0), axis=1)
    slot_unit = jnp.sum(jnp.where(covers, offset + unit_start[None, :], 0), axis=1)
    relative = (slot_unit // block_units - group + dp_count) % dp_count
    cache_place = relative * block_units + slot_unit % block_units
    places = jnp.arange(dp_count * block_units, dtype=I32)
    pick = (cache_place[:, None] == places[None, :]).astype(BF)
    raw_cache = jnp.dot(pick, blocks, preferred_element_type=F32)
    cache_local = norm_rotate(
        raw_cache, *turn(slot_offset * UNIT + column, half_rope), gain
    )

    head_share = w_uv.shape[0]
    share = request_total // columns
    chips = columns // 2

    def to_heads(part):
        count = part.shape[0]
        part = part.reshape(count, columns, head_share * LAT).transpose(1, 0, 2)
        part = lax.all_to_all(part, "expert", split_axis=0, concat_axis=0, tiled=True)
        return part.reshape(columns * count, head_share * LAT)

    member_column = group_rank // share
    member_row = (
        (member_column % 2 ^ core) * (chips * share)
        + member_column // 2 * share
        + group_rank % share
    )
    member_home = unit_start // local_units % columns
    is_row = own[None, :] & (member_row[None, :] == members[:, None])
    row_home = jnp.sum(jnp.where(is_row, member_home[None, :], 0), axis=1)
    row_slot = jnp.sum(jnp.where(is_row, home_rank[None, :], 0), axis=1)

    def in_order(part, first):
        count = part.shape[0]
        came = to_heads(part)
        cells = jnp.arange(columns * count, dtype=I32)
        wanted = row_home * count + row_slot - first
        inside = (row_slot >= first) & (row_slot < first + count)
        pick = (inside[:, None] & (wanted[:, None] == cells[None, :])).astype(BF)
        return jnp.dot(pick, came, preferred_element_type=F32)

    by_head = in_order(attended[:SLOTS], 0)
    by_head = lax.cond(
        jnp.max(home_rank) >= SLOTS,
        lambda held: held
        + in_order(
            jnp.where(
                slot_order[SLOTS:, None, None] < slot_number[0], attended[SLOTS:], jnp.zeros((), BF)
            ),
            SLOTS,
        ),
        lambda held: held,
        by_head,
    )
    by_head, cache_local = lax.optimization_barrier((by_head, cache_local))
    by_head = by_head.astype(BF).reshape(request_total, head_share, LAT)
    projected = jnp.einsum("jhl,hlv->jhv", by_head, w_uv, preferred_element_type=F32).astype(BF)
    partial_sums = jnp.dot(
        projected.reshape(request_total, -1), w_out, preferred_element_type=F32
    ).astype(BF)

    keep = chips * share
    other = lax.ppermute(partial_sums[keep:], "expert", [(i, i ^ 1) for i in range(columns)])
    pair_sums = (partial_sums[:keep].astype(F32) + other.astype(F32)).astype(BF)
    chip_sums = lax.all_to_all(
        pair_sums.reshape(chips, share, model_width),
        "expert",
        split_axis=0,
        concat_axis=0,
        tiled=True,
        axis_index_groups=[[2 * i + c for i in range(chips)] for c in range(2)],
    )
    attention_out = jnp.sum(chip_sums.astype(F32), axis=0)
    residual = resid[0].astype(F32) + attention_out
    normed = (
        residual
        * lax.rsqrt(jnp.mean(residual * residual, axis=1, keepdims=True) + eps)
        * moe_gain[None, :]
    ).astype(BF)

    downs = []
    down_held, _ = lax.optimization_barrier((w_down[0], by_head))
    for k in range(dp_count):
        to = (group - k + dp_count) % dp_count * piece
        part = lax.dynamic_slice_in_dim(down_held, to, piece, 1)
        downs.append(shift(part, k, dp_count, "dp") if k else part)

    tokens = resid.shape[1]
    capacity = 2
    expert_ids = jnp.arange(columns, dtype=I32)
    matches = route_ids[0][:, :, None] == expert_ids[None, None, :]
    combine_weights = jnp.sum(jnp.where(matches, route_weights[0][:, :, None], 0.0), axis=1)
    routed = jnp.any(matches, axis=1)
    token_order = jnp.arange(tokens, dtype=I32)
    earlier = token_order[None, :] < token_order[:, None]
    slot_rank = jnp.sum(jnp.where(earlier[:, :, None], routed.astype(I32)[None, :, :], 0), axis=1)
    slot_ids = jnp.arange(capacity, dtype=I32)
    slot_table = routed.T[:, None, :] & (slot_rank.T[:, None, :] == slot_ids[None, :, None])
    table = slot_table.reshape(columns * capacity, tokens)
    even = (jnp.arange(columns * capacity, dtype=I32) // capacity % 2 == 0)[:, None]
    table = jnp.concatenate([table & even, table & ~even], axis=1).astype(BF)
    outgoing = []
    for f in range(dp_count):
        both = jnp.concatenate(
            [
                normed[:, q * piece : (q + 1) * piece]
                for q in (quarters[f], quarters[(f - 1) % dp_count])
            ],
            axis=0,
        )
        outgoing.append(jnp.dot(table, both, preferred_element_type=F32).astype(BF))
    outgoing = jnp.stack(outgoing).reshape(devices, capacity, piece)
    outgoing, from_partner = lax.optimization_barrier((outgoing, from_partner))
    arrived = lax.all_to_all(
        outgoing, ("dp", "expert"), split_axis=0, concat_axis=0, tiled=True
    ).reshape(devices * capacity, piece)
    beside = lax.ppermute(arrived, ("dp", "expert"), token_perm)

    def gate_up(first, second):
        return jnp.dot(arrived, first, preferred_element_type=F32) + jnp.dot(
            beside, second, preferred_element_type=F32
        )

    given = gate_up(from_partner[0], from_partner[1]).astype(BF)
    given = lax.ppermute(given, ("dp", "expert"), weight_perm)
    own_half = width_half(my_quarter)
    sums = gate_up(own_half[0], own_half[1]) + given.astype(F32)
    half = sums.shape[1] // 2
    hidden = (jax.nn.silu(sums[:, :half]) * sums[:, half:]).astype(BF)
    hidden_all = jnp.concatenate(
        [hidden] + [shift(hidden, k, dp_count, "dp") for k in range(1, dp_count)], axis=1
    )
    out = jnp.dot(hidden_all, jnp.concatenate(downs, axis=0), preferred_element_type=F32)
    returned = lax.all_to_all(
        out.astype(BF).reshape(devices, capacity, piece),
        ("dp", "expert"),
        split_axis=0,
        concat_axis=0,
        tiled=True,
    )
    slot_weights = jnp.where(slot_table, combine_weights.T[:, None, :], 0.0)
    moe_sum = jnp.einsum(
        "xct,fxcd->tfd",
        slot_weights,
        returned.reshape(dp_count, columns, capacity, piece).astype(F32),
        precision=lax.Precision.HIGHEST,
    ).reshape(tokens, model_width)
    decoded = (residual + moe_sum).astype(BF)
    return (cache_local[None, None], decoded[None])


def solution(mesh):
    return jax.shard_map(
        shards,
        mesh=mesh,
        in_specs=(
            P(("dp", "expert"), None),
            P("dp", None, None),
            P(),
            P(),
            P(),
            P("dp", None, None, None),
            P("expert", None, None),
            P("expert", None),
            P("dp", "expert", None),
            P(),
            P("dp", "expert", None),
            P("dp", "expert", None),
            P("expert", None, "dp"),
            P("expert", None, "dp"),
            P("expert", "dp", None),
        ),
        out_specs=(P("dp", "expert", None, None), P("dp", "expert", None)),
        check_vma=False,
    )
```

```python
import jax
import jax.numpy as jnp
from jax import lax
from jax.experimental import pallas as pl
from jax.experimental.pallas import tpu as pltpu
from jax.sharding import PartitionSpec as P

LAT = 512
UNIT = 32
MOST = 3
SLOTS = 10

eps = 1e-06
theta = 10000.0
score_scale = 192.0 ** (-0.5)
BF = jnp.bfloat16
F32 = jnp.float32
I32 = jnp.int32


def turn(positions, half_width):
    frequency = theta ** (-jnp.arange(half_width, dtype=F32) / half_width)
    angles = positions.astype(F32)[:, None] * frequency[None, :]
    return jnp.cos(angles), jnp.sin(angles)


def norm_rotate(raw_rows, cosine, sine, kv_gain):
    raw_rows = raw_rows.astype(F32)
    latent = raw_rows[:, :LAT]
    half_width = cosine.shape[1]
    inverse = lax.rsqrt(jnp.mean(latent * latent, axis=1, keepdims=True) + eps)
    latent = latent * inverse * kv_gain
    lower = raw_rows[:, LAT : LAT + half_width]
    upper = raw_rows[:, LAT + half_width :]
    return jnp.concatenate(
        [latent, lower * cosine - upper * sine, upper * cosine + lower * sine], axis=1
    ).astype(BF)


def shift(x, step, size, axis):
    return lax.ppermute(x, axis, [((i + step) % size, i) for i in range(size)])


def attend_kernel(
    place_ref,
    count_ref,
    member_ref,
    number_ref,
    *refs,
    blocks,
    most_slots,
    sent_slots,
):
    rows_in = refs[:blocks]
    cos_ref, sin_ref, gain_ref, new_ref, query_ref, out_ref, keys, query, sems = refs[blocks:]
    number = number_ref[0]

    def fetch(slot):
        return pltpu.make_async_copy(
            query_ref.at[member_ref[slot]], query.at[slot], sems.at[slot]
        )

    @pl.loop(0, number)
    def _(slot):
        fetch(slot).start()

    gain = gain_ref[...]
    start = 0
    for block in range(blocks):
        ref = rows_in[block]
        span = slice(start, start + ref.shape[0])
        keys[span, :] = norm_rotate(ref[...], cos_ref[span, :], sin_ref[span, :], gain)
        start += ref.shape[0]

    @pl.loop(number, sent_slots)
    def _(slot):
        out_ref[slot] = jnp.zeros(out_ref.shape[1:], BF)

    heads = out_ref.shape[1]
    window = MOST * UNIT
    lanes = window + UNIT
    lane = lax.broadcasted_iota(I32, (heads, lanes), 1)

    @pl.loop(0, number)
    def _(slot):
        fetch(slot).wait()
        place = pl.multiple_of(place_ref[slot], UNIT)
        own = keys[pl.ds(place, window), :]
        new = jnp.broadcast_to(
            new_ref[pl.ds(member_ref[slot], 1), :].astype(BF), (UNIT, own.shape[1])
        )
        held = jnp.concatenate([own, new], axis=0)
        scores = (
            lax.dot_general(
                query[slot], held, (((1,), (1,)), ((), ())), preferred_element_type=F32
            )
            * score_scale
        )
        live = (lane < count_ref[slot] * UNIT) | (lane == window)
        scores = jnp.where(live, scores, -jnp.inf)
        weights = jnp.exp(scores - jnp.max(scores, axis=1, keepdims=True))
        total = jnp.sum(weights, axis=1, keepdims=True)
        mixture = jnp.dot(weights.astype(BF), held[:, :LAT], preferred_element_type=F32)
        out_ref[slot] = (mixture / total).astype(BF)


def attend(tables, rows, cosine, sine, gain, new_keys, queries, most_slots):
    heads = queries.shape[1]
    blocks = len(rows)
    total_rows = cosine.shape[0]
    whole = pl.BlockSpec(memory_space=pltpu.VMEM)
    scalar = pl.BlockSpec(memory_space=pltpu.SMEM)

    def body(*refs):
        attend_kernel(*refs, blocks=blocks, most_slots=most_slots, sent_slots=SLOTS)

    return pl.pallas_call(
        body,
        out_shape=jax.ShapeDtypeStruct((most_slots, heads, LAT), BF),
        in_specs=[scalar] * 4
        + [whole] * (blocks + 4)
        + [pl.BlockSpec(memory_space=pl.ANY)],
        out_specs=whole,
        scratch_shapes=[
            pltpu.VMEM((total_rows, queries.shape[2]), BF),
            pltpu.VMEM((most_slots,) + queries.shape[1:], BF),
            pltpu.SemaphoreType.DMA((most_slots,)),
        ],
        compiler_params=pltpu.CompilerParams(vmem_limit_bytes=32 * 1024 * 1024),
        cost_estimate=pl.CostEstimate(
            flops=10**8, bytes_accessed=4 * 10**6, transcendentals=10**5
        ),
        name="attend",
    )(*tables, *rows, cosine, sine, gain, new_keys, queries)


def shards(
    latent_rows,
    new_rows,
    kv_gain,
    lengths,
    owners,
    queries,
    w_uv,
    w_out,
    resid,
    moe_gain,
    route_ids,
    route_weights,
    w_gate,
    w_up,
    w_down,
):
    dp_count = lax.axis_size("dp")
    columns = lax.axis_size("expert")
    devices = dp_count * columns
    group = lax.axis_index("dp")
    column = lax.axis_index("expert")
    core = column % 2
    pre_rows, width = latent_rows.shape
    half_rope = (width - LAT) // 2
    local_units = pre_rows // UNIT
    block_units = columns * local_units
    gain = kv_gain[None, :]

    border = (MOST - 1) * UNIT
    next_rows = lax.ppermute(
        latent_rows[:border],
        ("dp", "expert"),
        [((i + 1) % devices, i) for i in range(devices)],
    )
    near_rows = jnp.concatenate([latent_rows, next_rows], axis=0)
    rows = [near_rows] + [shift(near_rows, k, dp_count, "dp") for k in range(1, dp_count)]

    requests = lengths.shape[0]
    request_total = queries.shape[1]
    unit_len = lengths // UNIT
    order = jnp.arange(requests, dtype=I32)
    before = order[None, :] < order[:, None]
    unit_start = jnp.sum(jnp.where(before, unit_len[None, :], 0), axis=1)
    home = owners * columns + unit_start // local_units % columns
    home_rank = jnp.sum((before & (home[None, :] == home[:, None])).astype(I32), axis=1)
    own = owners == group
    own_before = before & own[None, :]
    group_start = jnp.sum(jnp.where(own_before, unit_len[None, :], 0), axis=1)
    group_rank = jnp.sum(own_before.astype(I32), axis=1)

    most_slots = dp_count * local_units
    slot_order = jnp.arange(most_slots, dtype=I32)
    here = home == group * columns + column
    is_slot = here[None, :] & (home_rank[None, :] == slot_order[:, None])
    start_block = (unit_start // block_units - group + dp_count) % dp_count
    start_place = start_block * (pre_rows + border) + unit_start % local_units * UNIT
    slot_place = jnp.sum(jnp.where(is_slot, start_place[None, :], 0), axis=1)
    slot_count = jnp.sum(jnp.where(is_slot, unit_len[None, :], 0), axis=1)
    slot_member = jnp.sum(jnp.where(is_slot, group_rank[None, :], 0), axis=1)
    slot_number = jnp.sum(here.astype(I32), keepdims=True)

    near_units = local_units + MOST - 1
    near = jnp.arange(near_units * dp_count, dtype=I32)
    near_block = (group + near // near_units) % dp_count
    near_unit = near_block * block_units + column * local_units + near % near_units
    near_start = jnp.max(
        jnp.where(unit_start[None, :] <= near_unit[:, None], unit_start[None, :], 0), axis=1
    )
    near_position = ((near_unit - near_start) * UNIT)[:, None] + jnp.arange(UNIT, dtype=I32)
    cosine, sine = turn(near_position.reshape(-1), half_rope)
    members = jnp.arange(request_total, dtype=I32)
    is_member = own[None, :] & (group_rank[None, :] == members[:, None])
    member_length = jnp.sum(jnp.where(is_member, lengths[None, :], 0), axis=1)
    new_keys = norm_rotate(new_rows[0], *turn(member_length, half_rope), gain).astype(F32)

    model_width = w_out.shape[1]
    piece = model_width // dp_count
    halves = (0, 1, 1, 0)
    quarters = (0, 2, 3, 1)

    def pair_perm(partner):
        perm = []
        for f in range(dp_count):
            for x in range(columns):
                g = (f - x % 2) % dp_count
                perm.append((f * columns + x, (partner(g) + x % 2) % dp_count * columns + x))
        return perm

    weight_perm = pair_perm(lambda g: g ^ 1)
    token_perm = pair_perm(lambda g: dp_count - 1 - g)
    place = (group - core + dp_count) % dp_count
    quarter_of = jnp.array(quarters, I32)
    my_quarter = quarter_of[place]
    their_quarter = quarter_of[place ^ 1]

    def width_half(weight, first):
        return jnp.stack(
            [
                lax.dynamic_slice_in_dim(weight[0], q * piece, piece, 0)
                for q in (first, first ^ 1)
            ]
        )

    def down_part(k):
        return lax.dynamic_slice_in_dim(
            w_down[0], (group - k + dp_count) % dp_count * piece, piece, 1
        )

    to_partner, *rows = lax.optimization_barrier((width_half(w_gate, their_quarter), *rows))
    gate_came = lax.ppermute(to_partner, ("dp", "expert"), weight_perm)

    attended = attend(
        (slot_place, slot_count, slot_member, slot_number),
        rows,
        cosine,
        sine,
        gain,
        new_keys,
        queries[0],
        most_slots,
    )

    head_share = w_uv.shape[0]
    share = request_total // columns
    chips = columns // 2

    def to_heads(part):
        count = part.shape[0]
        part = part.reshape(count, columns, head_share * LAT).transpose(1, 0, 2)
        part = lax.all_to_all(part, "expert", split_axis=0, concat_axis=0, tiled=True)
        return part.reshape(columns * count, head_share * LAT)

    member_column = group_rank // share
    member_row = (
        (member_column % 2 ^ core) * (chips * share)
        + member_column // 2 * share
        + group_rank % share
    )
    member_home = unit_start // local_units % columns
    is_row = own[None, :] & (member_row[None, :] == members[:, None])
    row_home = jnp.sum(jnp.where(is_row, member_home[None, :], 0), axis=1)
    row_slot = jnp.sum(jnp.where(is_row, home_rank[None, :], 0), axis=1)

    def in_order(part, first):
        count = part.shape[0]
        came = to_heads(part)
        cells = jnp.arange(columns * count, dtype=I32)
        wanted = row_home * count + row_slot - first
        inside = (row_slot >= first) & (row_slot < first + count)
        pick = (inside[:, None] & (wanted[:, None] == cells[None, :])).astype(BF)
        return jnp.dot(pick, came, preferred_element_type=F32)

    by_head = in_order(attended[:SLOTS], 0)
    by_head = lax.cond(
        jnp.max(home_rank) >= SLOTS,
        lambda held: held
        + in_order(
            jnp.where(
                slot_order[SLOTS:, None, None] < slot_number[0], attended[SLOTS:], jnp.zeros((), BF)
            ),
            SLOTS,
        ),
        lambda held: held,
        by_head,
    )
    up_sent, down_near, down_last = width_half(w_up, their_quarter), down_part(1), down_part(3)
    by_head, gate_came, up_sent, down_near, down_last = lax.optimization_barrier(
        (by_head, gate_came, up_sent, down_near, down_last)
    )
    up_came = lax.ppermute(up_sent, ("dp", "expert"), weight_perm)
    down_near = shift(down_near, 1, dp_count, "dp")
    down_last = shift(down_last, 3, dp_count, "dp")
    by_head = by_head.astype(BF).reshape(request_total, head_share, LAT)
    projected = jnp.einsum("jhl,hlv->jhv", by_head, w_uv, preferred_element_type=F32).astype(BF)
    partial_sums = jnp.dot(
        projected.reshape(request_total, -1), w_out, preferred_element_type=F32
    ).astype(BF)

    keep = chips * share
    other = lax.ppermute(partial_sums[keep:], "expert", [(i, i ^ 1) for i in range(columns)])
    pair_sums = (partial_sums[:keep].astype(F32) + other.astype(F32)).astype(BF)
    chip_sums = lax.all_to_all(
        pair_sums.reshape(chips, share, model_width),
        "expert",
        split_axis=0,
        concat_axis=0,
        tiled=True,
        axis_index_groups=[[2 * i + c for i in range(chips)] for c in range(2)],
    )
    chip_sums, up_came, down_near, down_last, down_far = lax.optimization_barrier(
        (chip_sums, up_came, down_near, down_last, down_part(2))
    )
    down_far = shift(down_far, 2, dp_count, "dp")
    attention_out = jnp.sum(chip_sums.astype(F32), axis=0)
    residual = resid[0].astype(F32) + attention_out
    normed = (
        residual
        * lax.rsqrt(jnp.mean(residual * residual, axis=1, keepdims=True) + eps)
        * moe_gain[None, :]
    ).astype(BF)

    tokens = resid.shape[1]
    capacity = 2
    expert_ids = jnp.arange(columns, dtype=I32)
    matches = route_ids[0][:, :, None] == expert_ids[None, None, :]
    combine_weights = jnp.sum(jnp.where(matches, route_weights[0][:, :, None], 0.0), axis=1)
    routed = jnp.any(matches, axis=1)
    token_order = jnp.arange(tokens, dtype=I32)
    earlier = token_order[None, :] < token_order[:, None]
    slot_rank = jnp.sum(jnp.where(earlier[:, :, None], routed.astype(I32)[None, :, :], 0), axis=1)
    slot_ids = jnp.arange(capacity, dtype=I32)
    slot_table = routed.T[:, None, :] & (slot_rank.T[:, None, :] == slot_ids[None, :, None])
    table = slot_table.reshape(columns * capacity, tokens)
    even = (jnp.arange(columns * capacity, dtype=I32) // capacity % 2 == 0)[:, None]
    table = jnp.concatenate([table & even, table & ~even], axis=1).astype(BF)
    outgoing = []
    for f in range(dp_count):
        both = jnp.concatenate(
            [
                normed[:, q * piece : (q + 1) * piece]
                for q in (quarters[f], quarters[(f - 1) % dp_count])
            ],
            axis=0,
        )
        outgoing.append(jnp.dot(table, both, preferred_element_type=F32).astype(BF))
    outgoing = jnp.stack(outgoing).reshape(devices, capacity, piece)
    arrived = lax.all_to_all(
        outgoing, ("dp", "expert"), split_axis=0, concat_axis=0, tiled=True
    ).reshape(devices * capacity, piece)

    local_rows = local_units * UNIT
    to_rows = jnp.concatenate(
        [block[:local_rows].reshape(local_units, UNIT, width) for block in rows], axis=0
    ).transpose(1, 0, 2)
    arrived, down_far, to_rows = lax.optimization_barrier((arrived, down_far, to_rows))
    beside = lax.ppermute(arrived, ("dp", "expert"), token_perm)
    dealt = lax.all_to_all(to_rows, "expert", split_axis=0, concat_axis=0, tiled=True)

    gate_own, up_own = width_half(w_gate, my_quarter), width_half(w_up, my_quarter)
    weights = (gate_came, up_came, gate_own, up_own)
    first = [jnp.dot(arrived, weight[0], preferred_element_type=F32) for weight in weights]
    beside, *first = lax.optimization_barrier((beside, *first))
    gate_given, up_given, gate_sum, up_sum = (
        part + jnp.dot(beside, weight[1], preferred_element_type=F32)
        for part, weight in zip(first, weights)
    )
    given = jnp.concatenate([gate_given, up_given], axis=1).astype(BF)
    given = lax.ppermute(given, ("dp", "expert"), weight_perm).astype(F32)
    half = gate_sum.shape[1]
    hidden = (
        jax.nn.silu(gate_sum + given[:, :half]) * (up_sum + given[:, half:])
    ).astype(BF)
    hidden_all = jnp.concatenate(
        [hidden] + [shift(hidden, k, dp_count, "dp") for k in range(1, dp_count)], axis=1
    )
    hidden_all, dealt = lax.optimization_barrier((hidden_all, dealt))
    downs = jnp.concatenate([down_part(0), down_near, down_far, down_last], axis=0)
    out = jnp.dot(hidden_all, downs, preferred_element_type=F32)
    returned = lax.all_to_all(
        out.astype(BF).reshape(devices, capacity, piece),
        ("dp", "expert"),
        split_axis=0,
        concat_axis=0,
        tiled=True,
    )

    slots = jnp.arange(pre_rows, dtype=I32)
    offset = slots[:, None] - group_start[None, :]
    covers = own[None, :] & (offset >= 0) & (offset < unit_len[None, :])
    slot_offset = jnp.sum(jnp.where(covers, offset, 0), axis=1)
    slot_unit = jnp.sum(jnp.where(covers, offset + unit_start[None, :], 0), axis=1)
    relative = (slot_unit // block_units - group + dp_count) % dp_count
    cache_place = (
        slot_unit % block_units // local_units * most_slots
        + relative * local_units
        + slot_unit % local_units
    )
    places = jnp.arange(columns * most_slots, dtype=I32)
    pick = (cache_place[:, None] == places[None, :]).astype(BF)
    raw_cache = jnp.dot(
        pick, dealt.reshape(columns * most_slots, width), preferred_element_type=F32
    )
    cache_local = norm_rotate(raw_cache, *turn(slot_offset * UNIT + column, half_rope), gain)

    slot_weights = jnp.where(slot_table, combine_weights.T[:, None, :], 0.0)
    moe_sum = jnp.einsum(
        "xct,fxcd->tfd",
        slot_weights,
        returned.reshape(dp_count, columns, capacity, piece).astype(F32),
        precision=lax.Precision.HIGHEST,
    ).reshape(tokens, model_width)
    decoded = (residual + moe_sum).astype(BF)
    return (cache_local[None, None], decoded[None])


def solution(mesh):
    return jax.shard_map(
        shards,
        mesh=mesh,
        in_specs=(
            P(("dp", "expert"), None),
            P("dp", None, None),
            P(),
            P(),
            P(),
            P("dp", None, None, None),
            P("expert", None, None),
            P("expert", None),
            P("dp", "expert", None),
            P(),
            P("dp", "expert", None),
            P("dp", "expert", None),
            P("expert", None, "dp"),
            P("expert", None, "dp"),
            P("expert", "dp", None),
        ),
        out_specs=(P("dp", "expert", None, None), P("dp", "expert", None)),
        check_vma=False,
    )
```

```python
import jax
import jax.numpy as jnp
import numpy as np
from jax import lax
from jax.experimental import pallas as pl
from jax.experimental.pallas import tpu as pltpu
from jax.sharding import PartitionSpec as P

LAT = 512
UNIT = 32
MOST = 3
SLOTS = 8

eps = 1e-06
theta = 10000.0
score_scale = 192.0 ** (-0.5)
BF = jnp.bfloat16
F32 = jnp.float32
I32 = jnp.int32


def turn_table(half_width):
    exponent = -np.arange(half_width, dtype=np.float32) / np.float32(half_width)
    frequency = np.power(np.float32(theta), exponent).astype(np.float32)
    count = (MOST + 1) * UNIT
    angles = np.arange(count, dtype=np.float32)[:, None] * frequency[None, :]
    return np.cos(angles).astype(np.float32), np.sin(angles).astype(np.float32)


def norm_rotate(raw_rows, cosine, sine, kv_gain):
    raw_rows = raw_rows.astype(F32)
    latent = raw_rows[:, :LAT]
    half_width = cosine.shape[1]
    inverse = lax.rsqrt(jnp.mean(latent * latent, axis=1, keepdims=True) + eps)
    latent = latent * inverse * kv_gain
    lower = raw_rows[:, LAT : LAT + half_width]
    upper = raw_rows[:, LAT + half_width :]
    return jnp.concatenate(
        [latent, lower * cosine - upper * sine, upper * cosine + lower * sine], axis=1
    ).astype(BF)


def shift(x, step, size, axis):
    return lax.ppermute(x, axis, [((i + step) % size, i) for i in range(size)])


def table_kernel(where_ref, lengths_ref, owners_ref, slots_ref, rows_ref, *, sizes):
    dp_count, columns, local_units, near_units = sizes
    group, column = where_ref[0], where_ref[1]
    group_f, column_f = group.astype(F32), column.astype(F32)
    count = lengths_ref.shape[1]
    units = lengths_ref[...].astype(F32) * (1.0 / UNIT)
    owner = owners_ref[...].astype(F32)
    square = (count, count)
    down = lax.broadcasted_iota(I32, square, 0)
    along = lax.broadcasted_iota(I32, square, 1)
    before = down < along

    def upright(row):
        return jnp.sum(jnp.where(down == along, row, 0.0), axis=1, keepdims=True)

    def whole(x, size):
        return jnp.floor((x + 0.5) * (1.0 / size))

    units_up, owner_up = upright(units), upright(owner)
    start = jnp.sum(jnp.where(before, units_up, 0.0), axis=0, keepdims=True)
    start_source = whole(start, local_units)
    start_block = whole(start_source, columns)
    start_column = start_source - start_block * columns
    home = owner * columns + start_column
    home_up = upright(home)
    rank = jnp.sum(jnp.where(before & (home_up == home), 1.0, 0.0), axis=0, keepdims=True)
    own = owner == group_f
    own_before = before & (owner_up == group_f)
    group_start = jnp.sum(jnp.where(own_before, units_up, 0.0), axis=0, keepdims=True)
    group_rank = jnp.sum(jnp.where(own_before, 1.0, 0.0), axis=0, keepdims=True)

    lines = slots_ref.shape[0]
    line = lax.broadcasted_iota(I32, (lines, count), 0).astype(F32)
    here = home == group_f * columns + column_f
    is_slot = here & (rank == line)
    block = start_block - group_f
    block = jnp.where(block < 0.0, block + dp_count, block)
    place = block * near_units + (start - start_source * local_units)

    def pick(row):
        return jnp.sum(jnp.where(is_slot, row, 0.0), axis=1, keepdims=True)

    near = lax.broadcasted_iota(I32, (lines, 1), 0).astype(F32)
    near_block = whole(near, near_units)
    near_unit = near - near_block * near_units + column_f * local_units
    near_block = near_block + group_f
    near_block = jnp.where(near_block >= dp_count, near_block - dp_count, near_block)
    near_unit = near_unit + near_block * (columns * local_units)
    near_start = jnp.max(jnp.where(start <= near_unit, start, 0.0), axis=1, keepdims=True)
    near_offset = jnp.minimum(near_unit - near_start, MOST - 1.0)
    number = jnp.sum(jnp.where(here, 1.0, 0.0), axis=1, keepdims=True)
    lane = lax.broadcasted_iota(I32, slots_ref.shape, 1)
    packed = jnp.zeros(slots_ref.shape, F32)
    for i, value in enumerate((pick(place), pick(units), pick(group_rank), near_offset, number)):
        packed = jnp.where(lane == i, value, packed)
    slots_ref[...] = packed.astype(I32)
    rows_ref[...] = jnp.concatenate(
        [start, rank, group_start, group_rank, start_column] + [start] * 3, axis=0
    ).astype(I32)


def tables(where, lengths, owners, sizes):
    lines = sizes[0] * sizes[3]
    whole = pl.BlockSpec(memory_space=pltpu.VMEM)

    def body(*refs):
        table_kernel(*refs, sizes=sizes)

    return pl.pallas_call(
        body,
        out_shape=(
            jax.ShapeDtypeStruct((lines, 128), I32),
            jax.ShapeDtypeStruct((8, lengths.shape[0]), I32),
        ),
        in_specs=[pl.BlockSpec(memory_space=pltpu.SMEM), whole, whole],
        out_specs=(whole, whole),
        compiler_params=pltpu.CompilerParams(vmem_limit_bytes=32 * 1024 * 1024),
        cost_estimate=pl.CostEstimate(flops=1000, bytes_accessed=4096, transcendentals=0),
        name="tables",
    )(where, lengths[None, :], owners[None, :])


def slice_kernel(at_ref, gate_ref, up_ref, down_ref, gate_out, up_out, *refs):
    downs, sems = refs[:-1], refs[-1]
    piece = gate_out.shape[1]
    copies = []
    for out, weight in ((gate_out, gate_ref), (up_out, up_ref)):
        for i in range(2):
            rows = pl.ds(pl.multiple_of(at_ref[i], 128), piece)
            copies.append((weight.at[0, rows, :], out.at[i]))
    for i, out in enumerate(downs):
        columns = pl.ds(pl.multiple_of(at_ref[2 + i], 128), piece)
        copies.append((down_ref.at[0, :, columns], out))
    copies = [
        pltpu.make_async_copy(source, target, sems.at[i])
        for i, (source, target) in enumerate(copies)
    ]
    for copy in copies:
        copy.start()
    for copy in copies:
        copy.wait()


def weight_slices(at, w_gate, w_up, w_down, dp_count):
    piece = w_gate.shape[1] // dp_count
    away = pl.BlockSpec(memory_space=pl.ANY)
    halves = jax.ShapeDtypeStruct((2, piece, w_gate.shape[2]), BF)
    part = jax.ShapeDtypeStruct((w_down.shape[1], piece), BF)
    return pl.pallas_call(
        slice_kernel,
        out_shape=(halves, halves) + (part,) * (dp_count - 1),
        in_specs=[pl.BlockSpec(memory_space=pltpu.SMEM)] + [away] * 3,
        out_specs=(away,) * (dp_count + 1),
        scratch_shapes=[pltpu.SemaphoreType.DMA((dp_count + 3,))],
        cost_estimate=pl.CostEstimate(flops=1000, bytes_accessed=4096, transcendentals=0),
        name="weight_slices",
    )(at, w_gate, w_up, w_down)


def attend_kernel(slots_ref, *refs, blocks):
    rows_in = refs[:blocks]
    cos_ref, sin_ref, gain_ref, new_ref, query_ref = refs[blocks : blocks + 5]
    out_ref, rest_ref, keys, query, fresh, held_out, sems = refs[blocks + 5 :]
    number = slots_ref[0, 4]

    def fetch(slot):
        return pltpu.make_async_copy(
            query_ref.at[slots_ref[slot, 2]], query.at[slot], sems.at[slot]
        )

    @pl.loop(0, number)
    def _(slot):
        fetch(slot).start()

    gain = gain_ref[...]
    unit = 0
    for ref in rows_in:
        for first in range(0, ref.shape[0], UNIT):
            span = pl.ds(pl.multiple_of(slots_ref[unit, 3] * UNIT, UNIT), UNIT)
            keys[unit * UNIT : (unit + 1) * UNIT, :] = norm_rotate(
                ref[first : first + UNIT, :], cos_ref[span, :], sin_ref[span, :], gain
            )
            unit += 1
    fresh[...] = new_ref[...].astype(F32)
    held_out[...] = jnp.zeros(held_out.shape, F32)

    heads = out_ref.shape[0]
    sent = out_ref.shape[1]
    window = MOST * UNIT
    lanes = window + UNIT
    lane = lax.broadcasted_iota(I32, (heads, lanes), 1)

    def one(slot):
        fetch(slot).wait()
        count = slots_ref[slot, 1]
        own = keys[pl.ds(pl.multiple_of(slots_ref[slot, 0] * UNIT, UNIT), window), :]
        at = pl.ds(count * UNIT, 1)
        new = norm_rotate(
            fresh[pl.ds(slots_ref[slot, 2], 1), :], cos_ref[at, :], sin_ref[at, :], gain
        )
        new = jnp.broadcast_to(new.astype(F32), (UNIT, own.shape[1])).astype(BF)
        held = jnp.concatenate([own, new], axis=0)
        scores = (
            lax.dot_general(
                query[slot], held, (((1,), (1,)), ((), ())), preferred_element_type=F32
            )
            * score_scale
        )
        live = (lane < count * UNIT) | (lane == window)
        scores = jnp.where(live, scores, -jnp.inf)
        weights = jnp.exp(scores - jnp.max(scores, axis=1, keepdims=True))
        total = jnp.sum(weights, axis=1, keepdims=True)
        mixture = jnp.dot(weights.astype(BF), held[:, :LAT], preferred_element_type=F32)
        return mixture / total

    @pl.loop(0, jnp.minimum(number, sent))
    def _(slot):
        held_out[slot] = one(slot)

    out_ref[...] = jnp.swapaxes(held_out[...], 0, 1).astype(BF)

    @pl.loop(sent, number)
    def _(slot):
        rest_ref[slot - sent] = one(slot).astype(BF)


def attend(slots, rows, cosine, sine, gain, new_rows, queries, most_slots):
    heads = queries.shape[1]
    blocks = len(rows)
    total_rows = sum(block.shape[0] for block in rows)
    whole = pl.BlockSpec(memory_space=pltpu.VMEM)

    def body(*refs):
        attend_kernel(*refs, blocks=blocks)

    return pl.pallas_call(
        body,
        out_shape=(
            jax.ShapeDtypeStruct((heads, SLOTS, LAT), BF),
            jax.ShapeDtypeStruct((most_slots - SLOTS, heads, LAT), BF),
        ),
        in_specs=[pl.BlockSpec(memory_space=pltpu.SMEM)]
        + [whole] * (blocks + 4)
        + [pl.BlockSpec(memory_space=pl.ANY)],
        out_specs=(whole, whole),
        scratch_shapes=[
            pltpu.VMEM((total_rows, queries.shape[2]), BF),
            pltpu.VMEM((most_slots,) + queries.shape[1:], BF),
            pltpu.VMEM(new_rows.shape, F32),
            pltpu.VMEM((SLOTS, heads, LAT), F32),
            pltpu.SemaphoreType.DMA((most_slots,)),
        ],
        compiler_params=pltpu.CompilerParams(vmem_limit_bytes=32 * 1024 * 1024),
        cost_estimate=pl.CostEstimate(
            flops=10**8, bytes_accessed=4 * 10**6, transcendentals=10**5
        ),
        name="attend",
    )(slots, *rows, cosine, sine, gain, new_rows, queries)


def shards(
    latent_rows,
    new_rows,
    kv_gain,
    lengths,
    owners,
    queries,
    w_uv,
    w_out,
    resid,
    moe_gain,
    route_ids,
    route_weights,
    w_gate,
    w_up,
    w_down,
):
    dp_count = lax.axis_size("dp")
    columns = lax.axis_size("expert")
    devices = dp_count * columns
    group = lax.axis_index("dp")
    column = lax.axis_index("expert")
    core = column % 2
    pre_rows, width = latent_rows.shape
    half_rope = (width - LAT) // 2
    local_units = pre_rows // UNIT
    block_units = columns * local_units
    gain = kv_gain[None, :]

    border = (MOST - 1) * UNIT
    next_rows = lax.ppermute(
        latent_rows[:border],
        ("dp", "expert"),
        [((i + 1) % devices, i) for i in range(devices)],
    )
    near_rows = jnp.concatenate([latent_rows, next_rows], axis=0)
    rows = [near_rows] + [shift(near_rows, k, dp_count, "dp") for k in range(1, dp_count)]

    request_total = queries.shape[1]
    most_slots = dp_count * local_units
    near_units = local_units + MOST - 1
    where = jnp.stack([group, column]).astype(I32)
    slot_table_rows, request_rows = tables(
        where, lengths, owners, (dp_count, columns, local_units, near_units)
    )
    cosine, sine = turn_table(half_rope)

    model_width = w_out.shape[1]
    piece = model_width // dp_count
    halves = (0, 1, 1, 0)
    quarters = (0, 2, 3, 1)

    def pair_perm(partner):
        perm = []
        for f in range(dp_count):
            for x in range(columns):
                g = (f - x % 2) % dp_count
                perm.append((f * columns + x, (partner(g) + x % 2) % dp_count * columns + x))
        return perm

    weight_perm = pair_perm(lambda g: g ^ 1)
    token_perm = pair_perm(lambda g: dp_count - 1 - g)
    place = (group - core + dp_count) % dp_count
    quarter_of = jnp.array(quarters, I32)
    my_quarter = quarter_of[place]
    their_quarter = quarter_of[place ^ 1]

    def width_half(weight, first):
        return [
            lax.dynamic_slice_in_dim(weight[0], q * piece, piece, 0) for q in (first, first ^ 1)
        ]

    at = jnp.stack(
        [their_quarter, their_quarter ^ 1]
        + [(group - k + dp_count) % dp_count for k in range(1, dp_count)]
    ).astype(I32)
    gate_sent, up_sent, down_near, down_far, down_last = weight_slices(
        at * piece, w_gate, w_up, w_down, dp_count
    )
    gate_sent, up_sent, slot_table_rows, *rows = lax.optimization_barrier(
        (gate_sent, up_sent, slot_table_rows, *rows)
    )
    gate_came = lax.ppermute(gate_sent, ("dp", "expert"), weight_perm)
    up_came = lax.ppermute(up_sent, ("dp", "expert"), weight_perm)

    attended, attended_rest = attend(
        slot_table_rows, rows, cosine, sine, gain, new_rows[0], queries[0], most_slots
    )
    unit_start, home_rank, group_start, group_rank, start_column = (
        request_rows[i] for i in range(5)
    )
    own = owners == group
    unit_len = lengths // UNIT
    members = jnp.arange(request_total, dtype=I32)

    head_share = w_uv.shape[0]
    share = request_total // columns
    chips = columns // 2

    member_column = group_rank // share
    member_row = (
        (member_column % 2 ^ core) * (chips * share)
        + member_column // 2 * share
        + group_rank % share
    )
    is_row = own[None, :] & (member_row[None, :] == members[:, None])
    row_home = jnp.sum(jnp.where(is_row, start_column[None, :], 0), axis=1)
    row_slot = jnp.sum(jnp.where(is_row, home_rank[None, :], 0), axis=1)

    def in_order(part, first):
        count = part.shape[1]
        came = lax.all_to_all(part, "expert", split_axis=0, concat_axis=0, tiled=True)
        came = came.reshape(columns, head_share, count, LAT)
        cells = jnp.arange(columns * count, dtype=I32)
        wanted = row_home * count + row_slot - first
        inside = (row_slot >= first) & (row_slot < first + count)
        pick = (inside[:, None] & (wanted[:, None] == cells[None, :])).astype(BF)
        return [
            jnp.dot(
                pick, came[:, h].reshape(columns * count, LAT), preferred_element_type=F32
            ).astype(BF)
            for h in range(head_share)
        ]

    def spill(held):
        used = jnp.arange(SLOTS, most_slots, dtype=I32) < slot_table_rows[0, 4]
        rest = jnp.where(used[:, None, None], attended_rest, jnp.zeros((), BF))
        return [x + y for x, y in zip(held, in_order(rest.transpose(1, 0, 2), SLOTS))]

    by_head = in_order(attended, 0)
    by_head = lax.cond(jnp.max(home_rank) >= SLOTS, spill, lambda held: held, by_head)
    projected = jnp.concatenate(
        [
            jnp.dot(rows_h, w_uv[h], preferred_element_type=F32).astype(BF)
            for h, rows_h in enumerate(by_head)
        ],
        axis=1,
    )
    partial_sums = jnp.dot(
        projected, w_out, preferred_element_type=F32
    ).astype(BF)
    partial_sums, gate_came, up_came, down_near, down_last = lax.optimization_barrier(
        (partial_sums, gate_came, up_came, down_near, down_last)
    )
    down_near = shift(down_near, 1, dp_count, "dp")
    down_last = shift(down_last, 3, dp_count, "dp")

    keep = chips * share
    other = lax.ppermute(partial_sums[keep:], "expert", [(i, i ^ 1) for i in range(columns)])
    pair_sums = (partial_sums[:keep].astype(F32) + other.astype(F32)).astype(BF)
    chip_sums = lax.all_to_all(
        pair_sums.reshape(chips, share, model_width),
        "expert",
        split_axis=0,
        concat_axis=0,
        tiled=True,
        axis_index_groups=[[2 * i + c for i in range(chips)] for c in range(2)],
    )
    chip_sums, down_near, down_last, down_far = lax.optimization_barrier(
        (chip_sums, down_near, down_last, down_far)
    )
    down_far = shift(down_far, 2, dp_count, "dp")
    attention_out = jnp.sum(chip_sums.astype(F32), axis=0)
    residual = resid[0].astype(F32) + attention_out
    normed = (
        residual
        * lax.rsqrt(jnp.mean(residual * residual, axis=1, keepdims=True) + eps)
        * moe_gain[None, :]
    ).astype(BF)

    tokens = resid.shape[1]
    capacity = 2
    expert_ids = jnp.arange(columns, dtype=I32)
    matches = route_ids[0][:, :, None] == expert_ids[None, None, :]
    combine_weights = jnp.sum(jnp.where(matches, route_weights[0][:, :, None], 0.0), axis=1)
    routed = jnp.any(matches, axis=1)
    token_order = jnp.arange(tokens, dtype=I32)
    earlier = token_order[None, :] < token_order[:, None]
    slot_rank = jnp.sum(jnp.where(earlier[:, :, None], routed.astype(I32)[None, :, :], 0), axis=1)
    slot_ids = jnp.arange(capacity, dtype=I32)
    slot_table = routed.T[:, None, :] & (slot_rank.T[:, None, :] == slot_ids[None, :, None])
    table = slot_table.reshape(columns * capacity, tokens)
    even = (jnp.arange(columns * capacity, dtype=I32) // capacity % 2 == 0)[:, None]
    table = jnp.concatenate([table & even, table & ~even], axis=1).astype(BF)
    outgoing = []
    for f in range(dp_count):
        both = jnp.concatenate(
            [
                normed[:, q * piece : (q + 1) * piece]
                for q in (quarters[f], quarters[(f - 1) % dp_count])
            ],
            axis=0,
        )
        outgoing.append(jnp.dot(table, both, preferred_element_type=F32).astype(BF))
    outgoing = jnp.stack(outgoing).reshape(devices, capacity, piece)
    arrived = lax.all_to_all(
        outgoing, ("dp", "expert"), split_axis=0, concat_axis=0, tiled=True
    ).reshape(devices * capacity, piece)

    local_rows = local_units * UNIT
    to_rows = jnp.concatenate(
        [block[:local_rows].reshape(local_units, UNIT, width) for block in rows], axis=0
    ).transpose(1, 0, 2)
    arrived, down_far, to_rows = lax.optimization_barrier((arrived, down_far, to_rows))
    beside = lax.ppermute(arrived, ("dp", "expert"), token_perm)
    dealt = lax.all_to_all(to_rows, "expert", split_axis=0, concat_axis=0, tiled=True)

    gate_own, up_own = width_half(w_gate, my_quarter), width_half(w_up, my_quarter)
    weights = (gate_came, up_came, gate_own, up_own)
    first = [jnp.dot(arrived, weight[0], preferred_element_type=F32) for weight in weights]
    beside, *first = lax.optimization_barrier((beside, *first))
    gate_given, up_given, gate_sum, up_sum = (
        part + jnp.dot(beside, weight[1], preferred_element_type=F32)
        for part, weight in zip(first, weights)
    )
    given = jnp.concatenate([gate_given, up_given], axis=1).astype(BF)
    given = lax.ppermute(given, ("dp", "expert"), weight_perm).astype(F32)
    half = gate_sum.shape[1]
    hidden = (
        jax.nn.silu(gate_sum + given[:, :half]) * (up_sum + given[:, half:])
    ).astype(BF)
    hidden_all = jnp.concatenate(
        [hidden] + [shift(hidden, k, dp_count, "dp") for k in range(1, dp_count)], axis=1
    )
    hidden_all, dealt = lax.optimization_barrier((hidden_all, dealt))
    downs = jnp.concatenate([lax.dynamic_slice_in_dim(w_down[0], group * piece, piece, 1), down_near, down_far, down_last], axis=0)
    out = jnp.dot(hidden_all, downs, preferred_element_type=F32)
    returned = lax.all_to_all(
        out.astype(BF).reshape(devices, capacity, piece),
        ("dp", "expert"),
        split_axis=0,
        concat_axis=0,
        tiled=True,
    )

    slots = jnp.arange(pre_rows, dtype=I32)
    offset = slots[:, None] - group_start[None, :]
    covers = own[None, :] & (offset >= 0) & (offset < unit_len[None, :])
    slot_offset = jnp.sum(jnp.where(covers, offset, 0), axis=1)
    slot_unit = jnp.sum(jnp.where(covers, offset + unit_start[None, :], 0), axis=1)
    relative = (slot_unit // block_units - group + dp_count) % dp_count
    cache_place = (
        slot_unit % block_units // local_units * most_slots
        + relative * local_units
        + slot_unit % local_units
    )
    places = jnp.arange(columns * most_slots, dtype=I32)
    pick = (cache_place[:, None] == places[None, :]).astype(BF)
    raw_cache = jnp.dot(
        pick, dealt.reshape(columns * most_slots, width), preferred_element_type=F32
    )
    turned = []
    for table_rows in (cosine, sine):
        mine = jnp.asarray(table_rows).reshape(MOST + 1, UNIT, half_rope)
        mine = lax.dynamic_index_in_dim(mine, column, 1, keepdims=False)
        picked = mine[:1]
        for o in range(1, MOST):
            picked = jnp.where(slot_offset[:, None] == o, mine[o : o + 1], picked)
        turned.append(picked)
    cache_local = norm_rotate(raw_cache, *turned, gain)

    slot_weights = jnp.where(slot_table, combine_weights.T[:, None, :], 0.0)
    moe_sum = jnp.einsum(
        "xct,fxcd->tfd",
        slot_weights,
        returned.reshape(dp_count, columns, capacity, piece).astype(F32),
        precision=lax.Precision.HIGHEST,
    ).reshape(tokens, model_width)
    decoded = (residual + moe_sum).astype(BF)
    return (cache_local[None, None], decoded[None])


def solution(mesh):
    return jax.shard_map(
        shards,
        mesh=mesh,
        in_specs=(
            P(("dp", "expert"), None),
            P("dp", None, None),
            P(),
            P(),
            P(),
            P("dp", None, None, None),
            P("expert", None, None),
            P("expert", None),
            P("dp", "expert", None),
            P(),
            P("dp", "expert", None),
            P("dp", "expert", None),
            P("expert", None, "dp"),
            P("expert", None, "dp"),
            P("expert", "dp", None),
        ),
        out_specs=(P("dp", "expert", None, None), P("dp", "expert", None)),
        check_vma=False,
    )
```

```python
import jax
import jax.numpy as jnp
import numpy as np
from jax import lax
from jax.experimental import pallas as pl
from jax.experimental.pallas import tpu as pltpu
from jax.sharding import PartitionSpec as P

LAT = 512
UNIT = 32
MOST = 3
SLOTS = 8

eps = 1e-06
theta = 10000.0
score_scale = 192.0 ** (-0.5)
BF = jnp.bfloat16
F32 = jnp.float32
I32 = jnp.int32


def turn_table(half_width):
    exponent = -np.arange(half_width, dtype=np.float32) / np.float32(half_width)
    frequency = np.power(np.float32(theta), exponent).astype(np.float32)
    count = (MOST + 1) * UNIT
    angles = np.arange(count, dtype=np.float32)[:, None] * frequency[None, :]
    return np.cos(angles).astype(np.float32), np.sin(angles).astype(np.float32)


def norm_rotate(raw_rows, cosine, sine, kv_gain):
    raw_rows = raw_rows.astype(F32)
    latent = raw_rows[:, :LAT]
    half_width = cosine.shape[1]
    inverse = lax.rsqrt(jnp.mean(latent * latent, axis=1, keepdims=True) + eps)
    latent = latent * inverse * kv_gain
    lower = raw_rows[:, LAT : LAT + half_width]
    upper = raw_rows[:, LAT + half_width :]
    return jnp.concatenate(
        [latent, lower * cosine - upper * sine, upper * cosine + lower * sine], axis=1
    ).astype(BF)


def shift(x, step, size, axis):
    return lax.ppermute(x, axis, [((i + step) % size, i) for i in range(size)])


def table_kernel(where_ref, lengths_ref, owners_ref, slots_ref, rows_ref, *, sizes):
    dp_count, columns, local_units, near_units = sizes
    group, column = where_ref[0], where_ref[1]
    group_f, column_f = group.astype(F32), column.astype(F32)
    count = lengths_ref.shape[1]
    units = lengths_ref[...].astype(F32) * (1.0 / UNIT)
    owner = owners_ref[...].astype(F32)
    square = (count, count)
    down = lax.broadcasted_iota(I32, square, 0)
    along = lax.broadcasted_iota(I32, square, 1)
    before = down < along

    def upright(row):
        return jnp.sum(jnp.where(down == along, row, 0.0), axis=1, keepdims=True)

    def whole(x, size):
        return jnp.floor((x + 0.5) * (1.0 / size))

    units_up, owner_up = upright(units), upright(owner)
    start = jnp.sum(jnp.where(before, units_up, 0.0), axis=0, keepdims=True)
    start_source = whole(start, local_units)
    start_block = whole(start_source, columns)
    start_column = start_source - start_block * columns
    home = owner * columns + start_column
    home_up = upright(home)
    rank = jnp.sum(jnp.where(before & (home_up == home), 1.0, 0.0), axis=0, keepdims=True)
    own = owner == group_f
    own_before = before & (owner_up == group_f)
    group_start = jnp.sum(jnp.where(own_before, units_up, 0.0), axis=0, keepdims=True)
    group_rank = jnp.sum(jnp.where(own_before, 1.0, 0.0), axis=0, keepdims=True)

    lines = slots_ref.shape[0]
    line = lax.broadcasted_iota(I32, (lines, count), 0).astype(F32)
    here = home == group_f * columns + column_f
    is_slot = here & (rank == line)
    block = start_block - group_f
    block = jnp.where(block < 0.0, block + dp_count, block)
    place = block * near_units + (start - start_source * local_units)

    def pick(row):
        return jnp.sum(jnp.where(is_slot, row, 0.0), axis=1, keepdims=True)

    near = lax.broadcasted_iota(I32, (lines, 1), 0).astype(F32)
    near_block = whole(near, near_units)
    near_unit = near - near_block * near_units + column_f * local_units
    near_block = near_block + group_f
    near_block = jnp.where(near_block >= dp_count, near_block - dp_count, near_block)
    near_unit = near_unit + near_block * (columns * local_units)
    near_start = jnp.max(jnp.where(start <= near_unit, start, 0.0), axis=1, keepdims=True)
    near_offset = jnp.minimum(near_unit - near_start, MOST - 1.0)
    number = jnp.sum(jnp.where(here, 1.0, 0.0), axis=1, keepdims=True)
    lane = lax.broadcasted_iota(I32, slots_ref.shape, 1)
    packed = jnp.zeros(slots_ref.shape, F32)
    for i, value in enumerate((pick(place), pick(units), pick(group_rank), near_offset, number)):
        packed = jnp.where(lane == i, value, packed)
    slots_ref[...] = packed.astype(I32)
    rows_ref[...] = jnp.concatenate(
        [start, rank, group_start, group_rank, start_column] + [start] * 3, axis=0
    ).astype(I32)


def tables(where, lengths, owners, sizes):
    lines = sizes[0] * sizes[3]
    whole = pl.BlockSpec(memory_space=pltpu.VMEM)

    def body(*refs):
        table_kernel(*refs, sizes=sizes)

    return pl.pallas_call(
        body,
        out_shape=(
            jax.ShapeDtypeStruct((lines, 128), I32),
            jax.ShapeDtypeStruct((8, lengths.shape[0]), I32),
        ),
        in_specs=[pl.BlockSpec(memory_space=pltpu.SMEM), whole, whole],
        out_specs=(whole, whole),
        compiler_params=pltpu.CompilerParams(vmem_limit_bytes=32 * 1024 * 1024),
        cost_estimate=pl.CostEstimate(flops=1000, bytes_accessed=4096, transcendentals=0),
        name="tables",
    )(where, lengths[None, :], owners[None, :])


def slice_kernel(at_ref, gate_ref, up_ref, down_ref, half_out, *refs):
    downs, sems = refs[:-1], refs[-1]
    piece = half_out.shape[1]
    copies = []
    for i, weight in enumerate((gate_ref, gate_ref, up_ref, up_ref)):
        rows = pl.ds(pl.multiple_of(at_ref[i % 2] * piece, 128), piece)
        copies.append((weight.at[0, rows, :], half_out.at[i]))
    for i, out in enumerate(downs):
        columns = pl.ds(pl.multiple_of(at_ref[2 + i] * piece, 128), piece)
        copies.append((down_ref.at[0, :, columns], out))
    copies = [
        pltpu.make_async_copy(source, target, sems.at[i])
        for i, (source, target) in enumerate(copies)
    ]
    for copy in copies:
        copy.start()
    for copy in copies:
        copy.wait()


def weight_slices(at, w_gate, w_up, w_down, dp_count):
    piece = w_gate.shape[1] // dp_count
    away = pl.BlockSpec(memory_space=pltpu.HBM)
    whole = pl.BlockSpec(memory_space=pltpu.VMEM)
    halves = jax.ShapeDtypeStruct((4, piece, w_gate.shape[2]), BF)
    part = jax.ShapeDtypeStruct((w_down.shape[1], piece), BF)
    return pl.pallas_call(
        slice_kernel,
        out_shape=(halves,) + (part,) * (dp_count - 1),
        in_specs=[pl.BlockSpec(memory_space=pltpu.SMEM)] + [away] * 3,
        out_specs=(whole,) * dp_count,
        scratch_shapes=[pltpu.SemaphoreType.DMA((dp_count + 3,))],
        compiler_params=pltpu.CompilerParams(vmem_limit_bytes=32 * 1024 * 1024),
        cost_estimate=pl.CostEstimate(flops=1000, bytes_accessed=4096, transcendentals=0),
        name="weight_slices",
    )(at, w_gate, w_up, w_down)


def attend_kernel(slots_ref, *refs, blocks):
    rows_in = refs[:blocks]
    cos_ref, sin_ref, gain_ref, new_ref, query_ref = refs[blocks : blocks + 5]
    out_ref, rest_ref, keys, query, fresh, held_out, sems = refs[blocks + 5 :]
    number = slots_ref[0, 4]

    def fetch(slot):
        return pltpu.make_async_copy(
            query_ref.at[slots_ref[slot, 2]], query.at[slot], sems.at[slot]
        )

    @pl.loop(0, number)
    def _(slot):
        fetch(slot).start()

    gain = gain_ref[...]
    unit = 0
    for ref in rows_in:
        for first in range(0, ref.shape[0], UNIT):
            span = pl.ds(pl.multiple_of(slots_ref[unit, 3] * UNIT, UNIT), UNIT)
            keys[unit * UNIT : (unit + 1) * UNIT, :] = norm_rotate(
                ref[first : first + UNIT, :], cos_ref[span, :], sin_ref[span, :], gain
            )
            unit += 1
    fresh[...] = new_ref[...].astype(F32)
    held_out[...] = jnp.zeros(held_out.shape, F32)

    heads = out_ref.shape[0]
    sent = out_ref.shape[1]
    window = MOST * UNIT
    lanes = window + UNIT
    lane = lax.broadcasted_iota(I32, (heads, lanes), 1)

    def one(slot):
        fetch(slot).wait()
        count = slots_ref[slot, 1]
        own = keys[pl.ds(pl.multiple_of(slots_ref[slot, 0] * UNIT, UNIT), window), :]
        at = pl.ds(count * UNIT, 1)
        new = norm_rotate(
            fresh[pl.ds(slots_ref[slot, 2], 1), :], cos_ref[at, :], sin_ref[at, :], gain
        )
        new = jnp.broadcast_to(new.astype(F32), (UNIT, own.shape[1])).astype(BF)
        held = jnp.concatenate([own, new], axis=0)
        scores = (
            lax.dot_general(
                query[slot], held, (((1,), (1,)), ((), ())), preferred_element_type=F32
            )
            * score_scale
        )
        live = (lane < count * UNIT) | (lane == window)
        scores = jnp.where(live, scores, -jnp.inf)
        weights = jnp.exp(scores - jnp.max(scores, axis=1, keepdims=True))
        total = jnp.sum(weights, axis=1, keepdims=True)
        mixture = jnp.dot(weights.astype(BF), held[:, :LAT], preferred_element_type=F32)
        return mixture / total

    @pl.loop(0, jnp.minimum(number, sent))
    def _(slot):
        held_out[slot] = one(slot)

    out_ref[...] = jnp.swapaxes(held_out[...], 0, 1).astype(BF)

    @pl.loop(sent, number)
    def _(slot):
        rest_ref[slot - sent] = one(slot).astype(BF)


def attend(slots, rows, cosine, sine, gain, new_rows, queries, most_slots):
    heads = queries.shape[1]
    blocks = len(rows)
    total_rows = sum(block.shape[0] for block in rows)
    whole = pl.BlockSpec(memory_space=pltpu.VMEM)

    def body(*refs):
        attend_kernel(*refs, blocks=blocks)

    return pl.pallas_call(
        body,
        out_shape=(
            jax.ShapeDtypeStruct((heads, SLOTS, LAT), BF),
            jax.ShapeDtypeStruct((most_slots - SLOTS, heads, LAT), BF),
        ),
        in_specs=[pl.BlockSpec(memory_space=pltpu.SMEM)]
        + [whole] * (blocks + 4)
        + [pl.BlockSpec(memory_space=pltpu.HBM)],
        out_specs=(whole, whole),
        scratch_shapes=[
            pltpu.VMEM((total_rows, queries.shape[2]), BF),
            pltpu.VMEM((most_slots,) + queries.shape[1:], BF),
            pltpu.VMEM(new_rows.shape, F32),
            pltpu.VMEM((SLOTS, heads, LAT), F32),
            pltpu.SemaphoreType.DMA((most_slots,)),
        ],
        compiler_params=pltpu.CompilerParams(vmem_limit_bytes=32 * 1024 * 1024),
        cost_estimate=pl.CostEstimate(
            flops=10**8, bytes_accessed=4 * 10**6, transcendentals=10**5
        ),
        name="attend",
    )(slots, *rows, cosine, sine, gain, new_rows, queries)


def shards(
    latent_rows,
    new_rows,
    kv_gain,
    lengths,
    owners,
    queries,
    w_uv,
    w_out,
    resid,
    moe_gain,
    route_ids,
    route_weights,
    w_gate,
    w_up,
    w_down,
):
    dp_count = lax.axis_size("dp")
    columns = lax.axis_size("expert")
    devices = dp_count * columns
    group = lax.axis_index("dp")
    column = lax.axis_index("expert")
    core = column % 2
    pre_rows, width = latent_rows.shape
    half_rope = (width - LAT) // 2
    local_units = pre_rows // UNIT
    block_units = columns * local_units
    gain = kv_gain[None, :]

    border = (MOST - 1) * UNIT
    next_rows = lax.ppermute(
        latent_rows[:border],
        ("dp", "expert"),
        [((i + 1) % devices, i) for i in range(devices)],
    )
    near_rows = jnp.concatenate([latent_rows, next_rows], axis=0)
    near_rows, late_group = lax.optimization_barrier((near_rows, group))
    rows = [near_rows] + [shift(near_rows, k, dp_count, "dp") for k in range(1, dp_count)]

    request_total = queries.shape[1]
    most_slots = dp_count * local_units
    near_units = local_units + MOST - 1
    where = jnp.stack([group, column]).astype(I32)
    slot_table_rows, request_rows = tables(
        where, lengths, owners, (dp_count, columns, local_units, near_units)
    )
    cosine, sine = turn_table(half_rope)

    model_width = w_out.shape[1]
    piece = model_width // dp_count
    halves = (0, 1, 1, 0)
    quarters = (0, 2, 3, 1)

    def pair_perm(partner):
        perm = []
        for f in range(dp_count):
            for x in range(columns):
                g = (f - x % 2) % dp_count
                perm.append((f * columns + x, (partner(g) + x % 2) % dp_count * columns + x))
        return perm

    weight_perm = pair_perm(lambda g: g ^ 1)
    token_perm = pair_perm(lambda g: dp_count - 1 - g)
    place = (group - core + dp_count) % dp_count

    def quarter_of(g):
        return jnp.where(g == 0, 0, jnp.where(g == 1, 2, jnp.where(g == 2, 3, 1)))

    my_quarter = quarter_of(place)
    their_quarter = quarter_of(place ^ 1)

    def width_half(weight, first):
        return [
            lax.dynamic_slice_in_dim(weight[0], q * piece, piece, 0) for q in (first, first ^ 1)
        ]

    at = jnp.stack(
        [their_quarter, their_quarter ^ 1]
        + [(late_group - k + dp_count) % dp_count for k in range(1, dp_count)]
    ).astype(I32)
    half_sent, down_near, down_far, down_last = weight_slices(at, w_gate, w_up, w_down, dp_count)
    half_sent, slot_table_rows, *rows = lax.optimization_barrier(
        (half_sent, slot_table_rows, *rows)
    )
    half_came = lax.ppermute(half_sent, ("dp", "expert"), weight_perm)

    attended, attended_rest = attend(
        slot_table_rows, rows, cosine, sine, gain, new_rows[0], queries[0], most_slots
    )
    unit_start, home_rank, group_start, group_rank, start_column = (
        request_rows[i] for i in range(5)
    )
    own = owners == group
    unit_len = lengths // UNIT
    members = jnp.arange(request_total, dtype=I32)

    head_share = w_uv.shape[0]
    share = request_total // columns
    chips = columns // 2

    member_column = group_rank // share
    member_row = (
        (member_column % 2 ^ core) * (chips * share)
        + member_column // 2 * share
        + group_rank % share
    )
    is_row = own[None, :] & (member_row[None, :] == members[:, None])
    row_home = jnp.sum(jnp.where(is_row, start_column[None, :], 0), axis=1)
    row_slot = jnp.sum(jnp.where(is_row, home_rank[None, :], 0), axis=1)

    def in_order(part, first):
        count = part.shape[1]
        came = lax.all_to_all(part, "expert", split_axis=0, concat_axis=0, tiled=True)
        came = came.reshape(columns, head_share, count, LAT)
        cells = jnp.arange(columns * count, dtype=I32)
        wanted = row_home * count + row_slot - first
        inside = (row_slot >= first) & (row_slot < first + count)
        pick = (inside[:, None] & (wanted[:, None] == cells[None, :])).astype(BF)
        return [
            jnp.dot(
                pick, came[:, h].reshape(columns * count, LAT), preferred_element_type=F32
            ).astype(BF)
            for h in range(head_share)
        ]

    def spill(held):
        used = jnp.arange(SLOTS, most_slots, dtype=I32) < slot_table_rows[0, 4]
        rest = jnp.where(used[:, None, None], attended_rest, jnp.zeros((), BF))
        return [x + y for x, y in zip(held, in_order(rest.transpose(1, 0, 2), SLOTS))]

    by_head = in_order(attended, 0)
    by_head = lax.cond(jnp.max(home_rank) >= SLOTS, spill, lambda held: held, by_head)
    projected = jnp.concatenate(
        [
            jnp.dot(rows_h, w_uv[h], preferred_element_type=F32).astype(BF)
            for h, rows_h in enumerate(by_head)
        ],
        axis=1,
    )
    partial_sums = jnp.dot(
        projected, w_out, preferred_element_type=F32
    ).astype(BF)
    partial_sums, down_near, down_last = lax.optimization_barrier(
        (partial_sums, down_near, down_last)
    )
    down_near = shift(down_near, 1, dp_count, "dp")
    down_last = shift(down_last, 3, dp_count, "dp")

    keep = chips * share
    other = lax.ppermute(partial_sums[keep:], "expert", [(i, i ^ 1) for i in range(columns)])
    pair_sums = (partial_sums[:keep].astype(F32) + other.astype(F32)).astype(BF)
    chip_sums = lax.all_to_all(
        pair_sums.reshape(chips, share, model_width),
        "expert",
        split_axis=0,
        concat_axis=0,
        tiled=True,
        axis_index_groups=[[2 * i + c for i in range(chips)] for c in range(2)],
    )
    chip_sums, half_came, down_far = lax.optimization_barrier((chip_sums, half_came, down_far))
    down_far = shift(down_far, 2, dp_count, "dp")
    attention_out = jnp.sum(chip_sums.astype(F32), axis=0)
    residual = resid[0].astype(F32) + attention_out
    normed = (
        residual
        * lax.rsqrt(jnp.mean(residual * residual, axis=1, keepdims=True) + eps)
        * moe_gain[None, :]
    ).astype(BF)

    tokens = resid.shape[1]
    capacity = 2
    expert_ids = jnp.arange(columns, dtype=I32)
    matches = route_ids[0][:, :, None] == expert_ids[None, None, :]
    combine_weights = jnp.sum(jnp.where(matches, route_weights[0][:, :, None], 0.0), axis=1)
    routed = jnp.any(matches, axis=1)
    token_order = jnp.arange(tokens, dtype=I32)
    earlier = token_order[None, :] < token_order[:, None]
    slot_rank = jnp.sum(jnp.where(earlier[:, :, None], routed.astype(I32)[None, :, :], 0), axis=1)
    slot_ids = jnp.arange(capacity, dtype=I32)
    slot_table = routed.T[:, None, :] & (slot_rank.T[:, None, :] == slot_ids[None, :, None])
    table = slot_table.reshape(columns * capacity, tokens)
    even = (jnp.arange(columns * capacity, dtype=I32) // capacity % 2 == 0)[:, None]
    table = jnp.concatenate([table & even, table & ~even], axis=1).astype(BF)
    outgoing = []
    for f in range(dp_count):
        both = jnp.concatenate(
            [
                normed[:, q * piece : (q + 1) * piece]
                for q in (quarters[f], quarters[(f - 1) % dp_count])
            ],
            axis=0,
        )
        outgoing.append(jnp.dot(table, both, preferred_element_type=F32).astype(BF))
    outgoing = jnp.stack(outgoing).reshape(devices, capacity, piece)
    arrived = lax.all_to_all(
        outgoing, ("dp", "expert"), split_axis=0, concat_axis=0, tiled=True
    ).reshape(devices * capacity, piece)

    local_rows = local_units * UNIT
    to_rows = jnp.concatenate(
        [block[:local_rows].reshape(local_units, UNIT, width) for block in rows], axis=0
    ).transpose(1, 0, 2)
    arrived, down_near, down_last, to_rows = lax.optimization_barrier(
        (arrived, down_near, down_last, to_rows)
    )
    beside = lax.ppermute(arrived, ("dp", "expert"), token_perm)
    dealt = lax.all_to_all(to_rows, "expert", split_axis=0, concat_axis=0, tiled=True)

    gate_own, up_own = width_half(w_gate, my_quarter), width_half(w_up, my_quarter)
    weights = (half_came[:2], half_came[2:], gate_own, up_own)
    first = [jnp.dot(arrived, weight[0], preferred_element_type=F32) for weight in weights]
    beside, *first = lax.optimization_barrier((beside, *first))
    gate_given, up_given, gate_sum, up_sum = (
        part + jnp.dot(beside, weight[1], preferred_element_type=F32)
        for part, weight in zip(first, weights)
    )
    given = jnp.concatenate([gate_given, up_given], axis=1).astype(BF)
    given = lax.ppermute(given, ("dp", "expert"), weight_perm).astype(F32)
    half = gate_sum.shape[1]
    hidden = (
        jax.nn.silu(gate_sum + given[:, :half]) * (up_sum + given[:, half:])
    ).astype(BF)
    hidden_all = jnp.concatenate(
        [hidden] + [shift(hidden, k, dp_count, "dp") for k in range(1, dp_count)], axis=1
    )
    hidden_all, dealt = lax.optimization_barrier((hidden_all, dealt))
    downs = jnp.concatenate([lax.dynamic_slice_in_dim(w_down[0], group * piece, piece, 1), down_near, down_far, down_last], axis=0)
    out = jnp.dot(hidden_all, downs, preferred_element_type=F32)
    returned = lax.all_to_all(
        out.astype(BF).reshape(devices, capacity, piece),
        ("dp", "expert"),
        split_axis=0,
        concat_axis=0,
        tiled=True,
    )

    slots = jnp.arange(pre_rows, dtype=I32)
    offset = slots[:, None] - group_start[None, :]
    covers = own[None, :] & (offset >= 0) & (offset < unit_len[None, :])
    slot_offset = jnp.sum(jnp.where(covers, offset, 0), axis=1)
    slot_unit = jnp.sum(jnp.where(covers, offset + unit_start[None, :], 0), axis=1)
    relative = (slot_unit // block_units - group + dp_count) % dp_count
    cache_place = (
        slot_unit % block_units // local_units * most_slots
        + relative * local_units
        + slot_unit % local_units
    )
    places = jnp.arange(columns * most_slots, dtype=I32)
    pick = (cache_place[:, None] == places[None, :]).astype(BF)
    raw_cache = jnp.dot(
        pick, dealt.reshape(columns * most_slots, width), preferred_element_type=F32
    )
    turned = []
    for table_rows in (cosine, sine):
        mine = jnp.asarray(table_rows).reshape(MOST + 1, UNIT, half_rope)
        mine = lax.dynamic_index_in_dim(mine, column, 1, keepdims=False)
        picked = mine[:1]
        for o in range(1, MOST):
            picked = jnp.where(slot_offset[:, None] == o, mine[o : o + 1], picked)
        turned.append(picked)
    cache_local = norm_rotate(raw_cache, *turned, gain)

    slot_weights = jnp.where(slot_table, combine_weights.T[:, None, :], 0.0)
    moe_sum = jnp.einsum(
        "xct,fxcd->tfd",
        slot_weights,
        returned.reshape(dp_count, columns, capacity, piece).astype(F32),
        precision=lax.Precision.HIGHEST,
    ).reshape(tokens, model_width)
    decoded = (residual + moe_sum).astype(BF)
    return (cache_local[None, None], decoded[None])


def solution(mesh):
    return jax.shard_map(
        shards,
        mesh=mesh,
        in_specs=(
            P(("dp", "expert"), None),
            P("dp", None, None),
            P(),
            P(),
            P(),
            P("dp", None, None, None),
            P("expert", None, None),
            P("expert", None),
            P("dp", "expert", None),
            P(),
            P("dp", "expert", None),
            P("dp", "expert", None),
            P("expert", None, "dp"),
            P("expert", None, "dp"),
            P("expert", "dp", None),
        ),
        out_specs=(P("dp", "expert", None, None), P("dp", "expert", None)),
        check_vma=False,
    )
```

```python
import jax
import jax.numpy as jnp
import numpy as np
from jax import lax
from jax.experimental import pallas as pl
from jax.experimental.pallas import tpu as pltpu
from jax.sharding import PartitionSpec as P

LAT = 512
UNIT = 32
MOST = 3
SLOTS = 8

eps = 1e-06
theta = 10000.0
score_scale = 192.0 ** (-0.5)
BF = jnp.bfloat16
F32 = jnp.float32
I32 = jnp.int32


def turn_table(half_width):
    exponent = -np.arange(half_width, dtype=np.float32) / np.float32(half_width)
    frequency = np.power(np.float32(theta), exponent).astype(np.float32)
    count = (MOST + 1) * UNIT
    angles = np.arange(count, dtype=np.float32)[:, None] * frequency[None, :]
    return np.cos(angles).astype(np.float32), np.sin(angles).astype(np.float32)


def norm_rotate(raw_rows, cosine, sine, kv_gain):
    raw_rows = raw_rows.astype(F32)
    latent = raw_rows[:, :LAT]
    half_width = cosine.shape[1]
    inverse = lax.rsqrt(jnp.mean(latent * latent, axis=1, keepdims=True) + eps)
    latent = latent * inverse * kv_gain
    lower = raw_rows[:, LAT : LAT + half_width]
    upper = raw_rows[:, LAT + half_width :]
    return jnp.concatenate(
        [latent, lower * cosine - upper * sine, upper * cosine + lower * sine], axis=1
    ).astype(BF)


def shift(x, step, size, axis):
    return lax.ppermute(x, axis, [((i + step) % size, i) for i in range(size)])


def table_kernel(where_ref, lengths_ref, owners_ref, slots_ref, rows_ref, cells_ref, *, sizes):
    dp_count, columns, local_units, near_units, share = sizes
    group, column = where_ref[0], where_ref[1]
    group_f, column_f = group.astype(F32), column.astype(F32)
    count = lengths_ref.shape[1]
    units = lengths_ref[...].astype(F32) * (1.0 / UNIT)
    owner = owners_ref[...].astype(F32)
    square = (count, count)
    down = lax.broadcasted_iota(I32, square, 0)
    along = lax.broadcasted_iota(I32, square, 1)
    before = down < along

    def upright(row):
        return jnp.sum(jnp.where(down == along, row, 0.0), axis=1, keepdims=True)

    def whole(x, size):
        return jnp.floor((x + 0.5) * (1.0 / size))

    units_up, owner_up = upright(units), upright(owner)
    start = jnp.sum(jnp.where(before, units_up, 0.0), axis=0, keepdims=True)
    start_source = whole(start, local_units)
    start_block = whole(start_source, columns)
    start_column = start_source - start_block * columns
    home = owner * columns + start_column
    home_up = upright(home)
    rank = jnp.sum(jnp.where(before & (home_up == home), 1.0, 0.0), axis=0, keepdims=True)
    own = owner == group_f
    own_before = before & (owner_up == group_f)
    group_start = jnp.sum(jnp.where(own_before, units_up, 0.0), axis=0, keepdims=True)
    group_rank = jnp.sum(jnp.where(own_before, 1.0, 0.0), axis=0, keepdims=True)

    lines = slots_ref.shape[0]
    line = lax.broadcasted_iota(I32, (lines, count), 0).astype(F32)
    here = home == group_f * columns + column_f
    is_slot = here & (rank == line)
    block = start_block - group_f
    block = jnp.where(block < 0.0, block + dp_count, block)
    place = block * near_units + (start - start_source * local_units)

    def pick(row):
        return jnp.sum(jnp.where(is_slot, row, 0.0), axis=1, keepdims=True)

    near = lax.broadcasted_iota(I32, (lines, 1), 0).astype(F32)
    near_block = whole(near, near_units)
    near_unit = near - near_block * near_units + column_f * local_units
    near_block = near_block + group_f
    near_block = jnp.where(near_block >= dp_count, near_block - dp_count, near_block)
    near_unit = near_unit + near_block * (columns * local_units)
    near_start = jnp.max(jnp.where(start <= near_unit, start, 0.0), axis=1, keepdims=True)
    near_offset = jnp.minimum(near_unit - near_start, MOST - 1.0)
    number = jnp.sum(jnp.where(here, 1.0, 0.0), axis=1, keepdims=True)
    lane = lax.broadcasted_iota(I32, slots_ref.shape, 1)
    packed = jnp.zeros(slots_ref.shape, F32)
    for i, value in enumerate((pick(place), pick(units), pick(group_rank), near_offset, number)):
        packed = jnp.where(lane == i, value, packed)
    slots_ref[...] = packed.astype(I32)
    rows_ref[...] = jnp.concatenate(
        [start, rank, group_start, group_rank, start_column] + [start] * 3, axis=0
    ).astype(I32)

    member_column = whole(group_rank, share)
    member_chip = whole(member_column, 2)
    other_core = jnp.abs(member_column - 2.0 * member_chip - (column % 2).astype(F32))
    row = (other_core * (columns // 2) + member_chip) * share + (
        group_rank - member_column * share
    )
    lines = cells_ref.shape[0]
    line = lax.broadcasted_iota(I32, (lines, count), 0).astype(F32)
    cell = jnp.where(rank < SLOTS, start_column * SLOTS + rank, -1.0)
    found = jnp.sum(jnp.where(own & (row == line), cell, 0.0), axis=1, keepdims=True)
    cells_ref[...] = jnp.broadcast_to(found, cells_ref.shape).astype(I32)


def tables(where, lengths, owners, sizes):
    lines = sizes[0] * sizes[3]
    whole = pl.BlockSpec(memory_space=pltpu.VMEM)

    def body(*refs):
        table_kernel(*refs, sizes=sizes)

    return pl.pallas_call(
        body,
        out_shape=(
            jax.ShapeDtypeStruct((lines, 128), I32),
            jax.ShapeDtypeStruct((8, lengths.shape[0]), I32),
            jax.ShapeDtypeStruct((sizes[1] * sizes[4], 128), I32),
        ),
        in_specs=[pl.BlockSpec(memory_space=pltpu.SMEM), whole, whole],
        out_specs=(whole, whole, whole),
        compiler_params=pltpu.CompilerParams(vmem_limit_bytes=32 * 1024 * 1024),
        cost_estimate=pl.CostEstimate(flops=1000, bytes_accessed=4096, transcendentals=0),
        name="tables",
    )(where, lengths[None, :], owners[None, :])


def slice_kernel(at_ref, gate_ref, up_ref, down_ref, gate_out, up_out, *refs):
    downs, sems = refs[:-1], refs[-1]
    piece = gate_out.shape[1]
    copies = []
    for weight, out in ((gate_ref, gate_out), (up_ref, up_out)):
        for i in range(2):
            rows = pl.ds(pl.multiple_of(at_ref[i] * piece, 128), piece)
            copies.append((weight.at[0, rows, :], out.at[i]))
    for i, out in enumerate(downs):
        columns = pl.ds(pl.multiple_of(at_ref[2 + i] * piece, 128), piece)
        copies.append((down_ref.at[0, :, columns], out))
    copies = [
        pltpu.make_async_copy(source, target, sems.at[i])
        for i, (source, target) in enumerate(copies)
    ]
    for copy in copies:
        copy.start()
    for copy in copies:
        copy.wait()


def weight_slices(at, w_gate, w_up, w_down, dp_count):
    piece = w_gate.shape[1] // dp_count
    away = pl.BlockSpec(memory_space=pltpu.HBM)
    whole = pl.BlockSpec(memory_space=pltpu.VMEM)
    halves = jax.ShapeDtypeStruct((2, piece, w_gate.shape[2]), BF)
    part = jax.ShapeDtypeStruct((w_down.shape[1], piece), BF)
    return pl.pallas_call(
        slice_kernel,
        out_shape=(halves, halves) + (part,) * (dp_count - 1),
        in_specs=[pl.BlockSpec(memory_space=pltpu.SMEM)] + [away] * 3,
        out_specs=(whole,) * (dp_count + 1),
        scratch_shapes=[pltpu.SemaphoreType.DMA((dp_count + 3,))],
        compiler_params=pltpu.CompilerParams(vmem_limit_bytes=32 * 1024 * 1024),
        cost_estimate=pl.CostEstimate(flops=1000, bytes_accessed=4096, transcendentals=0),
        name="weight_slices",
    )(at, w_gate, w_up, w_down)


def attend_kernel(slots_ref, *refs, blocks):
    rows_in = refs[:blocks]
    cos_ref, sin_ref, gain_ref, new_ref, query_ref = refs[blocks : blocks + 5]
    out_ref, rest_ref, keys, query, fresh, held_out, sems = refs[blocks + 5 :]
    number = slots_ref[0, 4]

    def fetch(slot):
        return pltpu.make_async_copy(
            query_ref.at[slots_ref[slot, 2]], query.at[slot], sems.at[slot]
        )

    @pl.loop(0, number)
    def _(slot):
        fetch(slot).start()

    gain = gain_ref[...]
    unit = 0
    for ref in rows_in:
        for first in range(0, ref.shape[0], UNIT):
            span = pl.ds(pl.multiple_of(slots_ref[unit, 3] * UNIT, UNIT), UNIT)
            keys[unit * UNIT : (unit + 1) * UNIT, :] = norm_rotate(
                ref[first : first + UNIT, :], cos_ref[span, :], sin_ref[span, :], gain
            )
            unit += 1
    fresh[...] = new_ref[...].astype(F32)

    heads = out_ref.shape[0]
    sent = out_ref.shape[1]
    window = MOST * UNIT
    lanes = window + UNIT
    lane = lax.broadcasted_iota(I32, (heads, lanes), 1)

    def one(slot):
        count = slots_ref[slot, 1]
        own = keys[pl.ds(pl.multiple_of(slots_ref[slot, 0] * UNIT, UNIT), window), :]
        at = pl.ds(count * UNIT, 1)
        new = norm_rotate(
            fresh[pl.ds(slots_ref[slot, 2], 1), :], cos_ref[at, :], sin_ref[at, :], gain
        )
        new = jnp.broadcast_to(new.astype(F32), (UNIT, own.shape[1])).astype(BF)
        held = jnp.concatenate([own, new], axis=0)
        scores = (
            lax.dot_general(
                query[slot], held, (((1,), (1,)), ((), ())), preferred_element_type=F32
            )
            * score_scale
        )
        live = (lane < count * UNIT) | (lane == window)
        scores = jnp.where(live, scores, -jnp.inf)
        weights = jnp.exp(scores - jnp.max(scores, axis=1, keepdims=True))
        total = jnp.sum(weights, axis=1, keepdims=True)
        mixture = jnp.dot(weights.astype(BF), held[:, :LAT], preferred_element_type=F32)
        return mixture / total

    @pl.loop(0, number)
    def _(slot):
        fetch(slot).wait()

    for slot in range(sent):
        held_out[slot] = jnp.where(slot < number, one(slot), 0.0)

    out_ref[...] = jnp.swapaxes(held_out[...], 0, 1).astype(BF)

    @pl.loop(sent, number)
    def _(slot):
        rest_ref[slot - sent] = one(slot).astype(BF)


def attend(slots, rows, cosine, sine, gain, new_rows, queries, most_slots):
    heads = queries.shape[1]
    blocks = len(rows)
    total_rows = sum(block.shape[0] for block in rows)
    whole = pl.BlockSpec(memory_space=pltpu.VMEM)

    def body(*refs):
        attend_kernel(*refs, blocks=blocks)

    return pl.pallas_call(
        body,
        out_shape=(
            jax.ShapeDtypeStruct((heads, SLOTS, LAT), BF),
            jax.ShapeDtypeStruct((most_slots - SLOTS, heads, LAT), BF),
        ),
        in_specs=[pl.BlockSpec(memory_space=pltpu.SMEM)]
        + [whole] * (blocks + 4)
        + [pl.BlockSpec(memory_space=pltpu.HBM)],
        out_specs=(whole, whole),
        scratch_shapes=[
            pltpu.VMEM((total_rows, queries.shape[2]), BF),
            pltpu.VMEM((most_slots,) + queries.shape[1:], BF),
            pltpu.VMEM(new_rows.shape, F32),
            pltpu.VMEM((SLOTS, heads, LAT), F32),
            pltpu.SemaphoreType.DMA((most_slots,)),
        ],
        compiler_params=pltpu.CompilerParams(vmem_limit_bytes=32 * 1024 * 1024),
        cost_estimate=pl.CostEstimate(
            flops=10**8, bytes_accessed=4 * 10**6, transcendentals=10**5
        ),
        name="attend",
    )(slots, *rows, cosine, sine, gain, new_rows, queries)


def project_kernel(cells_ref, came_ref, more_ref, uv_ref, weight_ref, mine_ref, other_ref):
    requests = cells_ref.shape[0]
    sources, heads, slots, _ = came_ref.shape
    cells = sources * slots
    pick = cells_ref[:, :1] == lax.broadcasted_iota(I32, (requests, cells), 1)
    pick = jnp.where(pick, 1.0, 0.0).astype(BF)
    projected = []
    for h in range(heads):
        came = came_ref[:, h].astype(F32).reshape(cells, LAT).astype(BF)
        rows = jnp.dot(pick, came, preferred_element_type=F32) + more_ref[h].astype(F32)
        projected.append(
            jnp.dot(rows.astype(BF), uv_ref[h], preferred_element_type=F32).astype(BF)
        )
    projected = jnp.concatenate(projected, axis=1)
    keep = mine_ref.shape[0]
    step = weight_ref.shape[1] // 4
    for first in range(0, weight_ref.shape[1], step):
        span = slice(first, first + step)
        sums = jnp.dot(projected, weight_ref[:, span], preferred_element_type=F32).astype(BF)
        mine_ref[:, span] = sums[:keep]
        other_ref[:, span] = sums[keep:]


def project(cells, came, more, w_uv, w_out):
    whole = pl.BlockSpec(memory_space=pltpu.VMEM)
    half = jax.ShapeDtypeStruct((cells.shape[0] // 2, w_out.shape[1]), BF)
    return pl.pallas_call(
        project_kernel,
        out_shape=(half, half),
        in_specs=[whole] * 5,
        out_specs=(whole, whole),
        compiler_params=pltpu.CompilerParams(vmem_limit_bytes=32 * 1024 * 1024),
        cost_estimate=pl.CostEstimate(
            flops=4 * 10**8, bytes_accessed=6 * 10**6, transcendentals=0
        ),
        name="project",
    )(cells, came, more, w_uv, w_out)


def pair_kernel(mine_ref, other_ref, out_ref):
    chips, share, width = out_ref.shape
    step = width // 4
    for first in range(0, width, step):
        span = slice(first, first + step)
        sums = mine_ref[:, span].astype(F32) + other_ref[:, span].astype(F32)
        for chip in range(chips):
            out_ref[chip, :, span] = sums[chip * share : (chip + 1) * share].astype(BF)


def pair_sum(mine, other, chips):
    whole = pl.BlockSpec(memory_space=pltpu.VMEM)
    return pl.pallas_call(
        pair_kernel,
        out_shape=jax.ShapeDtypeStruct((chips, mine.shape[0] // chips, mine.shape[1]), BF),
        in_specs=[whole] * 2,
        out_specs=whole,
        compiler_params=pltpu.CompilerParams(vmem_limit_bytes=32 * 1024 * 1024),
        cost_estimate=pl.CostEstimate(
            flops=4 * 10**5, bytes_accessed=2 * 10**6, transcendentals=0
        ),
        name="pair_sum",
    )(mine, other)


def shards(
    latent_rows,
    new_rows,
    kv_gain,
    lengths,
    owners,
    queries,
    w_uv,
    w_out,
    resid,
    moe_gain,
    route_ids,
    route_weights,
    w_gate,
    w_up,
    w_down,
):
    dp_count = lax.axis_size("dp")
    columns = lax.axis_size("expert")
    devices = dp_count * columns
    group = lax.axis_index("dp")
    column = lax.axis_index("expert")
    core = column % 2
    pre_rows, width = latent_rows.shape
    half_rope = (width - LAT) // 2
    local_units = pre_rows // UNIT
    block_units = columns * local_units
    gain = kv_gain[None, :]

    border = (MOST - 1) * UNIT
    next_rows = lax.ppermute(
        latent_rows[:border],
        ("dp", "expert"),
        [((i + 1) % devices, i) for i in range(devices)],
    )
    near_rows = jnp.concatenate([latent_rows, next_rows], axis=0)
    near_rows, late_group = lax.optimization_barrier((near_rows, group))
    rows = [near_rows] + [shift(near_rows, k, dp_count, "dp") for k in range(1, dp_count)]

    request_total = queries.shape[1]
    most_slots = dp_count * local_units
    near_units = local_units + MOST - 1
    where = jnp.stack([group, column]).astype(I32)
    share = request_total // columns
    slot_table_rows, request_rows, cells = tables(
        where, lengths, owners, (dp_count, columns, local_units, near_units, share)
    )
    cosine, sine = turn_table(half_rope)

    model_width = w_out.shape[1]
    piece = model_width // dp_count
    halves = (0, 1, 1, 0)
    quarters = (0, 2, 3, 1)

    def pair_perm(partner):
        perm = []
        for f in range(dp_count):
            for x in range(columns):
                g = (f - x % 2) % dp_count
                perm.append((f * columns + x, (partner(g) + x % 2) % dp_count * columns + x))
        return perm

    weight_perm = pair_perm(lambda g: g ^ 1)
    token_perm = pair_perm(lambda g: dp_count - 1 - g)
    place = (group - core + dp_count) % dp_count

    def quarter_of(g):
        return jnp.where(g == 0, 0, jnp.where(g == 1, 2, jnp.where(g == 2, 3, 1)))

    my_quarter = quarter_of(place)
    their_quarter = quarter_of(place ^ 1)

    def width_half(weight, first):
        return [
            lax.dynamic_slice_in_dim(weight[0], q * piece, piece, 0) for q in (first, first ^ 1)
        ]

    at = jnp.stack(
        [their_quarter, their_quarter ^ 1]
        + [(late_group - k + dp_count) % dp_count for k in range(1, dp_count)]
    ).astype(I32)
    gate_sent, up_sent, down_near, down_far, down_last = weight_slices(
        at, w_gate, w_up, w_down, dp_count
    )
    gate_sent, up_sent, slot_table_rows, *rows = lax.optimization_barrier(
        (gate_sent, up_sent, slot_table_rows, *rows)
    )
    gate_came = lax.ppermute(gate_sent, ("dp", "expert"), weight_perm)
    up_came = lax.ppermute(up_sent, ("dp", "expert"), weight_perm)

    attended, attended_rest = attend(
        slot_table_rows, rows, cosine, sine, gain, new_rows[0], queries[0], most_slots
    )
    unit_start, home_rank, group_start, group_rank, start_column = (
        request_rows[i] for i in range(5)
    )
    own = owners == group
    unit_len = lengths // UNIT
    members = jnp.arange(request_total, dtype=I32)

    head_share = w_uv.shape[0]
    chips = columns // 2

    def to_heads(part):
        came = lax.all_to_all(part, "expert", split_axis=0, concat_axis=0, tiled=True)
        return came.reshape(columns, head_share, part.shape[1], LAT)

    def spill():
        used = jnp.arange(SLOTS, most_slots, dtype=I32) < slot_table_rows[0, 4]
        rest = jnp.where(used[:, None, None], attended_rest, jnp.zeros((), BF))
        came = to_heads(rest.transpose(1, 0, 2))
        count = came.shape[2]
        member_column = group_rank // share
        member_row = (
            (member_column % 2 ^ core) * (chips * share)
            + member_column // 2 * share
            + group_rank % share
        )
        member_cell = jnp.where(home_rank >= SLOTS, start_column * count + home_rank - SLOTS, -1)
        is_row = own[None, :] & (member_row[None, :] == members[:, None])
        cell = jnp.sum(jnp.where(is_row, member_cell[None, :], 0), axis=1)
        pick = (cell[:, None] == jnp.arange(columns * count, dtype=I32)[None, :]).astype(BF)
        return jnp.stack(
            [
                jnp.dot(
                    pick, came[:, h].reshape(columns * count, LAT), preferred_element_type=F32
                ).astype(BF)
                for h in range(head_share)
            ]
        )

    more = lax.cond(
        jnp.max(home_rank) >= SLOTS,
        spill,
        lambda: jnp.zeros((head_share, request_total, LAT), BF),
    )
    by_head = to_heads(attended)
    by_head, gate_came = lax.optimization_barrier((by_head, gate_came))
    mine, other = project(cells, by_head, more, w_uv, w_out)
    mine, other, up_came, down_near, down_far, down_last = lax.optimization_barrier(
        (mine, other, up_came, down_near, down_far, down_last)
    )
    down_near = shift(down_near, 1, dp_count, "dp")
    down_far = shift(down_far, 2, dp_count, "dp")
    down_last = shift(down_last, 3, dp_count, "dp")

    other = lax.ppermute(other, "expert", [(i, i ^ 1) for i in range(columns)])
    pair_sums = pair_sum(mine, other, chips)
    chip_sums = lax.all_to_all(
        pair_sums,
        "expert",
        split_axis=0,
        concat_axis=0,
        tiled=True,
        axis_index_groups=[[2 * i + c for i in range(chips)] for c in range(2)],
    )
    attention_out = jnp.sum(chip_sums.astype(F32), axis=0)
    residual = resid[0].astype(F32) + attention_out
    normed = (
        residual
        * lax.rsqrt(jnp.mean(residual * residual, axis=1, keepdims=True) + eps)
        * moe_gain[None, :]
    ).astype(BF)

    tokens = resid.shape[1]
    capacity = 2
    expert_ids = jnp.arange(columns, dtype=I32)
    matches = route_ids[0][:, :, None] == expert_ids[None, None, :]
    combine_weights = jnp.sum(jnp.where(matches, route_weights[0][:, :, None], 0.0), axis=1)
    routed = jnp.any(matches, axis=1)
    token_order = jnp.arange(tokens, dtype=I32)
    earlier = token_order[None, :] < token_order[:, None]
    slot_rank = jnp.sum(jnp.where(earlier[:, :, None], routed.astype(I32)[None, :, :], 0), axis=1)
    slot_ids = jnp.arange(capacity, dtype=I32)
    slot_table = routed.T[:, None, :] & (slot_rank.T[:, None, :] == slot_ids[None, :, None])
    table = slot_table.reshape(columns * capacity, tokens)
    even = (jnp.arange(columns * capacity, dtype=I32) // capacity % 2 == 0)[:, None]
    table = jnp.concatenate([table & even, table & ~even], axis=1).astype(BF)
    outgoing = []
    for f in range(dp_count):
        both = jnp.concatenate(
            [
                normed[:, q * piece : (q + 1) * piece]
                for q in (quarters[f], quarters[(f - 1) % dp_count])
            ],
            axis=0,
        )
        outgoing.append(jnp.dot(table, both, preferred_element_type=F32).astype(BF))
    outgoing = jnp.stack(outgoing).reshape(devices, capacity, piece)
    arrived = lax.all_to_all(
        outgoing, ("dp", "expert"), split_axis=0, concat_axis=0, tiled=True
    ).reshape(devices * capacity, piece)

    local_rows = local_units * UNIT
    to_rows = jnp.concatenate(
        [block[:local_rows].reshape(local_units, UNIT, width) for block in rows], axis=0
    ).transpose(1, 0, 2)
    arrived, down_near, down_far, down_last, to_rows = lax.optimization_barrier(
        (arrived, down_near, down_far, down_last, to_rows)
    )
    beside = lax.ppermute(arrived, ("dp", "expert"), token_perm)
    dealt = lax.all_to_all(to_rows, "expert", split_axis=0, concat_axis=0, tiled=True)

    gate_own, up_own = width_half(w_gate, my_quarter), width_half(w_up, my_quarter)
    weights = (gate_came, up_came, gate_own, up_own)
    first = [jnp.dot(arrived, weight[0], preferred_element_type=F32) for weight in weights]
    beside, *first = lax.optimization_barrier((beside, *first))
    gate_given, up_given, gate_sum, up_sum = (
        part + jnp.dot(beside, weight[1], preferred_element_type=F32)
        for part, weight in zip(first, weights)
    )
    given = jnp.concatenate([gate_given, up_given], axis=1).astype(BF)
    given = lax.ppermute(given, ("dp", "expert"), weight_perm).astype(F32)
    half = gate_sum.shape[1]
    hidden = (
        jax.nn.silu(gate_sum + given[:, :half]) * (up_sum + given[:, half:])
    ).astype(BF)
    hidden_all = jnp.concatenate(
        [hidden] + [shift(hidden, k, dp_count, "dp") for k in range(1, dp_count)], axis=1
    )
    hidden_all, dealt = lax.optimization_barrier((hidden_all, dealt))
    downs = jnp.concatenate([lax.dynamic_slice_in_dim(w_down[0], group * piece, piece, 1), down_near, down_far, down_last], axis=0)
    out = jnp.dot(hidden_all, downs, preferred_element_type=F32)
    returned = lax.all_to_all(
        out.astype(BF).reshape(devices, capacity, piece),
        ("dp", "expert"),
        split_axis=0,
        concat_axis=0,
        tiled=True,
    )

    slots = jnp.arange(pre_rows, dtype=I32)
    offset = slots[:, None] - group_start[None, :]
    covers = own[None, :] & (offset >= 0) & (offset < unit_len[None, :])
    slot_offset = jnp.sum(jnp.where(covers, offset, 0), axis=1)
    slot_unit = jnp.sum(jnp.where(covers, offset + unit_start[None, :], 0), axis=1)
    relative = (slot_unit // block_units - group + dp_count) % dp_count
    cache_place = (
        slot_unit % block_units // local_units * most_slots
        + relative * local_units
        + slot_unit % local_units
    )
    places = jnp.arange(columns * most_slots, dtype=I32)
    pick = (cache_place[:, None] == places[None, :]).astype(BF)
    raw_cache = jnp.dot(
        pick, dealt.reshape(columns * most_slots, width), preferred_element_type=F32
    )
    turned = []
    for table_rows in (cosine, sine):
        mine = jnp.asarray(table_rows).reshape(MOST + 1, UNIT, half_rope)
        mine = lax.dynamic_index_in_dim(mine, column, 1, keepdims=False)
        picked = mine[:1]
        for o in range(1, MOST):
            picked = jnp.where(slot_offset[:, None] == o, mine[o : o + 1], picked)
        turned.append(picked)
    cache_local = norm_rotate(raw_cache, *turned, gain)

    slot_weights = jnp.where(slot_table, combine_weights.T[:, None, :], 0.0)
    moe_sum = jnp.einsum(
        "xct,fxcd->tfd",
        slot_weights,
        returned.reshape(dp_count, columns, capacity, piece).astype(F32),
        precision=lax.Precision.HIGHEST,
    ).reshape(tokens, model_width)
    decoded = (residual + moe_sum).astype(BF)
    return (cache_local[None, None], decoded[None])


def solution(mesh):
    return jax.shard_map(
        shards,
        mesh=mesh,
        in_specs=(
            P(("dp", "expert"), None),
            P("dp", None, None),
            P(),
            P(),
            P(),
            P("dp", None, None, None),
            P("expert", None, None),
            P("expert", None),
            P("dp", "expert", None),
            P(),
            P("dp", "expert", None),
            P("dp", "expert", None),
            P("expert", None, "dp"),
            P("expert", None, "dp"),
            P("expert", "dp", None),
        ),
        out_specs=(P("dp", "expert", None, None), P("dp", "expert", None)),
        check_vma=False,
    )
```

```python
import jax
import jax.numpy as jnp
import numpy as np
from jax import lax
from jax.experimental import pallas as pl
from jax.experimental.pallas import tpu as pltpu
from jax.sharding import PartitionSpec as P

LAT = 512
UNIT = 32
MOST = 3
SLOTS = 8
VMEM = 58 * 1024 * 1024

eps = 1e-06
theta = 10000.0
score_scale = 192.0 ** (-0.5)
BF = jnp.bfloat16
F32 = jnp.float32
I32 = jnp.int32


def turn_table(half_width):
    exponent = -np.arange(half_width, dtype=np.float32) / np.float32(half_width)
    frequency = np.power(np.float32(theta), exponent).astype(np.float32)
    count = (MOST + 1) * UNIT
    angles = np.arange(count, dtype=np.float32)[:, None] * frequency[None, :]
    return np.cos(angles).astype(np.float32), np.sin(angles).astype(np.float32)


def norm_rotate(raw_rows, cosine, sine, kv_gain):
    raw_rows = raw_rows.astype(F32)
    latent = raw_rows[:, :LAT]
    half_width = cosine.shape[1]
    inverse = lax.rsqrt(jnp.mean(latent * latent, axis=1, keepdims=True) + eps)
    latent = latent * inverse * kv_gain
    lower = raw_rows[:, LAT : LAT + half_width]
    upper = raw_rows[:, LAT + half_width :]
    return jnp.concatenate(
        [latent, lower * cosine - upper * sine, upper * cosine + lower * sine], axis=1
    ).astype(BF)


def shift(x, step, size, axis):
    return lax.ppermute(x, axis, [((i + step) % size, i) for i in range(size)])


def table_kernel(where_ref, lengths_ref, owners_ref, slots_ref, rows_ref, cells_ref, *, sizes):
    dp_count, columns, local_units, near_units, share = sizes
    group, column = where_ref[0], where_ref[1]
    group_f, column_f = group.astype(F32), column.astype(F32)
    count = lengths_ref.shape[1]
    units = lengths_ref[...].astype(F32) * (1.0 / UNIT)
    owner = owners_ref[...].astype(F32)
    square = (count, count)
    down = lax.broadcasted_iota(I32, square, 0)
    along = lax.broadcasted_iota(I32, square, 1)
    before = down < along

    def upright(row):
        return jnp.sum(jnp.where(down == along, row, 0.0), axis=1, keepdims=True)

    def whole(x, size):
        return jnp.floor((x + 0.5) * (1.0 / size))

    units_up, owner_up = upright(units), upright(owner)
    start = jnp.sum(jnp.where(before, units_up, 0.0), axis=0, keepdims=True)
    start_source = whole(start, local_units)
    start_block = whole(start_source, columns)
    start_column = start_source - start_block * columns
    home = owner * columns + start_column
    home_up = upright(home)
    rank = jnp.sum(jnp.where(before & (home_up == home), 1.0, 0.0), axis=0, keepdims=True)
    own = owner == group_f
    own_before = before & (owner_up == group_f)
    group_start = jnp.sum(jnp.where(own_before, units_up, 0.0), axis=0, keepdims=True)
    group_rank = jnp.sum(jnp.where(own_before, 1.0, 0.0), axis=0, keepdims=True)

    lines = slots_ref.shape[0]
    line = lax.broadcasted_iota(I32, (lines, count), 0).astype(F32)
    here = home == group_f * columns + column_f
    is_slot = here & (rank == line)
    block = start_block - group_f
    block = jnp.where(block < 0.0, block + dp_count, block)
    place = block * near_units + (start - start_source * local_units)

    def pick(row):
        return jnp.sum(jnp.where(is_slot, row, 0.0), axis=1, keepdims=True)

    near = lax.broadcasted_iota(I32, (lines, 1), 0).astype(F32)
    near_block = whole(near, near_units)
    near_unit = near - near_block * near_units + column_f * local_units
    near_block = near_block + group_f
    near_block = jnp.where(near_block >= dp_count, near_block - dp_count, near_block)
    near_unit = near_unit + near_block * (columns * local_units)
    near_start = jnp.max(jnp.where(start <= near_unit, start, 0.0), axis=1, keepdims=True)
    near_offset = jnp.minimum(near_unit - near_start, MOST - 1.0)
    number = jnp.sum(jnp.where(here, 1.0, 0.0), axis=1, keepdims=True)
    lane = lax.broadcasted_iota(I32, slots_ref.shape, 1)
    packed = jnp.zeros(slots_ref.shape, F32)
    wraps = jnp.where(jnp.full((1, 1), column, I32) == columns - 1, 1.0, 0.0)
    values = (pick(place), pick(units), pick(group_rank), near_offset, number, wraps)
    for i, value in enumerate(values):
        packed = jnp.where(lane == i, value, packed)
    slots_ref[...] = packed.astype(I32)
    rows_ref[...] = jnp.concatenate(
        [start, rank, group_start, group_rank, start_column] + [start] * 3, axis=0
    ).astype(I32)

    member_column = whole(group_rank, share)
    member_chip = whole(member_column, 2)
    other_core = jnp.abs(member_column - 2.0 * member_chip - (column % 2).astype(F32))
    row = (other_core * (columns // 2) + member_chip) * share + (
        group_rank - member_column * share
    )
    lines = cells_ref.shape[0]
    line = lax.broadcasted_iota(I32, (lines, count), 0).astype(F32)
    cell = jnp.where(rank < SLOTS, start_column * SLOTS + rank, -1.0)
    found = jnp.sum(jnp.where(own & (row == line), cell, 0.0), axis=1, keepdims=True)
    cells_ref[...] = jnp.broadcast_to(found, cells_ref.shape).astype(I32)


def tables(where, lengths, owners, sizes):
    lines = sizes[0] * sizes[3]
    whole = pl.BlockSpec(memory_space=pltpu.VMEM)

    def body(*refs):
        table_kernel(*refs, sizes=sizes)

    return pl.pallas_call(
        body,
        out_shape=(
            jax.ShapeDtypeStruct((lines, 128), I32),
            jax.ShapeDtypeStruct((8, lengths.shape[0]), I32),
            jax.ShapeDtypeStruct((sizes[1] * sizes[4], 128), I32),
        ),
        in_specs=[pl.BlockSpec(memory_space=pltpu.SMEM), whole, whole],
        out_specs=(whole, whole, whole),
        compiler_params=pltpu.CompilerParams(vmem_limit_bytes=32 * 1024 * 1024),
        cost_estimate=pl.CostEstimate(flops=1000, bytes_accessed=4096, transcendentals=0),
        name="tables",
    )(where, lengths[None, :], owners[None, :])


def slice_kernel(at_ref, gate_ref, up_ref, down_ref, gate_out, up_out, *refs):
    downs, sems = refs[:-1], refs[-1]
    piece = gate_out.shape[1]
    copies = []
    for weight, out in ((gate_ref, gate_out), (up_ref, up_out)):
        for i in range(2):
            rows = pl.ds(pl.multiple_of(at_ref[i] * piece, 128), piece)
            copies.append((weight.at[0, rows, :], out.at[i]))
    for i, out in enumerate(downs):
        columns = pl.ds(pl.multiple_of(at_ref[2 + i] * piece, 128), piece)
        copies.append((down_ref.at[0, :, columns], out))
    copies = [
        pltpu.make_async_copy(source, target, sems.at[i])
        for i, (source, target) in enumerate(copies)
    ]
    for copy in copies:
        copy.start()
    for copy in copies:
        copy.wait()


def weight_slices(at, w_gate, w_up, w_down, dp_count):
    piece = w_gate.shape[1] // dp_count
    away = pl.BlockSpec(memory_space=pltpu.HBM)
    whole = pl.BlockSpec(memory_space=pltpu.VMEM)
    halves = jax.ShapeDtypeStruct((2, piece, w_gate.shape[2]), BF)
    part = jax.ShapeDtypeStruct((w_down.shape[1], piece), BF)
    return pl.pallas_call(
        slice_kernel,
        out_shape=(halves, halves) + (part,) * (dp_count - 1),
        in_specs=[pl.BlockSpec(memory_space=pltpu.SMEM)] + [away] * 3,
        out_specs=(whole,) * (dp_count + 1),
        scratch_shapes=[pltpu.SemaphoreType.DMA((dp_count + 3,))],
        compiler_params=pltpu.CompilerParams(vmem_limit_bytes=VMEM),
        cost_estimate=pl.CostEstimate(flops=1000, bytes_accessed=4096, transcendentals=0),
        name="weight_slices",
    )(at, w_gate, w_up, w_down)


def attend_kernel(slots_ref, *refs, blocks):
    rows_in = refs[:blocks]
    cos_ref, sin_ref, gain_ref, new_ref, query_ref = refs[blocks : blocks + 5]
    out_ref, rest_ref, keys, query, fresh, held_out, sems = refs[blocks + 5 :]
    number = slots_ref[0, 4]

    def fetch(slot):
        return pltpu.make_async_copy(
            query_ref.at[slots_ref[slot, 2]], query.at[slot], sems.at[slot]
        )

    @pl.loop(0, number)
    def _(slot):
        fetch(slot).start()

    gain = gain_ref[...]
    local_rows = rows_in[0].shape[0] - (MOST - 1) * UNIT
    near_units = rows_in[0].shape[0] // UNIT
    for block, ref in enumerate(rows_in):
        before = near_units * ((block + blocks - 1) % blocks - block)
        for first in range(0, ref.shape[0], UNIT):
            unit = block * near_units + first // UNIT
            if first >= local_rows:
                unit = unit + slots_ref[0, 5] * before
            span = pl.ds(pl.multiple_of(slots_ref[unit, 3] * UNIT, UNIT), UNIT)
            keys[pl.ds(pl.multiple_of(unit * UNIT, UNIT), UNIT), :] = norm_rotate(
                ref[first : first + UNIT, :], cos_ref[span, :], sin_ref[span, :], gain
            )
    fresh[...] = new_ref[...].astype(F32)

    heads = out_ref.shape[0]
    sent = out_ref.shape[1]
    window = MOST * UNIT
    lanes = window + UNIT
    lane = lax.broadcasted_iota(I32, (heads, lanes), 1)

    def one(slot):
        count = slots_ref[slot, 1]
        own = keys[pl.ds(pl.multiple_of(slots_ref[slot, 0] * UNIT, UNIT), window), :]
        at = pl.ds(count * UNIT, 1)
        new = norm_rotate(
            fresh[pl.ds(slots_ref[slot, 2], 1), :], cos_ref[at, :], sin_ref[at, :], gain
        )
        new = jnp.broadcast_to(new.astype(F32), (UNIT, own.shape[1])).astype(BF)
        held = jnp.concatenate([own, new], axis=0)
        scores = (
            lax.dot_general(
                query[slot], held, (((1,), (1,)), ((), ())), preferred_element_type=F32
            )
            * score_scale
        )
        live = (lane < count * UNIT) | (lane == window)
        scores = jnp.where(live, scores, -jnp.inf)
        weights = jnp.exp(scores - jnp.max(scores, axis=1, keepdims=True))
        total = jnp.sum(weights, axis=1, keepdims=True)
        mixture = jnp.dot(weights.astype(BF), held[:, :LAT], preferred_element_type=F32)
        return mixture / total

    @pl.loop(0, number)
    def _(slot):
        fetch(slot).wait()

    for slot in range(sent):
        held_out[slot] = jnp.where(slot < number, one(slot), 0.0)

    out_ref[...] = jnp.swapaxes(held_out[...], 0, 1).astype(BF)

    @pl.loop(sent, number)
    def _(slot):
        rest_ref[slot - sent] = one(slot).astype(BF)


def attend(slots, rows, cosine, sine, gain, new_rows, queries, most_slots):
    heads = queries.shape[1]
    blocks = len(rows)
    total_rows = sum(block.shape[0] for block in rows)
    whole = pl.BlockSpec(memory_space=pltpu.VMEM)

    def body(*refs):
        attend_kernel(*refs, blocks=blocks)

    return pl.pallas_call(
        body,
        out_shape=(
            jax.ShapeDtypeStruct((heads, SLOTS, LAT), BF),
            jax.ShapeDtypeStruct((most_slots - SLOTS, heads, LAT), BF),
        ),
        in_specs=[pl.BlockSpec(memory_space=pltpu.SMEM)]
        + [whole] * (blocks + 4)
        + [pl.BlockSpec(memory_space=pltpu.HBM)],
        out_specs=(whole, whole),
        scratch_shapes=[
            pltpu.VMEM((total_rows, queries.shape[2]), BF),
            pltpu.VMEM((most_slots,) + queries.shape[1:], BF),
            pltpu.VMEM(new_rows.shape, F32),
            pltpu.VMEM((SLOTS, heads, LAT), F32),
            pltpu.SemaphoreType.DMA((most_slots,)),
        ],
        compiler_params=pltpu.CompilerParams(vmem_limit_bytes=VMEM),
        cost_estimate=pl.CostEstimate(
            flops=10**8, bytes_accessed=4 * 10**6, transcendentals=10**5
        ),
        name="attend",
    )(slots, *rows, cosine, sine, gain, new_rows, queries)


def project_kernel(
    cells_ref, came_ref, more_ref, uv_ref, weight_ref, mine_ref, other_ref, weight, sems
):
    step = weight.shape[1] // 4
    spans = [slice(i * step, (i + 1) * step) for i in range(4)]
    copies = [
        pltpu.make_async_copy(weight_ref.at[:, span], weight.at[:, span], sems.at[i])
        for i, span in enumerate(spans)
    ]
    for copy in copies:
        copy.start()
    requests = cells_ref.shape[0]
    sources, heads, slots, _ = came_ref.shape
    cells = sources * slots
    pick = cells_ref[:, :1] == lax.broadcasted_iota(I32, (requests, cells), 1)
    pick = jnp.where(pick, 1.0, 0.0).astype(BF)
    projected = []
    for h in range(heads):
        came = came_ref[:, h].astype(F32).reshape(cells, LAT).astype(BF)
        rows = jnp.dot(pick, came, preferred_element_type=F32) + more_ref[h].astype(F32)
        projected.append(
            jnp.dot(rows.astype(BF), uv_ref[h], preferred_element_type=F32).astype(BF)
        )
    projected = jnp.concatenate(projected, axis=1)
    keep = mine_ref.shape[0]
    for span, copy in zip(spans, copies):
        copy.wait()
        sums = jnp.dot(projected, weight[:, span], preferred_element_type=F32).astype(BF)
        mine_ref[:, span] = sums[:keep]
        other_ref[:, span] = sums[keep:]


def project(cells, came, more, w_uv, w_out):
    whole = pl.BlockSpec(memory_space=pltpu.VMEM)
    half = jax.ShapeDtypeStruct((cells.shape[0] // 2, w_out.shape[1]), BF)
    return pl.pallas_call(
        project_kernel,
        out_shape=(half, half),
        in_specs=[whole] * 4 + [pl.BlockSpec(memory_space=pltpu.HBM)],
        out_specs=(whole, whole),
        scratch_shapes=[pltpu.VMEM(w_out.shape, BF), pltpu.SemaphoreType.DMA((4,))],
        compiler_params=pltpu.CompilerParams(vmem_limit_bytes=32 * 1024 * 1024),
        cost_estimate=pl.CostEstimate(
            flops=4 * 10**8, bytes_accessed=6 * 10**6, transcendentals=0
        ),
        name="project",
    )(cells, came, more, w_uv, w_out)


def pair_kernel(mine_ref, other_ref, out_ref):
    chips, share, width = out_ref.shape
    step = width // 4
    for first in range(0, width, step):
        span = slice(first, first + step)
        sums = mine_ref[:, span].astype(F32) + other_ref[:, span].astype(F32)
        for chip in range(chips):
            out_ref[chip, :, span] = sums[chip * share : (chip + 1) * share].astype(BF)


def pair_sum(mine, other, chips):
    whole = pl.BlockSpec(memory_space=pltpu.VMEM)
    return pl.pallas_call(
        pair_kernel,
        out_shape=jax.ShapeDtypeStruct((chips, mine.shape[0] // chips, mine.shape[1]), BF),
        in_specs=[whole] * 2,
        out_specs=whole,
        compiler_params=pltpu.CompilerParams(vmem_limit_bytes=32 * 1024 * 1024),
        cost_estimate=pl.CostEstimate(
            flops=4 * 10**5, bytes_accessed=2 * 10**6, transcendentals=0
        ),
        name="pair_sum",
    )(mine, other)


def shards(
    latent_rows,
    new_rows,
    kv_gain,
    lengths,
    owners,
    queries,
    w_uv,
    w_out,
    resid,
    moe_gain,
    route_ids,
    route_weights,
    w_gate,
    w_up,
    w_down,
):
    dp_count = lax.axis_size("dp")
    columns = lax.axis_size("expert")
    devices = dp_count * columns
    group = lax.axis_index("dp")
    column = lax.axis_index("expert")
    core = column % 2
    pre_rows, width = latent_rows.shape
    half_rope = (width - LAT) // 2
    local_units = pre_rows // UNIT
    block_units = columns * local_units
    gain = kv_gain[None, :]

    border = (MOST - 1) * UNIT
    next_rows = lax.ppermute(
        latent_rows[:border], "expert", [((i + 1) % columns, i) for i in range(columns)]
    )
    near_rows = jnp.concatenate([latent_rows, next_rows], axis=0)
    near_rows, late_group = lax.optimization_barrier((near_rows, group))
    rows = [near_rows] + [shift(near_rows, k, dp_count, "dp") for k in range(1, dp_count)]

    request_total = queries.shape[1]
    most_slots = dp_count * local_units
    near_units = local_units + MOST - 1
    where = jnp.stack([group, column]).astype(I32)
    share = request_total // columns
    slot_table_rows, request_rows, cells = tables(
        where, lengths, owners, (dp_count, columns, local_units, near_units, share)
    )
    cosine, sine = turn_table(half_rope)

    model_width = w_out.shape[1]
    piece = model_width // dp_count
    halves = (0, 1, 1, 0)
    quarters = (0, 2, 3, 1)

    def pair_perm(partner):
        perm = []
        for f in range(dp_count):
            for x in range(columns):
                g = (f - x % 2) % dp_count
                perm.append((f * columns + x, (partner(g) + x % 2) % dp_count * columns + x))
        return perm

    weight_perm = pair_perm(lambda g: g ^ 1)
    token_perm = pair_perm(lambda g: dp_count - 1 - g)
    place = (group - core + dp_count) % dp_count

    def quarter_of(g):
        return jnp.where(g == 0, 0, jnp.where(g == 1, 2, jnp.where(g == 2, 3, 1)))

    my_quarter = quarter_of(place)
    their_quarter = quarter_of(place ^ 1)

    def width_half(weight, first):
        return [
            lax.dynamic_slice_in_dim(weight[0], q * piece, piece, 0) for q in (first, first ^ 1)
        ]

    at = jnp.stack(
        [their_quarter, their_quarter ^ 1]
        + [(late_group - k + dp_count) % dp_count for k in range(1, dp_count)]
    ).astype(I32)
    gate_sent, up_sent, down_near, down_far, down_last = weight_slices(
        at, w_gate, w_up, w_down, dp_count
    )
    gate_sent, up_sent, slot_table_rows, *rows = lax.optimization_barrier(
        (gate_sent, up_sent, slot_table_rows, *rows)
    )
    gate_came = lax.ppermute(gate_sent, ("dp", "expert"), weight_perm)
    up_came = lax.ppermute(up_sent, ("dp", "expert"), weight_perm)

    attended, attended_rest = attend(
        slot_table_rows, rows, cosine, sine, gain, new_rows[0], queries[0], most_slots
    )
    unit_start, home_rank, group_start, group_rank, start_column = (
        request_rows[i] for i in range(5)
    )
    own = owners == group
    unit_len = lengths // UNIT
    members = jnp.arange(request_total, dtype=I32)

    head_share = w_uv.shape[0]
    chips = columns // 2

    def to_heads(part):
        came = lax.all_to_all(part, "expert", split_axis=0, concat_axis=0, tiled=True)
        return came.reshape(columns, head_share, part.shape[1], LAT)

    def spill():
        used = jnp.arange(SLOTS, most_slots, dtype=I32) < slot_table_rows[0, 4]
        rest = jnp.where(used[:, None, None], attended_rest, jnp.zeros((), BF))
        came = to_heads(rest.transpose(1, 0, 2))
        count = came.shape[2]
        member_column = group_rank // share
        member_row = (
            (member_column % 2 ^ core) * (chips * share)
            + member_column // 2 * share
            + group_rank % share
        )
        member_cell = jnp.where(home_rank >= SLOTS, start_column * count + home_rank - SLOTS, -1)
        is_row = own[None, :] & (member_row[None, :] == members[:, None])
        cell = jnp.sum(jnp.where(is_row, member_cell[None, :], 0), axis=1)
        pick = (cell[:, None] == jnp.arange(columns * count, dtype=I32)[None, :]).astype(BF)
        return jnp.stack(
            [
                jnp.dot(
                    pick, came[:, h].reshape(columns * count, LAT), preferred_element_type=F32
                ).astype(BF)
                for h in range(head_share)
            ]
        )

    more = lax.cond(
        jnp.max(home_rank) >= SLOTS,
        spill,
        lambda: jnp.zeros((head_share, request_total, LAT), BF),
    )
    by_head = to_heads(attended)
    by_head, gate_came = lax.optimization_barrier((by_head, gate_came))
    mine, other = project(cells, by_head, more, w_uv, w_out)
    mine, other, down_near, down_last = lax.optimization_barrier(
        (mine, other, down_near, down_last)
    )
    down_near = shift(down_near, 1, dp_count, "dp")
    down_last = shift(down_last, 3, dp_count, "dp")

    other = lax.ppermute(other, "expert", [(i, i ^ 1) for i in range(columns)])
    pair_sums = pair_sum(mine, other, chips)
    chip_sums = lax.all_to_all(
        pair_sums,
        "expert",
        split_axis=0,
        concat_axis=0,
        tiled=True,
        axis_index_groups=[[2 * i + c for i in range(chips)] for c in range(2)],
    )
    chip_sums, up_came, down_far = lax.optimization_barrier((chip_sums, up_came, down_far))
    down_far = shift(down_far, 2, dp_count, "dp")
    attention_out = jnp.sum(chip_sums.astype(F32), axis=0)
    residual = resid[0].astype(F32) + attention_out
    normed = (
        residual
        * lax.rsqrt(jnp.mean(residual * residual, axis=1, keepdims=True) + eps)
        * moe_gain[None, :]
    ).astype(BF)

    tokens = resid.shape[1]
    capacity = 2
    expert_ids = jnp.arange(columns, dtype=I32)
    matches = route_ids[0][:, :, None] == expert_ids[None, None, :]
    combine_weights = jnp.sum(jnp.where(matches, route_weights[0][:, :, None], 0.0), axis=1)
    routed = jnp.any(matches, axis=1)
    token_order = jnp.arange(tokens, dtype=I32)
    earlier = token_order[None, :] < token_order[:, None]
    slot_rank = jnp.sum(jnp.where(earlier[:, :, None], routed.astype(I32)[None, :, :], 0), axis=1)
    slot_ids = jnp.arange(capacity, dtype=I32)
    slot_table = routed.T[:, None, :] & (slot_rank.T[:, None, :] == slot_ids[None, :, None])
    table = slot_table.reshape(columns * capacity, tokens)
    even = (jnp.arange(columns * capacity, dtype=I32) // capacity % 2 == 0)[:, None]
    table = jnp.concatenate([table & even, table & ~even], axis=1).astype(BF)
    outgoing = []
    for f in range(dp_count):
        both = jnp.concatenate(
            [
                normed[:, q * piece : (q + 1) * piece]
                for q in (quarters[f], quarters[(f - 1) % dp_count])
            ],
            axis=0,
        )
        outgoing.append(jnp.dot(table, both, preferred_element_type=F32).astype(BF))
    outgoing = jnp.stack(outgoing).reshape(devices, capacity, piece)
    arrived = lax.all_to_all(
        outgoing, ("dp", "expert"), split_axis=0, concat_axis=0, tiled=True
    ).reshape(devices * capacity, piece)

    local_rows = local_units * UNIT
    to_rows = jnp.concatenate(
        [block[:local_rows].reshape(local_units, UNIT, width) for block in rows], axis=0
    ).transpose(1, 0, 2)
    arrived, down_near, down_far, down_last, to_rows = lax.optimization_barrier(
        (arrived, down_near, down_far, down_last, to_rows)
    )
    beside = lax.ppermute(arrived, ("dp", "expert"), token_perm)
    dealt = lax.all_to_all(to_rows, "expert", split_axis=0, concat_axis=0, tiled=True)

    gate_own, up_own = width_half(w_gate, my_quarter), width_half(w_up, my_quarter)
    weights = (gate_came, up_came, gate_own, up_own)
    first = [jnp.dot(arrived, weight[0], preferred_element_type=F32) for weight in weights]
    beside, *first = lax.optimization_barrier((beside, *first))
    gate_given, up_given, gate_sum, up_sum = (
        part + jnp.dot(beside, weight[1], preferred_element_type=F32)
        for part, weight in zip(first, weights)
    )
    given = jnp.concatenate([gate_given, up_given], axis=1).astype(BF)
    given = lax.ppermute(given, ("dp", "expert"), weight_perm).astype(F32)
    half = gate_sum.shape[1]
    hidden = (
        jax.nn.silu(gate_sum + given[:, :half]) * (up_sum + given[:, half:])
    ).astype(BF)
    hidden_all = jnp.concatenate(
        [hidden] + [shift(hidden, k, dp_count, "dp") for k in range(1, dp_count)], axis=1
    )
    hidden_all, dealt = lax.optimization_barrier((hidden_all, dealt))
    downs = jnp.concatenate([lax.dynamic_slice_in_dim(w_down[0], group * piece, piece, 1), down_near, down_far, down_last], axis=0)
    out = jnp.dot(hidden_all, downs, preferred_element_type=F32)
    returned = lax.all_to_all(
        out.astype(BF).reshape(devices, capacity, piece),
        ("dp", "expert"),
        split_axis=0,
        concat_axis=0,
        tiled=True,
    )

    slots = jnp.arange(pre_rows, dtype=I32)
    offset = slots[:, None] - group_start[None, :]
    covers = own[None, :] & (offset >= 0) & (offset < unit_len[None, :])
    slot_offset = jnp.sum(jnp.where(covers, offset, 0), axis=1)
    slot_unit = jnp.sum(jnp.where(covers, offset + unit_start[None, :], 0), axis=1)
    relative = (slot_unit // block_units - group + dp_count) % dp_count
    cache_place = (
        slot_unit % block_units // local_units * most_slots
        + relative * local_units
        + slot_unit % local_units
    )
    places = jnp.arange(columns * most_slots, dtype=I32)
    pick = (cache_place[:, None] == places[None, :]).astype(BF)
    raw_cache = jnp.dot(
        pick, dealt.reshape(columns * most_slots, width), preferred_element_type=F32
    )
    turned = []
    for table_rows in (cosine, sine):
        mine = jnp.asarray(table_rows).reshape(MOST + 1, UNIT, half_rope)
        mine = lax.dynamic_index_in_dim(mine, column, 1, keepdims=False)
        picked = mine[:1]
        for o in range(1, MOST):
            picked = jnp.where(slot_offset[:, None] == o, mine[o : o + 1], picked)
        turned.append(picked)
    cache_local = norm_rotate(raw_cache, *turned, gain)

    slot_weights = jnp.where(slot_table, combine_weights.T[:, None, :], 0.0)
    moe_sum = jnp.einsum(
        "xct,fxcd->tfd",
        slot_weights,
        returned.reshape(dp_count, columns, capacity, piece).astype(F32),
        precision=lax.Precision.HIGHEST,
    ).reshape(tokens, model_width)
    decoded = (residual + moe_sum).astype(BF)
    return (cache_local[None, None], decoded[None])


def solution(mesh):
    return jax.shard_map(
        shards,
        mesh=mesh,
        in_specs=(
            P(("dp", "expert"), None),
            P("dp", None, None),
            P(),
            P(),
            P(),
            P("dp", None, None, None),
            P("expert", None, None),
            P("expert", None),
            P("dp", "expert", None),
            P(),
            P("dp", "expert", None),
            P("dp", "expert", None),
            P("expert", None, "dp"),
            P("expert", None, "dp"),
            P("expert", "dp", None),
        ),
        out_specs=(P("dp", "expert", None, None), P("dp", "expert", None)),
        check_vma=False,
    )
```

```python
import jax
import jax.numpy as jnp
import numpy as np
from jax import lax
from jax.experimental import pallas as pl
from jax.experimental.pallas import tpu as pltpu
from jax.sharding import PartitionSpec as P

LAT = 512
UNIT = 32
MOST = 3
SLOTS = 8
VMEM = 58 * 1024 * 1024

eps = 1e-06
theta = 10000.0
score_scale = 192.0 ** (-0.5)
BF = jnp.bfloat16
F32 = jnp.float32
I32 = jnp.int32


def turn_table(half_width):
    exponent = -np.arange(half_width, dtype=np.float32) / np.float32(half_width)
    frequency = np.power(np.float32(theta), exponent).astype(np.float32)
    count = (MOST + 1) * UNIT
    angles = np.arange(count, dtype=np.float32)[:, None] * frequency[None, :]
    return np.cos(angles).astype(np.float32), np.sin(angles).astype(np.float32)


def norm_rotate(raw_rows, cosine, sine, kv_gain):
    raw_rows = raw_rows.astype(F32)
    latent = raw_rows[:, :LAT]
    half_width = cosine.shape[1]
    inverse = lax.rsqrt(jnp.mean(latent * latent, axis=1, keepdims=True) + eps)
    latent = latent * inverse * kv_gain
    lower = raw_rows[:, LAT : LAT + half_width]
    upper = raw_rows[:, LAT + half_width :]
    return jnp.concatenate(
        [latent, lower * cosine - upper * sine, upper * cosine + lower * sine], axis=1
    ).astype(BF)


def shift(x, step, size, axis):
    return lax.ppermute(x, axis, [((i + step) % size, i) for i in range(size)])


def table_kernel(where_ref, lengths_ref, owners_ref, slots_ref, rows_ref, cells_ref, *, sizes):
    dp_count, columns, local_units, near_units, share = sizes
    group, column = where_ref[0], where_ref[1]
    group_f, column_f = group.astype(F32), column.astype(F32)
    count = lengths_ref.shape[1]
    units = lengths_ref[...].astype(F32) * (1.0 / UNIT)
    owner = owners_ref[...].astype(F32)
    square = (count, count)
    down = lax.broadcasted_iota(I32, square, 0)
    along = lax.broadcasted_iota(I32, square, 1)
    before = down < along

    def upright(row):
        return jnp.sum(jnp.where(down == along, row, 0.0), axis=1, keepdims=True)

    def whole(x, size):
        return jnp.floor((x + 0.5) * (1.0 / size))

    units_up, owner_up = upright(units), upright(owner)
    start = jnp.sum(jnp.where(before, units_up, 0.0), axis=0, keepdims=True)
    start_source = whole(start, local_units)
    start_block = whole(start_source, columns)
    start_column = start_source - start_block * columns
    home = owner * columns + start_column
    home_up = upright(home)
    rank = jnp.sum(jnp.where(before & (home_up == home), 1.0, 0.0), axis=0, keepdims=True)
    own = owner == group_f
    own_before = before & (owner_up == group_f)
    group_start = jnp.sum(jnp.where(own_before, units_up, 0.0), axis=0, keepdims=True)
    group_rank = jnp.sum(jnp.where(own_before, 1.0, 0.0), axis=0, keepdims=True)

    lines = slots_ref.shape[0]
    line = lax.broadcasted_iota(I32, (lines, count), 0).astype(F32)
    here = home == group_f * columns + column_f
    is_slot = here & (rank == line)
    block = start_block - group_f
    block = jnp.where(block < 0.0, block + dp_count, block)
    place = block * near_units + (start - start_source * local_units)

    def pick(row):
        return jnp.sum(jnp.where(is_slot, row, 0.0), axis=1, keepdims=True)

    near = lax.broadcasted_iota(I32, (lines, 1), 0).astype(F32)
    near_block = whole(near, near_units)
    near_unit = near - near_block * near_units + column_f * local_units
    near_block = near_block + group_f
    near_block = jnp.where(near_block >= dp_count, near_block - dp_count, near_block)
    near_unit = near_unit + near_block * (columns * local_units)
    near_start = jnp.max(jnp.where(start <= near_unit, start, 0.0), axis=1, keepdims=True)
    near_offset = jnp.minimum(near_unit - near_start, MOST - 1.0)
    number = jnp.sum(jnp.where(here, 1.0, 0.0), axis=1, keepdims=True)
    lane = lax.broadcasted_iota(I32, slots_ref.shape, 1)
    packed = jnp.zeros(slots_ref.shape, F32)
    wraps = jnp.where(jnp.full((1, 1), column, I32) == columns - 1, 1.0, 0.0)
    values = (pick(place), pick(units), pick(group_rank), near_offset, number, wraps)
    for i, value in enumerate(values):
        packed = jnp.where(lane == i, value, packed)
    slots_ref[...] = packed.astype(I32)
    rows_ref[...] = jnp.concatenate(
        [start, rank, group_start, group_rank, start_column] + [start] * 3, axis=0
    ).astype(I32)

    member_column = whole(group_rank, share)
    member_chip = whole(member_column, 2)
    other_core = jnp.abs(member_column - 2.0 * member_chip - (column % 2).astype(F32))
    row = (other_core * (columns // 2) + member_chip) * share + (
        group_rank - member_column * share
    )
    lines = cells_ref.shape[0]
    line = lax.broadcasted_iota(I32, (lines, count), 0).astype(F32)
    cell = jnp.where(rank < SLOTS, start_column * SLOTS + rank, -1.0)
    found = jnp.sum(jnp.where(own & (row == line), cell, 0.0), axis=1, keepdims=True)
    cells_ref[...] = jnp.broadcast_to(found, cells_ref.shape).astype(I32)


def tables(where, lengths, owners, sizes):
    lines = sizes[0] * sizes[3]
    whole = pl.BlockSpec(memory_space=pltpu.VMEM)

    def body(*refs):
        table_kernel(*refs, sizes=sizes)

    return pl.pallas_call(
        body,
        out_shape=(
            jax.ShapeDtypeStruct((lines, 128), I32),
            jax.ShapeDtypeStruct((8, lengths.shape[0]), I32),
            jax.ShapeDtypeStruct((sizes[1] * sizes[4], 128), I32),
        ),
        in_specs=[pl.BlockSpec(memory_space=pltpu.SMEM), whole, whole],
        out_specs=(whole, whole, whole),
        compiler_params=pltpu.CompilerParams(vmem_limit_bytes=32 * 1024 * 1024),
        cost_estimate=pl.CostEstimate(flops=1000, bytes_accessed=4096, transcendentals=0),
        name="tables",
    )(where, lengths[None, :], owners[None, :])


def slice_kernel(at_ref, gate_ref, up_ref, down_ref, gate_out, up_out, *refs):
    downs, sems = refs[:-1], refs[-1]
    piece = gate_out.shape[1]
    copies = []
    for weight, out in ((gate_ref, gate_out), (up_ref, up_out)):
        for i in range(2):
            rows = pl.ds(pl.multiple_of(at_ref[i] * piece, 128), piece)
            copies.append((weight.at[0, rows, :], out.at[i]))
    for i, out in enumerate(downs):
        columns = pl.ds(pl.multiple_of(at_ref[2 + i] * piece, 128), piece)
        copies.append((down_ref.at[0, :, columns], out))
    copies = [
        pltpu.make_async_copy(source, target, sems.at[i])
        for i, (source, target) in enumerate(copies)
    ]
    for copy in copies:
        copy.start()
    for copy in copies:
        copy.wait()


def weight_slices(at, w_gate, w_up, w_down, dp_count):
    piece = w_gate.shape[1] // dp_count
    away = pl.BlockSpec(memory_space=pltpu.HBM)
    whole = pl.BlockSpec(memory_space=pltpu.VMEM)
    halves = jax.ShapeDtypeStruct((2, piece, w_gate.shape[2]), BF)
    part = jax.ShapeDtypeStruct((w_down.shape[1], piece), BF)
    return pl.pallas_call(
        slice_kernel,
        out_shape=(halves, halves) + (part,) * (dp_count - 1),
        in_specs=[pl.BlockSpec(memory_space=pltpu.SMEM)] + [away] * 3,
        out_specs=(whole,) * (dp_count + 1),
        scratch_shapes=[pltpu.SemaphoreType.DMA((dp_count + 3,))],
        compiler_params=pltpu.CompilerParams(vmem_limit_bytes=VMEM),
        cost_estimate=pl.CostEstimate(flops=1000, bytes_accessed=4096, transcendentals=0),
        name="weight_slices",
    )(at, w_gate, w_up, w_down)


def attend_kernel(slots_ref, *refs, blocks):
    rows_in = refs[:blocks]
    cos_ref, sin_ref, gain_ref, new_ref, query_ref = refs[blocks : blocks + 5]
    out_ref, rest_ref, keys, query, fresh, held_out, spare, sems, spare_sem = refs[blocks + 5 :]
    number = slots_ref[0, 4]

    def fetch(slot):
        return pltpu.make_async_copy(
            query_ref.at[slots_ref[slot, 2]], query.at[slot], sems.at[slot]
        )

    @pl.loop(0, number)
    def _(slot):
        fetch(slot).start()

    gain = gain_ref[...]
    local_rows = rows_in[0].shape[0] - (MOST - 1) * UNIT
    near_units = rows_in[0].shape[0] // UNIT
    for block, ref in enumerate(rows_in):
        before = near_units * ((block + blocks - 1) % blocks - block)
        for first in range(0, ref.shape[0], UNIT):
            unit = block * near_units + first // UNIT
            if first >= local_rows:
                unit = unit + slots_ref[0, 5] * before
            span = pl.ds(pl.multiple_of(slots_ref[unit, 3] * UNIT, UNIT), UNIT)
            keys[pl.ds(pl.multiple_of(unit * UNIT, UNIT), UNIT), :] = norm_rotate(
                ref[first : first + UNIT, :], cos_ref[span, :], sin_ref[span, :], gain
            )
    fresh[...] = new_ref[...].astype(F32)

    heads = out_ref.shape[0]
    sent = out_ref.shape[1]
    window = MOST * UNIT
    lanes = window + UNIT
    lane = lax.broadcasted_iota(I32, (heads, lanes), 1)

    def one(slot):
        count = slots_ref[slot, 1]
        own = keys[pl.ds(pl.multiple_of(slots_ref[slot, 0] * UNIT, UNIT), window), :]
        at = pl.ds(count * UNIT, 1)
        new = norm_rotate(
            fresh[pl.ds(slots_ref[slot, 2], 1), :], cos_ref[at, :], sin_ref[at, :], gain
        )
        new = jnp.broadcast_to(new.astype(F32), (UNIT, own.shape[1])).astype(BF)
        held = jnp.concatenate([own, new], axis=0)
        scores = (
            lax.dot_general(
                query[slot], held, (((1,), (1,)), ((), ())), preferred_element_type=F32
            )
            * score_scale
        )
        live = (lane < count * UNIT) | (lane == window)
        scores = jnp.where(live, scores, -jnp.inf)
        weights = jnp.exp(scores - jnp.max(scores, axis=1, keepdims=True))
        total = jnp.sum(weights, axis=1, keepdims=True)
        mixture = jnp.dot(weights.astype(BF), held[:, :LAT], preferred_element_type=F32)
        return mixture / total

    @pl.loop(0, number)
    def _(slot):
        fetch(slot).wait()

    for slot in range(sent):
        held_out[slot] = jnp.where(slot < number, one(slot), 0.0)

    out_ref[...] = jnp.swapaxes(held_out[...], 0, 1).astype(BF)

    @pl.loop(sent, number)
    def _(slot):
        spare[...] = one(slot).astype(BF)
        copy = pltpu.make_async_copy(spare, rest_ref.at[slot - sent], spare_sem)
        copy.start()
        copy.wait()


def attend(slots, rows, cosine, sine, gain, new_rows, queries, most_slots):
    heads = queries.shape[1]
    blocks = len(rows)
    total_rows = sum(block.shape[0] for block in rows)
    whole = pl.BlockSpec(memory_space=pltpu.VMEM)

    def body(*refs):
        attend_kernel(*refs, blocks=blocks)

    return pl.pallas_call(
        body,
        out_shape=(
            jax.ShapeDtypeStruct((heads, SLOTS, LAT), BF),
            jax.ShapeDtypeStruct((most_slots - SLOTS, heads, LAT), BF),
        ),
        in_specs=[pl.BlockSpec(memory_space=pltpu.SMEM)]
        + [whole] * (blocks + 4)
        + [pl.BlockSpec(memory_space=pltpu.HBM)],
        out_specs=(whole, pl.BlockSpec(memory_space=pltpu.HBM)),
        scratch_shapes=[
            pltpu.VMEM((total_rows, queries.shape[2]), BF),
            pltpu.VMEM((most_slots,) + queries.shape[1:], BF),
            pltpu.VMEM(new_rows.shape, F32),
            pltpu.VMEM((SLOTS, heads, LAT), F32),
            pltpu.VMEM((heads, LAT), BF),
            pltpu.SemaphoreType.DMA((most_slots,)),
            pltpu.SemaphoreType.DMA,
        ],
        compiler_params=pltpu.CompilerParams(vmem_limit_bytes=VMEM),
        cost_estimate=pl.CostEstimate(
            flops=10**8, bytes_accessed=4 * 10**6, transcendentals=10**5
        ),
        name="attend",
    )(slots, *rows, cosine, sine, gain, new_rows, queries)


def project_kernel(
    cells_ref, came_ref, more_ref, uv_ref, weight_ref, mine_ref, other_ref, weight, sems
):
    step = weight.shape[1] // 4
    spans = [slice(i * step, (i + 1) * step) for i in range(4)]
    copies = [
        pltpu.make_async_copy(weight_ref.at[:, span], weight.at[:, span], sems.at[i])
        for i, span in enumerate(spans)
    ]
    for copy in copies:
        copy.start()
    requests = cells_ref.shape[0]
    sources, heads, slots, _ = came_ref.shape
    cells = sources * slots
    pick = cells_ref[:, :1] == lax.broadcasted_iota(I32, (requests, cells), 1)
    pick = jnp.where(pick, 1.0, 0.0).astype(BF)
    projected = []
    for h in range(heads):
        came = came_ref[:, h].astype(F32).reshape(cells, LAT).astype(BF)
        rows = jnp.dot(pick, came, preferred_element_type=F32) + more_ref[h].astype(F32)
        projected.append(
            jnp.dot(rows.astype(BF), uv_ref[h], preferred_element_type=F32).astype(BF)
        )
    projected = jnp.concatenate(projected, axis=1)
    keep = mine_ref.shape[0]
    for span, copy in zip(spans, copies):
        copy.wait()
        sums = jnp.dot(projected, weight[:, span], preferred_element_type=F32).astype(BF)
        mine_ref[:, span] = sums[:keep]
        other_ref[:, span] = sums[keep:]


def project(cells, came, more, w_uv, w_out):
    whole = pl.BlockSpec(memory_space=pltpu.VMEM)
    half = jax.ShapeDtypeStruct((cells.shape[0] // 2, w_out.shape[1]), BF)
    return pl.pallas_call(
        project_kernel,
        out_shape=(half, half),
        in_specs=[whole] * 4 + [pl.BlockSpec(memory_space=pltpu.HBM)],
        out_specs=(whole, whole),
        scratch_shapes=[pltpu.VMEM(w_out.shape, BF), pltpu.SemaphoreType.DMA((4,))],
        compiler_params=pltpu.CompilerParams(vmem_limit_bytes=VMEM),
        cost_estimate=pl.CostEstimate(
            flops=4 * 10**8, bytes_accessed=6 * 10**6, transcendentals=0
        ),
        name="project",
    )(cells, came, more, w_uv, w_out)


def pair_kernel(mine_ref, other_ref, out_ref):
    chips, share, width = out_ref.shape
    step = width // 4
    for first in range(0, width, step):
        span = slice(first, first + step)
        sums = mine_ref[:, span].astype(F32) + other_ref[:, span].astype(F32)
        for chip in range(chips):
            out_ref[chip, :, span] = sums[chip * share : (chip + 1) * share].astype(BF)


def pair_sum(mine, other, chips):
    whole = pl.BlockSpec(memory_space=pltpu.VMEM)
    return pl.pallas_call(
        pair_kernel,
        out_shape=jax.ShapeDtypeStruct((chips, mine.shape[0] // chips, mine.shape[1]), BF),
        in_specs=[whole] * 2,
        out_specs=whole,
        compiler_params=pltpu.CompilerParams(vmem_limit_bytes=32 * 1024 * 1024),
        cost_estimate=pl.CostEstimate(
            flops=4 * 10**5, bytes_accessed=2 * 10**6, transcendentals=0
        ),
        name="pair_sum",
    )(mine, other)


def shards(
    latent_rows,
    new_rows,
    kv_gain,
    lengths,
    owners,
    queries,
    w_uv,
    w_out,
    resid,
    moe_gain,
    route_ids,
    route_weights,
    w_gate,
    w_up,
    w_down,
):
    dp_count = lax.axis_size("dp")
    columns = lax.axis_size("expert")
    devices = dp_count * columns
    group = lax.axis_index("dp")
    column = lax.axis_index("expert")
    core = column % 2
    pre_rows, width = latent_rows.shape
    half_rope = (width - LAT) // 2
    local_units = pre_rows // UNIT
    block_units = columns * local_units
    gain = kv_gain[None, :]

    border = (MOST - 1) * UNIT
    next_rows = lax.ppermute(
        latent_rows[:border], "expert", [((i + 1) % columns, i) for i in range(columns)]
    )
    near_rows = jnp.concatenate([latent_rows, next_rows], axis=0)
    near_rows, late_group = lax.optimization_barrier((near_rows, group))
    rows = [near_rows] + [shift(near_rows, k, dp_count, "dp") for k in range(1, dp_count)]

    request_total = queries.shape[1]
    most_slots = dp_count * local_units
    near_units = local_units + MOST - 1
    where = jnp.stack([group, column]).astype(I32)
    share = request_total // columns
    slot_table_rows, request_rows, cells = tables(
        where, lengths, owners, (dp_count, columns, local_units, near_units, share)
    )
    cosine, sine = turn_table(half_rope)

    model_width = w_out.shape[1]
    piece = model_width // dp_count
    halves = (0, 1, 1, 0)
    quarters = (0, 2, 3, 1)

    def pair_perm(partner):
        perm = []
        for f in range(dp_count):
            for x in range(columns):
                g = (f - x % 2) % dp_count
                perm.append((f * columns + x, (partner(g) + x % 2) % dp_count * columns + x))
        return perm

    weight_perm = pair_perm(lambda g: g ^ 1)
    token_perm = pair_perm(lambda g: dp_count - 1 - g)
    place = (group - core + dp_count) % dp_count

    def quarter_of(g):
        return jnp.where(g == 0, 0, jnp.where(g == 1, 2, jnp.where(g == 2, 3, 1)))

    my_quarter = quarter_of(place)
    their_quarter = quarter_of(place ^ 1)

    def width_half(weight, first):
        return [
            lax.dynamic_slice_in_dim(weight[0], q * piece, piece, 0) for q in (first, first ^ 1)
        ]

    at = jnp.stack(
        [their_quarter, their_quarter ^ 1]
        + [(late_group - k + dp_count) % dp_count for k in range(1, dp_count)]
    ).astype(I32)
    gate_sent, up_sent, down_near, down_far, down_last = weight_slices(
        at, w_gate, w_up, w_down, dp_count
    )
    gate_sent, up_sent, slot_table_rows, *rows = lax.optimization_barrier(
        (gate_sent, up_sent, slot_table_rows, *rows)
    )
    gate_came = lax.ppermute(gate_sent, ("dp", "expert"), weight_perm)
    up_came = lax.ppermute(up_sent, ("dp", "expert"), weight_perm)

    attended, attended_rest = attend(
        slot_table_rows, rows, cosine, sine, gain, new_rows[0], queries[0], most_slots
    )
    unit_start, home_rank, group_start, group_rank, start_column = (
        request_rows[i] for i in range(5)
    )
    own = owners == group
    unit_len = lengths // UNIT
    members = jnp.arange(request_total, dtype=I32)

    head_share = w_uv.shape[0]
    chips = columns // 2

    def to_heads(part):
        came = lax.all_to_all(part, "expert", split_axis=0, concat_axis=0, tiled=True)
        return came.reshape(columns, head_share, part.shape[1], LAT)

    def spill():
        used = jnp.arange(SLOTS, most_slots, dtype=I32) < slot_table_rows[0, 4]
        rest = jnp.where(used[:, None, None], attended_rest, jnp.zeros((), BF))
        came = to_heads(rest.transpose(1, 0, 2))
        count = came.shape[2]
        member_column = group_rank // share
        member_row = (
            (member_column % 2 ^ core) * (chips * share)
            + member_column // 2 * share
            + group_rank % share
        )
        member_cell = jnp.where(home_rank >= SLOTS, start_column * count + home_rank - SLOTS, -1)
        is_row = own[None, :] & (member_row[None, :] == members[:, None])
        cell = jnp.sum(jnp.where(is_row, member_cell[None, :], 0), axis=1)
        pick = (cell[:, None] == jnp.arange(columns * count, dtype=I32)[None, :]).astype(BF)
        return jnp.stack(
            [
                jnp.dot(
                    pick, came[:, h].reshape(columns * count, LAT), preferred_element_type=F32
                ).astype(BF)
                for h in range(head_share)
            ]
        )

    more = lax.cond(
        jnp.max(home_rank) >= SLOTS,
        spill,
        lambda: jnp.zeros((head_share, request_total, LAT), BF),
    )
    by_head = to_heads(attended)
    by_head, gate_came = lax.optimization_barrier((by_head, gate_came))
    mine, other = project(cells, by_head, more, w_uv, w_out)
    mine, other, down_near, down_far, down_last = lax.optimization_barrier(
        (mine, other, down_near, down_far, down_last)
    )
    down_near = shift(down_near, 1, dp_count, "dp")
    down_far = shift(down_far, 2, dp_count, "dp")
    down_last = shift(down_last, 3, dp_count, "dp")

    other = lax.ppermute(other, "expert", [(i, i ^ 1) for i in range(columns)])
    pair_sums = pair_sum(mine, other, chips)
    chip_sums = lax.all_to_all(
        pair_sums,
        "expert",
        split_axis=0,
        concat_axis=0,
        tiled=True,
        axis_index_groups=[[2 * i + c for i in range(chips)] for c in range(2)],
    )
    chip_sums, up_came = lax.optimization_barrier((chip_sums, up_came))
    attention_out = jnp.sum(chip_sums.astype(F32), axis=0)
    residual = resid[0].astype(F32) + attention_out
    normed = (
        residual
        * lax.rsqrt(jnp.mean(residual * residual, axis=1, keepdims=True) + eps)
        * moe_gain[None, :]
    ).astype(BF)

    tokens = resid.shape[1]
    capacity = 2
    expert_ids = jnp.arange(columns, dtype=I32)
    matches = route_ids[0][:, :, None] == expert_ids[None, None, :]
    combine_weights = jnp.sum(jnp.where(matches, route_weights[0][:, :, None], 0.0), axis=1)
    routed = jnp.any(matches, axis=1)
    token_order = jnp.arange(tokens, dtype=I32)
    earlier = token_order[None, :] < token_order[:, None]
    slot_rank = jnp.sum(jnp.where(earlier[:, :, None], routed.astype(I32)[None, :, :], 0), axis=1)
    slot_ids = jnp.arange(capacity, dtype=I32)
    slot_table = routed.T[:, None, :] & (slot_rank.T[:, None, :] == slot_ids[None, :, None])
    table = slot_table.reshape(columns * capacity, tokens)
    even = (jnp.arange(columns * capacity, dtype=I32) // capacity % 2 == 0)[:, None]
    table = jnp.concatenate([table & even, table & ~even], axis=1).astype(BF)
    outgoing = []
    for f in range(dp_count):
        both = jnp.concatenate(
            [
                normed[:, q * piece : (q + 1) * piece]
                for q in (quarters[f], quarters[(f - 1) % dp_count])
            ],
            axis=0,
        )
        outgoing.append(jnp.dot(table, both, preferred_element_type=F32).astype(BF))
    outgoing = jnp.stack(outgoing).reshape(devices, capacity, piece)
    arrived = lax.all_to_all(
        outgoing, ("dp", "expert"), split_axis=0, concat_axis=0, tiled=True
    ).reshape(devices * capacity, piece)

    local_rows = local_units * UNIT
    to_rows = jnp.concatenate(
        [block[:local_rows].reshape(local_units, UNIT, width) for block in rows], axis=0
    ).transpose(1, 0, 2)
    arrived, down_near, down_far, down_last, to_rows = lax.optimization_barrier(
        (arrived, down_near, down_far, down_last, to_rows)
    )
    beside = lax.ppermute(arrived, ("dp", "expert"), token_perm)
    dealt = lax.all_to_all(to_rows, "expert", split_axis=0, concat_axis=0, tiled=True)

    gate_own, up_own = width_half(w_gate, my_quarter), width_half(w_up, my_quarter)
    weights = (gate_came, up_came, gate_own, up_own)
    first = [jnp.dot(arrived, weight[0], preferred_element_type=F32) for weight in weights]
    beside, *first = lax.optimization_barrier((beside, *first))
    gate_given, up_given, gate_sum, up_sum = (
        part + jnp.dot(beside, weight[1], preferred_element_type=F32)
        for part, weight in zip(first, weights)
    )
    given = jnp.concatenate([gate_given, up_given], axis=1).astype(BF)
    given = lax.ppermute(given, ("dp", "expert"), weight_perm).astype(F32)
    half = gate_sum.shape[1]
    hidden = (
        jax.nn.silu(gate_sum + given[:, :half]) * (up_sum + given[:, half:])
    ).astype(BF)
    blocks = [hidden] + [shift(hidden, k, dp_count, "dp") for k in (1, 3, 2)]
    downs = [
        lax.dynamic_slice_in_dim(w_down[0], group * piece, piece, 1),
        down_near,
        down_last,
        down_far,
    ]
    out = jnp.dot(blocks[0], downs[0], preferred_element_type=F32)
    for block, down in zip(blocks[1:3], downs[1:3]):
        out = out + jnp.dot(block, down, preferred_element_type=F32)
    out, last_block, dealt = lax.optimization_barrier((out, blocks[3], dealt))
    out = out + jnp.dot(last_block, downs[3], preferred_element_type=F32)
    returned = lax.all_to_all(
        out.astype(BF).reshape(devices, capacity, piece),
        ("dp", "expert"),
        split_axis=0,
        concat_axis=0,
        tiled=True,
    )

    slots = jnp.arange(pre_rows, dtype=I32)
    offset = slots[:, None] - group_start[None, :]
    covers = own[None, :] & (offset >= 0) & (offset < unit_len[None, :])
    slot_offset = jnp.sum(jnp.where(covers, offset, 0), axis=1)
    slot_unit = jnp.sum(jnp.where(covers, offset + unit_start[None, :], 0), axis=1)
    relative = (slot_unit // block_units - group + dp_count) % dp_count
    cache_place = (
        slot_unit % block_units // local_units * most_slots
        + relative * local_units
        + slot_unit % local_units
    )
    places = jnp.arange(columns * most_slots, dtype=I32)
    pick = (cache_place[:, None] == places[None, :]).astype(BF)
    raw_cache = jnp.dot(
        pick, dealt.reshape(columns * most_slots, width), preferred_element_type=F32
    )
    turned = []
    for table_rows in (cosine, sine):
        mine = jnp.asarray(table_rows).reshape(MOST + 1, UNIT, half_rope)
        mine = lax.dynamic_index_in_dim(mine, column, 1, keepdims=False)
        picked = mine[:1]
        for o in range(1, MOST):
            picked = jnp.where(slot_offset[:, None] == o, mine[o : o + 1], picked)
        turned.append(picked)
    cache_local = norm_rotate(raw_cache, *turned, gain)

    slot_weights = jnp.where(slot_table, combine_weights.T[:, None, :], 0.0)
    moe_sum = jnp.einsum(
        "xct,fxcd->tfd",
        slot_weights,
        returned.reshape(dp_count, columns, capacity, piece).astype(F32),
        precision=lax.Precision.HIGHEST,
    ).reshape(tokens, model_width)
    decoded = (residual + moe_sum).astype(BF)
    return (cache_local[None, None], decoded[None])


def solution(mesh):
    return jax.shard_map(
        shards,
        mesh=mesh,
        in_specs=(
            P(("dp", "expert"), None),
            P("dp", None, None),
            P(),
            P(),
            P(),
            P("dp", None, None, None),
            P("expert", None, None),
            P("expert", None),
            P("dp", "expert", None),
            P(),
            P("dp", "expert", None),
            P("dp", "expert", None),
            P("expert", None, "dp"),
            P("expert", None, "dp"),
            P("expert", "dp", None),
        ),
        out_specs=(P("dp", "expert", None, None), P("dp", "expert", None)),
        check_vma=False,
    )
```

```python
import jax
import jax.numpy as jnp
import numpy as np
from jax import lax
from jax.experimental import pallas as pl
from jax.experimental.pallas import tpu as pltpu
from jax.sharding import PartitionSpec as P

LAT = 512
UNIT = 32
MOST = 3
SLOTS = 8
VMEM = 58 * 1024 * 1024

eps = 1e-06
theta = 10000.0
score_scale = 192.0 ** (-0.5)
BF = jnp.bfloat16
F32 = jnp.float32
I32 = jnp.int32


def turn_table(half_width):
    exponent = -np.arange(half_width, dtype=np.float32) / np.float32(half_width)
    frequency = np.power(np.float32(theta), exponent).astype(np.float32)
    count = (MOST + 1) * UNIT
    angles = np.arange(count, dtype=np.float32)[:, None] * frequency[None, :]
    return np.cos(angles).astype(np.float32), np.sin(angles).astype(np.float32)


def norm_rotate(raw_rows, cosine, sine, kv_gain):
    raw_rows = raw_rows.astype(F32)
    latent = raw_rows[:, :LAT]
    half_width = cosine.shape[1]
    inverse = lax.rsqrt(jnp.mean(latent * latent, axis=1, keepdims=True) + eps)
    latent = latent * inverse * kv_gain
    lower = raw_rows[:, LAT : LAT + half_width]
    upper = raw_rows[:, LAT + half_width :]
    return jnp.concatenate(
        [latent, lower * cosine - upper * sine, upper * cosine + lower * sine], axis=1
    ).astype(BF)


def shift(x, step, size, axis):
    return lax.ppermute(x, axis, [((i + step) % size, i) for i in range(size)])


def table_kernel(where_ref, lengths_ref, owners_ref, slots_ref, rows_ref, cells_ref, *, sizes):
    dp_count, columns, local_units, near_units, share = sizes
    group, column = where_ref[0], where_ref[1]
    group_f, column_f = group.astype(F32), column.astype(F32)
    count = lengths_ref.shape[1]
    units = lengths_ref[...].astype(F32) * (1.0 / UNIT)
    owner = owners_ref[...].astype(F32)
    square = (count, count)
    down = lax.broadcasted_iota(I32, square, 0)
    along = lax.broadcasted_iota(I32, square, 1)
    before = down < along

    def upright(row):
        return jnp.sum(jnp.where(down == along, row, 0.0), axis=1, keepdims=True)

    def whole(x, size):
        return jnp.floor((x + 0.5) * (1.0 / size))

    units_up, owner_up = upright(units), upright(owner)
    start = jnp.sum(jnp.where(before, units_up, 0.0), axis=0, keepdims=True)
    start_source = whole(start, local_units)
    start_block = whole(start_source, columns)
    start_column = start_source - start_block * columns
    home = owner * columns + start_column
    home_up = upright(home)
    rank = jnp.sum(jnp.where(before & (home_up == home), 1.0, 0.0), axis=0, keepdims=True)
    own = owner == group_f
    own_before = before & (owner_up == group_f)
    group_start = jnp.sum(jnp.where(own_before, units_up, 0.0), axis=0, keepdims=True)
    group_rank = jnp.sum(jnp.where(own_before, 1.0, 0.0), axis=0, keepdims=True)

    lines = slots_ref.shape[0]
    line = lax.broadcasted_iota(I32, (lines, count), 0).astype(F32)
    here = home == group_f * columns + column_f
    is_slot = here & (rank == line)
    block = start_block - group_f
    block = jnp.where(block < 0.0, block + dp_count, block)
    place = block * near_units + (start - start_source * local_units)

    def pick(row):
        return jnp.sum(jnp.where(is_slot, row, 0.0), axis=1, keepdims=True)

    near = lax.broadcasted_iota(I32, (lines, 1), 0).astype(F32)
    near_block = whole(near, near_units)
    near_unit = near - near_block * near_units + column_f * local_units
    near_block = near_block + group_f
    near_block = jnp.where(near_block >= dp_count, near_block - dp_count, near_block)
    near_unit = near_unit + near_block * (columns * local_units)
    near_start = jnp.max(jnp.where(start <= near_unit, start, 0.0), axis=1, keepdims=True)
    near_offset = jnp.minimum(near_unit - near_start, MOST - 1.0)
    number = jnp.sum(jnp.where(here, 1.0, 0.0), axis=1, keepdims=True)
    lane = lax.broadcasted_iota(I32, slots_ref.shape, 1)
    packed = jnp.zeros(slots_ref.shape, F32)
    wraps = jnp.where(jnp.full((1, 1), column, I32) == columns - 1, 1.0, 0.0)
    values = (pick(place), pick(units), pick(group_rank), near_offset, number, wraps)
    for i, value in enumerate(values):
        packed = jnp.where(lane == i, value, packed)
    slots_ref[...] = packed.astype(I32)
    rows_ref[...] = jnp.concatenate(
        [start, rank, group_start, group_rank, start_column] + [start] * 3, axis=0
    ).astype(I32)

    member_column = whole(group_rank, share)
    member_chip = whole(member_column, 2)
    other_core = jnp.abs(member_column - 2.0 * member_chip - (column % 2).astype(F32))
    row = (other_core * (columns // 2) + member_chip) * share + (
        group_rank - member_column * share
    )
    lines = cells_ref.shape[0]
    line = lax.broadcasted_iota(I32, (lines, count), 0).astype(F32)
    cell = jnp.where(rank < SLOTS, start_column * SLOTS + rank, -1.0)
    found = jnp.sum(jnp.where(own & (row == line), cell, 0.0), axis=1, keepdims=True)
    cells_ref[...] = jnp.broadcast_to(found, cells_ref.shape).astype(I32)


def tables(where, lengths, owners, sizes):
    lines = sizes[0] * sizes[3]
    whole = pl.BlockSpec(memory_space=pltpu.VMEM)

    def body(*refs):
        table_kernel(*refs, sizes=sizes)

    return pl.pallas_call(
        body,
        out_shape=(
            jax.ShapeDtypeStruct((lines, 128), I32),
            jax.ShapeDtypeStruct((8, lengths.shape[0]), I32),
            jax.ShapeDtypeStruct((sizes[1] * sizes[4], 128), I32),
        ),
        in_specs=[pl.BlockSpec(memory_space=pltpu.SMEM), whole, whole],
        out_specs=(whole, whole, whole),
        compiler_params=pltpu.CompilerParams(vmem_limit_bytes=32 * 1024 * 1024),
        cost_estimate=pl.CostEstimate(flops=1000, bytes_accessed=4096, transcendentals=0),
        name="tables",
    )(where, lengths[None, :], owners[None, :])


def slice_kernel(at_ref, gate_ref, up_ref, down_ref, gate_out, up_out, *refs):
    downs, sems = refs[:-1], refs[-1]
    piece = gate_out.shape[1]
    copies = []
    for weight, out in ((gate_ref, gate_out), (up_ref, up_out)):
        for i in range(2):
            rows = pl.ds(pl.multiple_of(at_ref[i] * piece, 128), piece)
            copies.append((weight.at[0, rows, :], out.at[i]))
    for i, out in enumerate(downs):
        columns = pl.ds(pl.multiple_of(at_ref[2 + i] * piece, 128), piece)
        copies.append((down_ref.at[0, :, columns], out))
    copies = [
        pltpu.make_async_copy(source, target, sems.at[i])
        for i, (source, target) in enumerate(copies)
    ]
    for copy in copies:
        copy.start()
    for copy in copies:
        copy.wait()


def weight_slices(at, w_gate, w_up, w_down, dp_count):
    piece = w_gate.shape[1] // dp_count
    away = pl.BlockSpec(memory_space=pltpu.HBM)
    whole = pl.BlockSpec(memory_space=pltpu.VMEM)
    halves = jax.ShapeDtypeStruct((2, piece, w_gate.shape[2]), BF)
    part = jax.ShapeDtypeStruct((w_down.shape[1], piece), BF)
    return pl.pallas_call(
        slice_kernel,
        out_shape=(halves, halves) + (part,) * (dp_count - 1),
        in_specs=[pl.BlockSpec(memory_space=pltpu.SMEM)] + [away] * 3,
        out_specs=(whole,) * (dp_count + 1),
        scratch_shapes=[pltpu.SemaphoreType.DMA((dp_count + 3,))],
        compiler_params=pltpu.CompilerParams(vmem_limit_bytes=VMEM),
        cost_estimate=pl.CostEstimate(flops=1000, bytes_accessed=4096, transcendentals=0),
        name="weight_slices",
    )(at, w_gate, w_up, w_down)


def attend_kernel(slots_ref, *refs, blocks):
    rows_in = refs[:blocks]
    cos_ref, sin_ref, gain_ref, new_ref, query_ref = refs[blocks : blocks + 5]
    out_ref, rest_ref, keys, query, fresh, held_out, spare, sems, spare_sem = refs[blocks + 5 :]
    number = slots_ref[0, 4]

    def fetch(slot):
        return pltpu.make_async_copy(
            query_ref.at[slots_ref[slot, 2]], query.at[slot], sems.at[slot]
        )

    @pl.loop(0, number)
    def _(slot):
        fetch(slot).start()

    gain = gain_ref[...]
    local_rows = rows_in[0].shape[0] - (MOST - 1) * UNIT
    near_units = rows_in[0].shape[0] // UNIT
    for block, ref in enumerate(rows_in):
        before = near_units * ((block + blocks - 1) % blocks - block)
        for first in range(0, ref.shape[0], UNIT):
            unit = block * near_units + first // UNIT
            if first >= local_rows:
                unit = unit + slots_ref[0, 5] * before
            span = pl.ds(pl.multiple_of(slots_ref[unit, 3] * UNIT, UNIT), UNIT)
            keys[pl.ds(pl.multiple_of(unit * UNIT, UNIT), UNIT), :] = norm_rotate(
                ref[first : first + UNIT, :], cos_ref[span, :], sin_ref[span, :], gain
            )
    fresh[...] = new_ref[...].astype(F32)

    heads = out_ref.shape[0]
    sent = out_ref.shape[1]
    window = MOST * UNIT
    lanes = window + UNIT
    lane = lax.broadcasted_iota(I32, (heads, lanes), 1)

    def one(slot):
        count = slots_ref[slot, 1]
        own = keys[pl.ds(pl.multiple_of(slots_ref[slot, 0] * UNIT, UNIT), window), :]
        at = pl.ds(count * UNIT, 1)
        new = norm_rotate(
            fresh[pl.ds(slots_ref[slot, 2], 1), :], cos_ref[at, :], sin_ref[at, :], gain
        )
        new = jnp.broadcast_to(new.astype(F32), (UNIT, own.shape[1])).astype(BF)
        held = jnp.concatenate([own, new], axis=0)
        scores = (
            lax.dot_general(
                query[slot], held, (((1,), (1,)), ((), ())), preferred_element_type=F32
            )
            * score_scale
        )
        live = (lane < count * UNIT) | (lane == window)
        scores = jnp.where(live, scores, -jnp.inf)
        weights = jnp.exp(scores - jnp.max(scores, axis=1, keepdims=True))
        total = jnp.sum(weights, axis=1, keepdims=True)
        mixture = jnp.dot(weights.astype(BF), held[:, :LAT], preferred_element_type=F32)
        return mixture / total

    @pl.loop(0, number)
    def _(slot):
        fetch(slot).wait()

    for slot in range(sent):
        held_out[slot] = jnp.where(slot < number, one(slot), 0.0)

    out_ref[...] = jnp.swapaxes(held_out[...], 0, 1).astype(BF)

    @pl.loop(sent, number)
    def _(slot):
        spare[...] = one(slot).astype(BF)
        copy = pltpu.make_async_copy(spare, rest_ref.at[slot - sent], spare_sem)
        copy.start()
        copy.wait()


def attend(slots, rows, cosine, sine, gain, new_rows, queries, most_slots):
    heads = queries.shape[1]
    blocks = len(rows)
    total_rows = sum(block.shape[0] for block in rows)
    whole = pl.BlockSpec(memory_space=pltpu.VMEM)

    def body(*refs):
        attend_kernel(*refs, blocks=blocks)

    return pl.pallas_call(
        body,
        out_shape=(
            jax.ShapeDtypeStruct((heads, SLOTS, LAT), BF),
            jax.ShapeDtypeStruct((most_slots - SLOTS, heads, LAT), BF),
        ),
        in_specs=[pl.BlockSpec(memory_space=pltpu.SMEM)]
        + [whole] * (blocks + 4)
        + [pl.BlockSpec(memory_space=pltpu.HBM)],
        out_specs=(whole, pl.BlockSpec(memory_space=pltpu.HBM)),
        scratch_shapes=[
            pltpu.VMEM((total_rows, queries.shape[2]), BF),
            pltpu.VMEM((most_slots,) + queries.shape[1:], BF),
            pltpu.VMEM(new_rows.shape, F32),
            pltpu.VMEM((SLOTS, heads, LAT), F32),
            pltpu.VMEM((heads, LAT), BF),
            pltpu.SemaphoreType.DMA((most_slots,)),
            pltpu.SemaphoreType.DMA,
        ],
        compiler_params=pltpu.CompilerParams(vmem_limit_bytes=VMEM),
        cost_estimate=pl.CostEstimate(
            flops=10**8, bytes_accessed=4 * 10**6, transcendentals=10**5
        ),
        name="attend",
    )(slots, *rows, cosine, sine, gain, new_rows, queries)


def project_kernel(cells_ref, came_ref, more_ref, uv_ref, weight_ref, mine_ref, other_ref):
    requests = cells_ref.shape[0]
    sources, heads, slots, _ = came_ref.shape
    cells = sources * slots
    pick = cells_ref[:, :1] == lax.broadcasted_iota(I32, (requests, cells), 1)
    pick = jnp.where(pick, 1.0, 0.0).astype(BF)
    projected = []
    for h in range(heads):
        came = came_ref[:, h].astype(F32).reshape(cells, LAT).astype(BF)
        rows = jnp.dot(pick, came, preferred_element_type=F32) + more_ref[h].astype(F32)
        projected.append(
            jnp.dot(rows.astype(BF), uv_ref[h], preferred_element_type=F32).astype(BF)
        )
    projected = jnp.concatenate(projected, axis=1)
    keep = mine_ref.shape[0]
    step = weight_ref.shape[1] // 4
    for first in range(0, weight_ref.shape[1], step):
        span = slice(first, first + step)
        sums = jnp.dot(projected, weight_ref[:, span], preferred_element_type=F32).astype(BF)
        mine_ref[:, span] = sums[:keep]
        other_ref[:, span] = sums[keep:]


def project(cells, came, more, w_uv, w_out):
    whole = pl.BlockSpec(memory_space=pltpu.VMEM)
    half = jax.ShapeDtypeStruct((cells.shape[0] // 2, w_out.shape[1]), BF)
    return pl.pallas_call(
        project_kernel,
        out_shape=(half, half),
        in_specs=[whole] * 5,
        out_specs=(whole, whole),
        compiler_params=pltpu.CompilerParams(vmem_limit_bytes=32 * 1024 * 1024),
        cost_estimate=pl.CostEstimate(
            flops=4 * 10**8, bytes_accessed=6 * 10**6, transcendentals=0
        ),
        name="project",
    )(cells, came, more, w_uv, w_out)


def pair_kernel(mine_ref, other_ref, out_ref):
    chips, share, width = out_ref.shape
    step = width // 4
    for first in range(0, width, step):
        span = slice(first, first + step)
        sums = mine_ref[:, span].astype(F32) + other_ref[:, span].astype(F32)
        for chip in range(chips):
            out_ref[chip, :, span] = sums[chip * share : (chip + 1) * share].astype(BF)


def pair_sum(mine, other, chips):
    whole = pl.BlockSpec(memory_space=pltpu.VMEM)
    return pl.pallas_call(
        pair_kernel,
        out_shape=jax.ShapeDtypeStruct((chips, mine.shape[0] // chips, mine.shape[1]), BF),
        in_specs=[whole] * 2,
        out_specs=whole,
        compiler_params=pltpu.CompilerParams(vmem_limit_bytes=32 * 1024 * 1024),
        cost_estimate=pl.CostEstimate(
            flops=4 * 10**5, bytes_accessed=2 * 10**6, transcendentals=0
        ),
        name="pair_sum",
    )(mine, other)


def gate_up_kernel(rows_ref, gate_ref, up_ref, *refs):
    base_ref, out_ref = refs if len(refs) == 2 else (None, refs[0])
    half = gate_ref.shape[2]
    for i, weight_ref in enumerate((gate_ref, up_ref)):
        span = slice(i * half, (i + 1) * half)
        sums = jnp.dot(rows_ref[...], weight_ref[0], preferred_element_type=F32)
        if base_ref is not None:
            sums = sums + base_ref[:, span]
        out_ref[:, span] = sums.astype(out_ref.dtype)


def gate_up(rows, gate, up, quarter, base=None):
    half = gate.shape[2]
    shape = (rows.shape[0], 2 * half)
    whole = pl.BlockSpec(shape, lambda i: (0, 0))
    weight = pl.BlockSpec((1,) + gate.shape[1:], lambda i: (quarter, 0, 0))
    return pl.pallas_call(
        gate_up_kernel,
        grid=(1,),
        out_shape=jax.ShapeDtypeStruct(shape, F32 if base is None else BF),
        in_specs=[pl.BlockSpec(rows.shape, lambda i: (0, 0)), weight, weight]
        + ([] if base is None else [whole]),
        out_specs=whole,
        compiler_params=pltpu.CompilerParams(vmem_limit_bytes=32 * 1024 * 1024),
        cost_estimate=pl.CostEstimate(
            flops=5 * 10**8, bytes_accessed=4 * 10**6, transcendentals=0
        ),
        name="gate_up",
    )(rows, gate, up, *(() if base is None else (base,)))


def shards(
    latent_rows,
    new_rows,
    kv_gain,
    lengths,
    owners,
    queries,
    w_uv,
    w_out,
    resid,
    moe_gain,
    route_ids,
    route_weights,
    w_gate,
    w_up,
    w_down,
):
    dp_count = lax.axis_size("dp")
    columns = lax.axis_size("expert")
    devices = dp_count * columns
    group = lax.axis_index("dp")
    column = lax.axis_index("expert")
    core = column % 2
    pre_rows, width = latent_rows.shape
    half_rope = (width - LAT) // 2
    local_units = pre_rows // UNIT
    block_units = columns * local_units
    gain = kv_gain[None, :]

    border = (MOST - 1) * UNIT
    next_rows = lax.ppermute(
        latent_rows[:border], "expert", [((i + 1) % columns, i) for i in range(columns)]
    )
    near_rows = jnp.concatenate([latent_rows, next_rows], axis=0)
    near_rows, late_group = lax.optimization_barrier((near_rows, group))
    rows = [near_rows] + [shift(near_rows, k, dp_count, "dp") for k in range(1, dp_count)]

    request_total = queries.shape[1]
    most_slots = dp_count * local_units
    near_units = local_units + MOST - 1
    where = jnp.stack([group, column]).astype(I32)
    share = request_total // columns
    slot_table_rows, request_rows, cells = tables(
        where, lengths, owners, (dp_count, columns, local_units, near_units, share)
    )
    cosine, sine = turn_table(half_rope)

    model_width = w_out.shape[1]
    piece = model_width // dp_count
    halves = (0, 1, 1, 0)
    quarters = (0, 2, 3, 1)

    def pair_perm(partner):
        perm = []
        for f in range(dp_count):
            for x in range(columns):
                g = (f - x % 2) % dp_count
                perm.append((f * columns + x, (partner(g) + x % 2) % dp_count * columns + x))
        return perm

    weight_perm = pair_perm(lambda g: g ^ 1)
    token_perm = pair_perm(lambda g: dp_count - 1 - g)
    place = (group - core + dp_count) % dp_count

    def quarter_of(g):
        return jnp.where(g == 0, 0, jnp.where(g == 1, 2, jnp.where(g == 2, 3, 1)))

    my_quarter = quarter_of(place)
    their_quarter = quarter_of(place ^ 1)

    def width_half(weight, first):
        return [
            lax.dynamic_slice_in_dim(weight[0], q * piece, piece, 0) for q in (first, first ^ 1)
        ]

    at = jnp.stack(
        [their_quarter, their_quarter ^ 1]
        + [(late_group - k + dp_count) % dp_count for k in range(1, dp_count)]
    ).astype(I32)
    gate_sent, up_sent, down_near, down_far, down_last = weight_slices(
        at, w_gate, w_up, w_down, dp_count
    )
    gate_sent, up_sent, slot_table_rows, *rows = lax.optimization_barrier(
        (gate_sent, up_sent, slot_table_rows, *rows)
    )
    gate_came = lax.ppermute(gate_sent, ("dp", "expert"), weight_perm)
    up_came = lax.ppermute(up_sent, ("dp", "expert"), weight_perm)

    attended, attended_rest = attend(
        slot_table_rows, rows, cosine, sine, gain, new_rows[0], queries[0], most_slots
    )
    unit_start, home_rank, group_start, group_rank, start_column = (
        request_rows[i] for i in range(5)
    )
    own = owners == group
    unit_len = lengths // UNIT
    members = jnp.arange(request_total, dtype=I32)

    head_share = w_uv.shape[0]
    chips = columns // 2

    def to_heads(part):
        came = lax.all_to_all(part, "expert", split_axis=0, concat_axis=0, tiled=True)
        return came.reshape(columns, head_share, part.shape[1], LAT)

    def spill():
        used = jnp.arange(SLOTS, most_slots, dtype=I32) < slot_table_rows[0, 4]
        rest = jnp.where(used[:, None, None], attended_rest, jnp.zeros((), BF))
        came = to_heads(rest.transpose(1, 0, 2))
        count = came.shape[2]
        member_column = group_rank // share
        member_row = (
            (member_column % 2 ^ core) * (chips * share)
            + member_column // 2 * share
            + group_rank % share
        )
        member_cell = jnp.where(home_rank >= SLOTS, start_column * count + home_rank - SLOTS, -1)
        is_row = own[None, :] & (member_row[None, :] == members[:, None])
        cell = jnp.sum(jnp.where(is_row, member_cell[None, :], 0), axis=1)
        pick = (cell[:, None] == jnp.arange(columns * count, dtype=I32)[None, :]).astype(BF)
        return jnp.stack(
            [
                jnp.dot(
                    pick, came[:, h].reshape(columns * count, LAT), preferred_element_type=F32
                ).astype(BF)
                for h in range(head_share)
            ]
        )

    more = lax.cond(
        jnp.max(home_rank) >= SLOTS,
        spill,
        lambda: jnp.zeros((head_share, request_total, LAT), BF),
    )
    by_head = to_heads(attended)
    by_head, gate_came = lax.optimization_barrier((by_head, gate_came))
    mine, other = project(cells, by_head, more, w_uv, w_out)
    mine, other, down_near, down_last = lax.optimization_barrier(
        (mine, other, down_near, down_last)
    )
    down_near = shift(down_near, 1, dp_count, "dp")
    down_last = shift(down_last, 3, dp_count, "dp")

    other = lax.ppermute(other, "expert", [(i, i ^ 1) for i in range(columns)])
    pair_sums = pair_sum(mine, other, chips)
    chip_sums = lax.all_to_all(
        pair_sums,
        "expert",
        split_axis=0,
        concat_axis=0,
        tiled=True,
        axis_index_groups=[[2 * i + c for i in range(chips)] for c in range(2)],
    )
    chip_sums, up_came = lax.optimization_barrier((chip_sums, up_came))
    attention_out = jnp.sum(chip_sums.astype(F32), axis=0)
    residual = resid[0].astype(F32) + attention_out
    normed = (
        residual
        * lax.rsqrt(jnp.mean(residual * residual, axis=1, keepdims=True) + eps)
        * moe_gain[None, :]
    ).astype(BF)

    tokens = resid.shape[1]
    capacity = 2
    expert_ids = jnp.arange(columns, dtype=I32)
    matches = route_ids[0][:, :, None] == expert_ids[None, None, :]
    combine_weights = jnp.sum(jnp.where(matches, route_weights[0][:, :, None], 0.0), axis=1)
    routed = jnp.any(matches, axis=1)
    token_order = jnp.arange(tokens, dtype=I32)
    earlier = token_order[None, :] < token_order[:, None]
    slot_rank = jnp.sum(jnp.where(earlier[:, :, None], routed.astype(I32)[None, :, :], 0), axis=1)
    slot_ids = jnp.arange(capacity, dtype=I32)
    slot_table = routed.T[:, None, :] & (slot_rank.T[:, None, :] == slot_ids[None, :, None])
    table = slot_table.reshape(columns * capacity, tokens)
    even = (jnp.arange(columns * capacity, dtype=I32) // capacity % 2 == 0)[:, None]
    table = jnp.concatenate([table & even, table & ~even], axis=1).astype(BF)
    outgoing = []
    for f in range(dp_count):
        both = jnp.concatenate(
            [
                normed[:, q * piece : (q + 1) * piece]
                for q in (quarters[f], quarters[(f - 1) % dp_count])
            ],
            axis=0,
        )
        outgoing.append(jnp.dot(table, both, preferred_element_type=F32).astype(BF))
    outgoing = jnp.stack(outgoing).reshape(devices, capacity, piece)
    arrived = lax.all_to_all(
        outgoing, ("dp", "expert"), split_axis=0, concat_axis=0, tiled=True
    ).reshape(devices * capacity, piece)

    local_rows = local_units * UNIT
    to_rows = jnp.concatenate(
        [block[:local_rows].reshape(local_units, UNIT, width) for block in rows], axis=0
    ).transpose(1, 0, 2)
    arrived, down_near, down_last, to_rows = lax.optimization_barrier(
        (arrived, down_near, down_last, to_rows)
    )
    beside = lax.ppermute(arrived, ("dp", "expert"), token_perm)
    dealt = lax.all_to_all(to_rows, "expert", split_axis=0, concat_axis=0, tiled=True)

    gate_own, up_own = width_half(w_gate, my_quarter), width_half(w_up, my_quarter)
    own_halves = (gate_own, up_own)
    first = [jnp.dot(arrived, weight[0], preferred_element_type=F32) for weight in own_halves]
    given = gate_up(arrived, gate_came, up_came, 0)
    beside, given, down_far, *first = lax.optimization_barrier((beside, given, down_far, *first))
    given = gate_up(beside, gate_came, up_came, 1, given)
    given = lax.ppermute(given, ("dp", "expert"), weight_perm).astype(F32)
    down_far = shift(down_far, 2, dp_count, "dp")
    gate_sum, up_sum = (
        part + jnp.dot(beside, weight[1], preferred_element_type=F32)
        for part, weight in zip(first, own_halves)
    )
    half = gate_sum.shape[1]
    hidden = (
        jax.nn.silu(gate_sum + given[:, :half]) * (up_sum + given[:, half:])
    ).astype(BF)
    hidden_all = jnp.concatenate(
        [hidden] + [shift(hidden, k, dp_count, "dp") for k in range(1, dp_count)], axis=1
    )
    hidden_all, dealt = lax.optimization_barrier((hidden_all, dealt))
    downs = jnp.concatenate([lax.dynamic_slice_in_dim(w_down[0], group * piece, piece, 1), down_near, down_far, down_last], axis=0)
    out = jnp.dot(hidden_all, downs, preferred_element_type=F32)
    returned = lax.all_to_all(
        out.astype(BF).reshape(devices, capacity, piece),
        ("dp", "expert"),
        split_axis=0,
        concat_axis=0,
        tiled=True,
    )

    slots = jnp.arange(pre_rows, dtype=I32)
    offset = slots[:, None] - group_start[None, :]
    covers = own[None, :] & (offset >= 0) & (offset < unit_len[None, :])
    slot_offset = jnp.sum(jnp.where(covers, offset, 0), axis=1)
    slot_unit = jnp.sum(jnp.where(covers, offset + unit_start[None, :], 0), axis=1)
    relative = (slot_unit // block_units - group + dp_count) % dp_count
    cache_place = (
        slot_unit % block_units // local_units * most_slots
        + relative * local_units
        + slot_unit % local_units
    )
    places = jnp.arange(columns * most_slots, dtype=I32)
    pick = (cache_place[:, None] == places[None, :]).astype(BF)
    raw_cache = jnp.dot(
        pick, dealt.reshape(columns * most_slots, width), preferred_element_type=F32
    )
    turned = []
    for table_rows in (cosine, sine):
        mine = jnp.asarray(table_rows).reshape(MOST + 1, UNIT, half_rope)
        mine = lax.dynamic_index_in_dim(mine, column, 1, keepdims=False)
        picked = mine[:1]
        for o in range(1, MOST):
            picked = jnp.where(slot_offset[:, None] == o, mine[o : o + 1], picked)
        turned.append(picked)
    cache_local = norm_rotate(raw_cache, *turned, gain)

    slot_weights = jnp.where(slot_table, combine_weights.T[:, None, :], 0.0)
    moe_sum = jnp.einsum(
        "xct,fxcd->tfd",
        slot_weights,
        returned.reshape(dp_count, columns, capacity, piece).astype(F32),
        precision=lax.Precision.HIGHEST,
    ).reshape(tokens, model_width)
    decoded = (residual + moe_sum).astype(BF)
    return (cache_local[None, None], decoded[None])


def solution(mesh):
    return jax.shard_map(
        shards,
        mesh=mesh,
        in_specs=(
            P(("dp", "expert"), None),
            P("dp", None, None),
            P(),
            P(),
            P(),
            P("dp", None, None, None),
            P("expert", None, None),
            P("expert", None),
            P("dp", "expert", None),
            P(),
            P("dp", "expert", None),
            P("dp", "expert", None),
            P("expert", None, "dp"),
            P("expert", None, "dp"),
            P("expert", "dp", None),
        ),
        out_specs=(P("dp", "expert", None, None), P("dp", "expert", None)),
        check_vma=False,
    )
```

```python
import jax
import jax.numpy as jnp
import numpy as np
from jax import lax
from jax.experimental import pallas as pl
from jax.experimental.pallas import tpu as pltpu
from jax.sharding import PartitionSpec as P

LAT = 512
UNIT = 32
MOST = 3
MAIN = 8
SLOTS = 10
PARTS = MAIN // (SLOTS - MAIN)
EXTRA = LAT // PARTS
VMEM = 58 * 1024 * 1024

eps = 1e-06
theta = 10000.0
score_scale = 192.0 ** (-0.5)
BF = jnp.bfloat16
F32 = jnp.float32
I32 = jnp.int32


def turn_table(half_width):
    exponent = -np.arange(half_width, dtype=np.float32) / np.float32(half_width)
    frequency = np.power(np.float32(theta), exponent).astype(np.float32)
    count = (MOST + 1) * UNIT
    angles = np.arange(count, dtype=np.float32)[:, None] * frequency[None, :]
    return np.cos(angles).astype(np.float32), np.sin(angles).astype(np.float32)


def norm_rotate(raw_rows, cosine, sine, kv_gain):
    raw_rows = raw_rows.astype(F32)
    latent = raw_rows[:, :LAT]
    half_width = cosine.shape[1]
    inverse = lax.rsqrt(jnp.mean(latent * latent, axis=1, keepdims=True) + eps)
    latent = latent * inverse * kv_gain
    lower = raw_rows[:, LAT : LAT + half_width]
    upper = raw_rows[:, LAT + half_width :]
    return jnp.concatenate(
        [latent, lower * cosine - upper * sine, upper * cosine + lower * sine], axis=1
    ).astype(BF)


def shift(x, step, size, axis):
    return lax.ppermute(x, axis, [((i + step) % size, i) for i in range(size)])


def table_kernel(where_ref, lengths_ref, owners_ref, slots_ref, rows_ref, cells_ref, *, sizes):
    dp_count, columns, local_units, near_units, share = sizes
    group, column = where_ref[0], where_ref[1]
    group_f, column_f = group.astype(F32), column.astype(F32)
    count = lengths_ref.shape[1]
    units = lengths_ref[...].astype(F32) * (1.0 / UNIT)
    owner = owners_ref[...].astype(F32)
    square = (count, count)
    down = lax.broadcasted_iota(I32, square, 0)
    along = lax.broadcasted_iota(I32, square, 1)
    before = down < along

    def upright(row):
        return jnp.sum(jnp.where(down == along, row, 0.0), axis=1, keepdims=True)

    def whole(x, size):
        return jnp.floor((x + 0.5) * (1.0 / size))

    units_up, owner_up = upright(units), upright(owner)
    start = jnp.sum(jnp.where(before, units_up, 0.0), axis=0, keepdims=True)
    start_source = whole(start, local_units)
    start_block = whole(start_source, columns)
    start_column = start_source - start_block * columns
    home = owner * columns + start_column
    home_up = upright(home)
    rank = jnp.sum(jnp.where(before & (home_up == home), 1.0, 0.0), axis=0, keepdims=True)
    own = owner == group_f
    own_before = before & (owner_up == group_f)
    group_start = jnp.sum(jnp.where(own_before, units_up, 0.0), axis=0, keepdims=True)
    group_rank = jnp.sum(jnp.where(own_before, 1.0, 0.0), axis=0, keepdims=True)

    lines = slots_ref.shape[0]
    line = lax.broadcasted_iota(I32, (lines, count), 0).astype(F32)
    here = home == group_f * columns + column_f
    is_slot = here & (rank == line)
    block = start_block - group_f
    block = jnp.where(block < 0.0, block + dp_count, block)
    place = block * near_units + (start - start_source * local_units)

    def pick(row):
        return jnp.sum(jnp.where(is_slot, row, 0.0), axis=1, keepdims=True)

    near = lax.broadcasted_iota(I32, (lines, 1), 0).astype(F32)
    near_block = whole(near, near_units)
    near_unit = near - near_block * near_units + column_f * local_units
    near_block = near_block + group_f
    near_block = jnp.where(near_block >= dp_count, near_block - dp_count, near_block)
    near_unit = near_unit + near_block * (columns * local_units)
    near_start = jnp.max(jnp.where(start <= near_unit, start, 0.0), axis=1, keepdims=True)
    near_offset = jnp.minimum(near_unit - near_start, MOST - 1.0)
    number = jnp.sum(jnp.where(here, 1.0, 0.0), axis=1, keepdims=True)
    lane = lax.broadcasted_iota(I32, slots_ref.shape, 1)
    packed = jnp.zeros(slots_ref.shape, F32)
    wraps = jnp.where(jnp.full((1, 1), column, I32) == columns - 1, 1.0, 0.0)
    values = (pick(place), pick(units), pick(group_rank), near_offset, number, wraps)
    for i, value in enumerate(values):
        packed = jnp.where(lane == i, value, packed)
    slots_ref[...] = packed.astype(I32)
    rows_ref[...] = jnp.concatenate(
        [start, rank, group_start, group_rank, start_column] + [start] * 3, axis=0
    ).astype(I32)

    member_column = whole(group_rank, share)
    member_chip = whole(member_column, 2)
    other_core = jnp.abs(member_column - 2.0 * member_chip - (column % 2).astype(F32))
    row = (other_core * (columns // 2) + member_chip) * share + (
        group_rank - member_column * share
    )
    lines = cells_ref.shape[0]
    line = lax.broadcasted_iota(I32, (lines, count), 0).astype(F32)
    first_row = start_column * MAIN
    main = jnp.where(rank < MAIN, first_row + rank, -1.0 * MAIN)
    extra = jnp.where(
        (rank >= MAIN) & (rank < SLOTS), first_row + (rank - MAIN) * PARTS, -1.0 * MAIN
    )
    found = [
        jnp.sum(jnp.where(own & (row == line), cell, 0.0), axis=1, keepdims=True)
        for cell in (main, extra)
    ]
    lane = lax.broadcasted_iota(I32, cells_ref.shape, 1)
    cells_ref[...] = jnp.where(lane == 0, found[0], found[1]).astype(I32)


def tables(where, lengths, owners, sizes):
    lines = sizes[0] * sizes[3]
    whole = pl.BlockSpec(memory_space=pltpu.VMEM)

    def body(*refs):
        table_kernel(*refs, sizes=sizes)

    return pl.pallas_call(
        body,
        out_shape=(
            jax.ShapeDtypeStruct((lines, 128), I32),
            jax.ShapeDtypeStruct((8, lengths.shape[0]), I32),
            jax.ShapeDtypeStruct((sizes[1] * sizes[4], 128), I32),
        ),
        in_specs=[pl.BlockSpec(memory_space=pltpu.SMEM), whole, whole],
        out_specs=(whole, whole, whole),
        compiler_params=pltpu.CompilerParams(vmem_limit_bytes=32 * 1024 * 1024),
        cost_estimate=pl.CostEstimate(flops=1000, bytes_accessed=4096, transcendentals=0),
        name="tables",
    )(where, lengths[None, :], owners[None, :])


def slice_kernel(at_ref, gate_ref, up_ref, down_ref, gate_out, up_out, *refs):
    downs, sems = refs[:-1], refs[-1]
    piece = gate_out.shape[1]
    copies = []
    for weight, out in ((gate_ref, gate_out), (up_ref, up_out)):
        for i in range(2):
            rows = pl.ds(pl.multiple_of(at_ref[i] * piece, 128), piece)
            copies.append((weight.at[0, rows, :], out.at[i]))
    for i, out in enumerate(downs):
        columns = pl.ds(pl.multiple_of(at_ref[2 + i] * piece, 128), piece)
        copies.append((down_ref.at[0, :, columns], out))
    copies = [
        pltpu.make_async_copy(source, target, sems.at[i])
        for i, (source, target) in enumerate(copies)
    ]
    for copy in copies:
        copy.start()
    for copy in copies:
        copy.wait()


def weight_slices(at, w_gate, w_up, w_down, dp_count):
    piece = w_gate.shape[1] // dp_count
    away = pl.BlockSpec(memory_space=pltpu.HBM)
    whole = pl.BlockSpec(memory_space=pltpu.VMEM)
    halves = jax.ShapeDtypeStruct((2, piece, w_gate.shape[2]), BF)
    part = jax.ShapeDtypeStruct((w_down.shape[1], piece), BF)
    return pl.pallas_call(
        slice_kernel,
        out_shape=(halves, halves) + (part,) * (dp_count - 1),
        in_specs=[pl.BlockSpec(memory_space=pltpu.SMEM)] + [away] * 3,
        out_specs=(whole,) * (dp_count + 1),
        scratch_shapes=[pltpu.SemaphoreType.DMA((dp_count + 3,))],
        compiler_params=pltpu.CompilerParams(vmem_limit_bytes=VMEM),
        cost_estimate=pl.CostEstimate(flops=1000, bytes_accessed=4096, transcendentals=0),
        name="weight_slices",
    )(at, w_gate, w_up, w_down)


def attend_kernel(slots_ref, *refs, blocks):
    rows_in = refs[:blocks]
    cos_ref, sin_ref, gain_ref, new_ref, query_ref = refs[blocks : blocks + 5]
    out_ref, rest_ref, keys, query, fresh, held_out, spare, sems, spare_sem = refs[blocks + 5 :]
    number = slots_ref[0, 4]

    def fetch(slot):
        return pltpu.make_async_copy(
            query_ref.at[slots_ref[slot, 2]], query.at[slot], sems.at[slot]
        )

    @pl.loop(0, number)
    def _(slot):
        fetch(slot).start()

    gain = gain_ref[...]
    local_rows = rows_in[0].shape[0] - (MOST - 1) * UNIT
    near_units = rows_in[0].shape[0] // UNIT
    for block, ref in enumerate(rows_in):
        before = near_units * ((block + blocks - 1) % blocks - block)
        for first in range(0, ref.shape[0], UNIT):
            unit = block * near_units + first // UNIT
            if first >= local_rows:
                unit = unit + slots_ref[0, 5] * before
            span = pl.ds(pl.multiple_of(slots_ref[unit, 3] * UNIT, UNIT), UNIT)
            keys[pl.ds(pl.multiple_of(unit * UNIT, UNIT), UNIT), :] = norm_rotate(
                ref[first : first + UNIT, :], cos_ref[span, :], sin_ref[span, :], gain
            )
    fresh[...] = new_ref[...].astype(F32)

    heads = out_ref.shape[0]
    sent = SLOTS
    window = MOST * UNIT
    lanes = window + UNIT
    lane = lax.broadcasted_iota(I32, (heads, lanes), 1)

    def one(slot):
        count = slots_ref[slot, 1]
        own = keys[pl.ds(pl.multiple_of(slots_ref[slot, 0] * UNIT, UNIT), window), :]
        at = pl.ds(count * UNIT, 1)
        new = norm_rotate(
            fresh[pl.ds(slots_ref[slot, 2], 1), :], cos_ref[at, :], sin_ref[at, :], gain
        )
        new = jnp.broadcast_to(new.astype(F32), (UNIT, own.shape[1])).astype(BF)
        held = jnp.concatenate([own, new], axis=0)
        scores = (
            lax.dot_general(
                query[slot], held, (((1,), (1,)), ((), ())), preferred_element_type=F32
            )
            * score_scale
        )
        live = (lane < count * UNIT) | (lane == window)
        scores = jnp.where(live, scores, -jnp.inf)
        weights = jnp.exp(scores - jnp.max(scores, axis=1, keepdims=True))
        total = jnp.sum(weights, axis=1, keepdims=True)
        mixture = jnp.dot(weights.astype(BF), held[:, :LAT], preferred_element_type=F32)
        return mixture / total

    @pl.loop(0, number)
    def _(slot):
        fetch(slot).wait()

    for slot in range(sent):
        value = jnp.where(slot < number, one(slot), 0.0)
        if slot < MAIN:
            held_out[slot, :, :LAT] = value
        for i in range(PARTS if slot >= MAIN else 0):
            held_out[(slot - MAIN) * PARTS + i, :, LAT:] = value[:, i * EXTRA : (i + 1) * EXTRA]

    out_ref[...] = jnp.swapaxes(held_out[...], 0, 1).astype(BF)

    @pl.loop(sent, number)
    def _(slot):
        spare[...] = one(slot).astype(BF)
        copy = pltpu.make_async_copy(spare, rest_ref.at[slot - sent], spare_sem)
        copy.start()
        copy.wait()


def attend(slots, rows, cosine, sine, gain, new_rows, queries, most_slots):
    heads = queries.shape[1]
    blocks = len(rows)
    total_rows = sum(block.shape[0] for block in rows)
    whole = pl.BlockSpec(memory_space=pltpu.VMEM)

    def body(*refs):
        attend_kernel(*refs, blocks=blocks)

    return pl.pallas_call(
        body,
        out_shape=(
            jax.ShapeDtypeStruct((heads, MAIN, LAT + EXTRA), BF),
            jax.ShapeDtypeStruct((most_slots - SLOTS, heads, LAT), BF),
        ),
        in_specs=[pl.BlockSpec(memory_space=pltpu.SMEM)]
        + [whole] * (blocks + 4)
        + [pl.BlockSpec(memory_space=pltpu.HBM)],
        out_specs=(whole, pl.BlockSpec(memory_space=pltpu.HBM)),
        scratch_shapes=[
            pltpu.VMEM((total_rows, queries.shape[2]), BF),
            pltpu.VMEM((most_slots,) + queries.shape[1:], BF),
            pltpu.VMEM(new_rows.shape, F32),
            pltpu.VMEM((MAIN, heads, LAT + EXTRA), F32),
            pltpu.VMEM((heads, LAT), BF),
            pltpu.SemaphoreType.DMA((most_slots,)),
            pltpu.SemaphoreType.DMA,
        ],
        compiler_params=pltpu.CompilerParams(vmem_limit_bytes=VMEM),
        cost_estimate=pl.CostEstimate(
            flops=10**8, bytes_accessed=4 * 10**6, transcendentals=10**5
        ),
        name="attend",
    )(slots, *rows, cosine, sine, gain, new_rows, queries)


def project_kernel(cells_ref, came_ref, more_ref, uv_ref, weight_ref, mine_ref, other_ref):
    requests = cells_ref.shape[0]
    sources, heads, slots, _ = came_ref.shape
    cells = sources * slots
    cell = lax.broadcasted_iota(I32, (requests, cells), 1)

    def pick(at):
        return jnp.where(at == cell, 1.0, 0.0).astype(BF)

    main = pick(cells_ref[:, :1])
    extra = [pick(cells_ref[:, 1:2] + i) for i in range(PARTS)]
    projected = []
    for h in range(heads):
        came = came_ref[:, h].astype(F32).reshape(cells, LAT + EXTRA).astype(BF)
        rows = jnp.dot(main, came[:, :LAT], preferred_element_type=F32)
        rest = [jnp.dot(part, came[:, LAT:], preferred_element_type=F32) for part in extra]
        rows = rows + jnp.concatenate(rest, axis=1) + more_ref[h].astype(F32)
        projected.append(
            jnp.dot(rows.astype(BF), uv_ref[h], preferred_element_type=F32).astype(BF)
        )
    projected = jnp.concatenate(projected, axis=1)
    keep = mine_ref.shape[0]
    step = weight_ref.shape[1] // 4
    for first in range(0, weight_ref.shape[1], step):
        span = slice(first, first + step)
        sums = jnp.dot(projected, weight_ref[:, span], preferred_element_type=F32).astype(BF)
        mine_ref[:, span] = sums[:keep]
        other_ref[:, span] = sums[keep:]


def project(cells, came, more, w_uv, w_out):
    whole = pl.BlockSpec(memory_space=pltpu.VMEM)
    half = jax.ShapeDtypeStruct((cells.shape[0] // 2, w_out.shape[1]), BF)
    return pl.pallas_call(
        project_kernel,
        out_shape=(half, half),
        in_specs=[whole] * 5,
        out_specs=(whole, whole),
        compiler_params=pltpu.CompilerParams(vmem_limit_bytes=32 * 1024 * 1024),
        cost_estimate=pl.CostEstimate(
            flops=4 * 10**8, bytes_accessed=6 * 10**6, transcendentals=0
        ),
        name="project",
    )(cells, came, more, w_uv, w_out)


def pair_kernel(mine_ref, other_ref, out_ref):
    chips, share, width = out_ref.shape
    step = width // 4
    for first in range(0, width, step):
        span = slice(first, first + step)
        sums = mine_ref[:, span].astype(F32) + other_ref[:, span].astype(F32)
        for chip in range(chips):
            out_ref[chip, :, span] = sums[chip * share : (chip + 1) * share].astype(BF)


def pair_sum(mine, other, chips):
    whole = pl.BlockSpec(memory_space=pltpu.VMEM)
    return pl.pallas_call(
        pair_kernel,
        out_shape=jax.ShapeDtypeStruct((chips, mine.shape[0] // chips, mine.shape[1]), BF),
        in_specs=[whole] * 2,
        out_specs=whole,
        compiler_params=pltpu.CompilerParams(vmem_limit_bytes=32 * 1024 * 1024),
        cost_estimate=pl.CostEstimate(
            flops=4 * 10**5, bytes_accessed=2 * 10**6, transcendentals=0
        ),
        name="pair_sum",
    )(mine, other)


def gate_up_kernel(rows_ref, gate_ref, up_ref, *refs):
    base_ref, out_ref = refs if len(refs) == 2 else (None, refs[0])
    half = gate_ref.shape[2]
    for i, weight_ref in enumerate((gate_ref, up_ref)):
        span = slice(i * half, (i + 1) * half)
        sums = jnp.dot(rows_ref[...], weight_ref[0], preferred_element_type=F32)
        if base_ref is not None:
            sums = sums + base_ref[:, span]
        out_ref[:, span] = sums.astype(out_ref.dtype)


def gate_up(rows, gate, up, quarter, base=None):
    half = gate.shape[2]
    shape = (rows.shape[0], 2 * half)
    whole = pl.BlockSpec(shape, lambda i: (0, 0))
    weight = pl.BlockSpec((1,) + gate.shape[1:], lambda i: (quarter, 0, 0))
    return pl.pallas_call(
        gate_up_kernel,
        grid=(1,),
        out_shape=jax.ShapeDtypeStruct(shape, F32 if base is None else BF),
        in_specs=[pl.BlockSpec(rows.shape, lambda i: (0, 0)), weight, weight]
        + ([] if base is None else [whole]),
        out_specs=whole,
        compiler_params=pltpu.CompilerParams(vmem_limit_bytes=32 * 1024 * 1024),
        cost_estimate=pl.CostEstimate(
            flops=5 * 10**8, bytes_accessed=4 * 10**6, transcendentals=0
        ),
        name="gate_up",
    )(rows, gate, up, *(() if base is None else (base,)))


def shards(
    latent_rows,
    new_rows,
    kv_gain,
    lengths,
    owners,
    queries,
    w_uv,
    w_out,
    resid,
    moe_gain,
    route_ids,
    route_weights,
    w_gate,
    w_up,
    w_down,
):
    dp_count = lax.axis_size("dp")
    columns = lax.axis_size("expert")
    devices = dp_count * columns
    group = lax.axis_index("dp")
    column = lax.axis_index("expert")
    core = column % 2
    pre_rows, width = latent_rows.shape
    half_rope = (width - LAT) // 2
    local_units = pre_rows // UNIT
    block_units = columns * local_units
    gain = kv_gain[None, :]

    border = (MOST - 1) * UNIT
    next_rows = lax.ppermute(
        latent_rows[:border], "expert", [((i + 1) % columns, i) for i in range(columns)]
    )
    near_rows = jnp.concatenate([latent_rows, next_rows], axis=0)
    near_rows, late_group = lax.optimization_barrier((near_rows, group))
    rows = [near_rows] + [shift(near_rows, k, dp_count, "dp") for k in range(1, dp_count)]

    request_total = queries.shape[1]
    most_slots = dp_count * local_units
    near_units = local_units + MOST - 1
    where = jnp.stack([group, column]).astype(I32)
    share = request_total // columns
    slot_table_rows, request_rows, cells = tables(
        where, lengths, owners, (dp_count, columns, local_units, near_units, share)
    )
    cosine, sine = turn_table(half_rope)

    model_width = w_out.shape[1]
    piece = model_width // dp_count
    halves = (0, 1, 1, 0)
    quarters = (0, 2, 3, 1)

    def pair_perm(partner):
        perm = []
        for f in range(dp_count):
            for x in range(columns):
                g = (f - x % 2) % dp_count
                perm.append((f * columns + x, (partner(g) + x % 2) % dp_count * columns + x))
        return perm

    weight_perm = pair_perm(lambda g: g ^ 1)
    token_perm = pair_perm(lambda g: dp_count - 1 - g)
    place = (group - core + dp_count) % dp_count

    def quarter_of(g):
        return jnp.where(g == 0, 0, jnp.where(g == 1, 2, jnp.where(g == 2, 3, 1)))

    my_quarter = quarter_of(place)
    their_quarter = quarter_of(place ^ 1)

    def width_half(weight, first):
        return [
            lax.dynamic_slice_in_dim(weight[0], q * piece, piece, 0) for q in (first, first ^ 1)
        ]

    at = jnp.stack(
        [their_quarter, their_quarter ^ 1]
        + [(late_group - k + dp_count) % dp_count for k in range(1, dp_count)]
    ).astype(I32)
    gate_sent, up_sent, down_near, down_far, down_last = weight_slices(
        at, w_gate, w_up, w_down, dp_count
    )
    gate_sent, up_sent, slot_table_rows, *rows = lax.optimization_barrier(
        (gate_sent, up_sent, slot_table_rows, *rows)
    )
    gate_came = lax.ppermute(gate_sent, ("dp", "expert"), weight_perm)
    up_came = lax.ppermute(up_sent, ("dp", "expert"), weight_perm)

    attended, attended_rest = attend(
        slot_table_rows, rows, cosine, sine, gain, new_rows[0], queries[0], most_slots
    )
    unit_start, home_rank, group_start, group_rank, start_column = (
        request_rows[i] for i in range(5)
    )
    own = owners == group
    unit_len = lengths // UNIT
    members = jnp.arange(request_total, dtype=I32)

    head_share = w_uv.shape[0]
    chips = columns // 2

    def to_heads(part):
        came = lax.all_to_all(part, "expert", split_axis=0, concat_axis=0, tiled=True)
        return came.reshape((columns, head_share) + part.shape[1:])

    def spill():
        used = jnp.arange(SLOTS, most_slots, dtype=I32) < slot_table_rows[0, 4]
        rest = jnp.where(used[:, None, None], attended_rest, jnp.zeros((), BF))
        came = to_heads(rest.transpose(1, 0, 2))
        count = came.shape[2]
        member_column = group_rank // share
        member_row = (
            (member_column % 2 ^ core) * (chips * share)
            + member_column // 2 * share
            + group_rank % share
        )
        member_cell = jnp.where(home_rank >= SLOTS, start_column * count + home_rank - SLOTS, -1)
        is_row = own[None, :] & (member_row[None, :] == members[:, None])
        cell = jnp.sum(jnp.where(is_row, member_cell[None, :], 0), axis=1)
        pick = (cell[:, None] == jnp.arange(columns * count, dtype=I32)[None, :]).astype(BF)
        return jnp.stack(
            [
                jnp.dot(
                    pick, came[:, h].reshape(columns * count, LAT), preferred_element_type=F32
                ).astype(BF)
                for h in range(head_share)
            ]
        )

    more = lax.cond(
        jnp.max(home_rank) >= SLOTS,
        spill,
        lambda: jnp.zeros((head_share, request_total, LAT), BF),
    )
    by_head = to_heads(attended)
    by_head, gate_came = lax.optimization_barrier((by_head, gate_came))
    mine, other = project(cells, by_head, more, w_uv, w_out)
    mine, other, down_near, down_last = lax.optimization_barrier(
        (mine, other, down_near, down_last)
    )
    down_near = shift(down_near, 1, dp_count, "dp")
    down_last = shift(down_last, 3, dp_count, "dp")

    other = lax.ppermute(other, "expert", [(i, i ^ 1) for i in range(columns)])
    pair_sums = pair_sum(mine, other, chips)
    chip_sums = lax.all_to_all(
        pair_sums,
        "expert",
        split_axis=0,
        concat_axis=0,
        tiled=True,
        axis_index_groups=[[2 * i + c for i in range(chips)] for c in range(2)],
    )
    cut = down_far.shape[0] // 2
    chip_sums, up_came, down_far = lax.optimization_barrier((chip_sums, up_came, down_far))
    far_first = shift(down_far[:cut], 2, dp_count, "dp")
    attention_out = jnp.sum(chip_sums.astype(F32), axis=0)
    residual = resid[0].astype(F32) + attention_out
    normed = (
        residual
        * lax.rsqrt(jnp.mean(residual * residual, axis=1, keepdims=True) + eps)
        * moe_gain[None, :]
    ).astype(BF)

    tokens = resid.shape[1]
    capacity = 2
    expert_ids = jnp.arange(columns, dtype=I32)
    matches = route_ids[0][:, :, None] == expert_ids[None, None, :]
    combine_weights = jnp.sum(jnp.where(matches, route_weights[0][:, :, None], 0.0), axis=1)
    routed = jnp.any(matches, axis=1)
    token_order = jnp.arange(tokens, dtype=I32)
    earlier = token_order[None, :] < token_order[:, None]
    slot_rank = jnp.sum(jnp.where(earlier[:, :, None], routed.astype(I32)[None, :, :], 0), axis=1)
    slot_ids = jnp.arange(capacity, dtype=I32)
    slot_table = routed.T[:, None, :] & (slot_rank.T[:, None, :] == slot_ids[None, :, None])
    table = slot_table.reshape(columns * capacity, tokens)
    even = (jnp.arange(columns * capacity, dtype=I32) // capacity % 2 == 0)[:, None]
    table = jnp.concatenate([table & even, table & ~even], axis=1).astype(BF)
    outgoing = []
    for f in range(dp_count):
        both = jnp.concatenate(
            [
                normed[:, q * piece : (q + 1) * piece]
                for q in (quarters[f], quarters[(f - 1) % dp_count])
            ],
            axis=0,
        )
        outgoing.append(jnp.dot(table, both, preferred_element_type=F32).astype(BF))
    outgoing = jnp.stack(outgoing).reshape(devices, capacity, piece)
    arrived = lax.all_to_all(
        outgoing, ("dp", "expert"), split_axis=0, concat_axis=0, tiled=True
    ).reshape(devices * capacity, piece)

    local_rows = local_units * UNIT
    to_rows = jnp.concatenate(
        [block[:local_rows].reshape(local_units, UNIT, width) for block in rows], axis=0
    ).transpose(1, 0, 2)
    arrived, down_near, far_first, down_last, to_rows = lax.optimization_barrier(
        (arrived, down_near, far_first, down_last, to_rows)
    )
    beside = lax.ppermute(arrived, ("dp", "expert"), token_perm)
    dealt = lax.all_to_all(to_rows, "expert", split_axis=0, concat_axis=0, tiled=True)

    gate_own, up_own = width_half(w_gate, my_quarter), width_half(w_up, my_quarter)
    own_halves = (gate_own, up_own)
    first = [jnp.dot(arrived, weight[0], preferred_element_type=F32) for weight in own_halves]
    given = gate_up(arrived, gate_came, up_came, 0)
    beside, given, down_far, *first = lax.optimization_barrier((beside, given, down_far, *first))
    given = gate_up(beside, gate_came, up_came, 1, given)
    given = lax.ppermute(given, ("dp", "expert"), weight_perm).astype(F32)
    far_second = shift(down_far[cut:], 2, dp_count, "dp")
    gate_sum, up_sum = (
        part + jnp.dot(beside, weight[1], preferred_element_type=F32)
        for part, weight in zip(first, own_halves)
    )
    half = gate_sum.shape[1]
    hidden = (
        jax.nn.silu(gate_sum + given[:, :half]) * (up_sum + given[:, half:])
    ).astype(BF)
    hidden_all = jnp.concatenate(
        [hidden] + [shift(hidden, k, dp_count, "dp") for k in range(1, dp_count)], axis=1
    )
    hidden_all, dealt = lax.optimization_barrier((hidden_all, dealt))
    downs = jnp.concatenate([lax.dynamic_slice_in_dim(w_down[0], group * piece, piece, 1), down_near, far_first, far_second, down_last], axis=0)
    out = jnp.dot(hidden_all, downs, preferred_element_type=F32)
    returned = lax.all_to_all(
        out.astype(BF).reshape(devices, capacity, piece),
        ("dp", "expert"),
        split_axis=0,
        concat_axis=0,
        tiled=True,
    )

    slots = jnp.arange(pre_rows, dtype=I32)
    offset = slots[:, None] - group_start[None, :]
    covers = own[None, :] & (offset >= 0) & (offset < unit_len[None, :])
    slot_offset = jnp.sum(jnp.where(covers, offset, 0), axis=1)
    slot_unit = jnp.sum(jnp.where(covers, offset + unit_start[None, :], 0), axis=1)
    relative = (slot_unit // block_units - group + dp_count) % dp_count
    cache_place = (
        slot_unit % block_units // local_units * most_slots
        + relative * local_units
        + slot_unit % local_units
    )
    places = jnp.arange(columns * most_slots, dtype=I32)
    pick = (cache_place[:, None] == places[None, :]).astype(BF)
    raw_cache = jnp.dot(
        pick, dealt.reshape(columns * most_slots, width), preferred_element_type=F32
    )
    turned = []
    for table_rows in (cosine, sine):
        mine = jnp.asarray(table_rows).reshape(MOST + 1, UNIT, half_rope)
        mine = lax.dynamic_index_in_dim(mine, column, 1, keepdims=False)
        picked = mine[:1]
        for o in range(1, MOST):
            picked = jnp.where(slot_offset[:, None] == o, mine[o : o + 1], picked)
        turned.append(picked)
    cache_local = norm_rotate(raw_cache, *turned, gain)

    slot_weights = jnp.where(slot_table, combine_weights.T[:, None, :], 0.0)
    moe_sum = jnp.einsum(
        "xct,fxcd->tfd",
        slot_weights,
        returned.reshape(dp_count, columns, capacity, piece).astype(F32),
        precision=lax.Precision.HIGHEST,
    ).reshape(tokens, model_width)
    decoded = (residual + moe_sum).astype(BF)
    return (cache_local[None, None], decoded[None])


def solution(mesh):
    return jax.shard_map(
        shards,
        mesh=mesh,
        in_specs=(
            P(("dp", "expert"), None),
            P("dp", None, None),
            P(),
            P(),
            P(),
            P("dp", None, None, None),
            P("expert", None, None),
            P("expert", None),
            P("dp", "expert", None),
            P(),
            P("dp", "expert", None),
            P("dp", "expert", None),
            P("expert", None, "dp"),
            P("expert", None, "dp"),
            P("expert", "dp", None),
        ),
        out_specs=(P("dp", "expert", None, None), P("dp", "expert", None)),
        check_vma=False,
    )
```

```python
import jax
import jax.numpy as jnp
import numpy as np
from jax import lax
from jax.experimental import pallas as pl
from jax.experimental.pallas import tpu as pltpu
from jax.sharding import PartitionSpec as P

LAT = 512
UNIT = 32
MOST = 3
MAIN = 8
SLOTS = 10
PARTS = MAIN // (SLOTS - MAIN)
EXTRA = LAT // PARTS
VMEM = 58 * 1024 * 1024
SMALL = 20 * 1024 * 1024

eps = 1e-06
theta = 10000.0
score_scale = 192.0 ** (-0.5)
BF = jnp.bfloat16
F32 = jnp.float32
I32 = jnp.int32


def turn_table(half_width):
    exponent = -np.arange(half_width, dtype=np.float32) / np.float32(half_width)
    frequency = np.power(np.float32(theta), exponent).astype(np.float32)
    count = (MOST + 1) * UNIT
    angles = np.arange(count, dtype=np.float32)[:, None] * frequency[None, :]
    return np.cos(angles).astype(np.float32), np.sin(angles).astype(np.float32)


def norm_rotate(raw_rows, cosine, sine, kv_gain):
    raw_rows = raw_rows.astype(F32)
    latent = raw_rows[:, :LAT]
    half_width = cosine.shape[1]
    inverse = lax.rsqrt(jnp.mean(latent * latent, axis=1, keepdims=True) + eps)
    latent = latent * inverse * kv_gain
    lower = raw_rows[:, LAT : LAT + half_width]
    upper = raw_rows[:, LAT + half_width :]
    return jnp.concatenate(
        [latent, lower * cosine - upper * sine, upper * cosine + lower * sine], axis=1
    ).astype(BF)


def shift(x, step, size, axis):
    return lax.ppermute(x, axis, [((i + step) % size, i) for i in range(size)])


def table_kernel(where_ref, lengths_ref, owners_ref, slots_ref, rows_ref, cells_ref, *, sizes):
    dp_count, columns, local_units, near_units, share = sizes
    group, column = where_ref[0], where_ref[1]
    group_f, column_f = group.astype(F32), column.astype(F32)
    count = lengths_ref.shape[1]
    units = lengths_ref[...].astype(F32) * (1.0 / UNIT)
    owner = owners_ref[...].astype(F32)
    square = (count, count)
    down = lax.broadcasted_iota(I32, square, 0)
    along = lax.broadcasted_iota(I32, square, 1)
    before = down < along

    def upright(row):
        return jnp.sum(jnp.where(down == along, row, 0.0), axis=1, keepdims=True)

    def whole(x, size):
        return jnp.floor((x + 0.5) * (1.0 / size))

    units_up, owner_up = upright(units), upright(owner)
    start = jnp.sum(jnp.where(before, units_up, 0.0), axis=0, keepdims=True)
    start_source = whole(start, local_units)
    start_block = whole(start_source, columns)
    start_column = start_source - start_block * columns
    home = owner * columns + start_column
    home_up = upright(home)
    rank = jnp.sum(jnp.where(before & (home_up == home), 1.0, 0.0), axis=0, keepdims=True)
    own = owner == group_f
    own_before = before & (owner_up == group_f)
    group_start = jnp.sum(jnp.where(own_before, units_up, 0.0), axis=0, keepdims=True)
    group_rank = jnp.sum(jnp.where(own_before, 1.0, 0.0), axis=0, keepdims=True)

    lines = slots_ref.shape[0]
    line = lax.broadcasted_iota(I32, (lines, count), 0).astype(F32)
    here = home == group_f * columns + column_f
    is_slot = here & (rank == line)
    block = start_block - group_f
    block = jnp.where(block < 0.0, block + dp_count, block)
    place = block * near_units + (start - start_source * local_units)

    def pick(row):
        return jnp.sum(jnp.where(is_slot, row, 0.0), axis=1, keepdims=True)

    near = lax.broadcasted_iota(I32, (lines, 1), 0).astype(F32)
    near_block = whole(near, near_units)
    near_unit = near - near_block * near_units + column_f * local_units
    near_block = near_block + group_f
    near_block = jnp.where(near_block >= dp_count, near_block - dp_count, near_block)
    near_unit = near_unit + near_block * (columns * local_units)
    near_start = jnp.max(jnp.where(start <= near_unit, start, 0.0), axis=1, keepdims=True)
    near_offset = jnp.minimum(near_unit - near_start, MOST - 1.0)
    number = jnp.sum(jnp.where(here, 1.0, 0.0), axis=1, keepdims=True)
    lane = lax.broadcasted_iota(I32, slots_ref.shape, 1)
    packed = jnp.zeros(slots_ref.shape, F32)
    wraps = jnp.where(jnp.full((1, 1), column, I32) == columns - 1, 1.0, 0.0)
    values = (pick(place), pick(units), pick(group_rank), near_offset, number, wraps)
    for i, value in enumerate(values):
        packed = jnp.where(lane == i, value, packed)
    slots_ref[...] = packed.astype(I32)
    rows_ref[...] = jnp.concatenate(
        [start, rank, group_start, group_rank, start_column] + [start] * 3, axis=0
    ).astype(I32)

    member_column = whole(group_rank, share)
    member_chip = whole(member_column, 2)
    other_core = jnp.abs(member_column - 2.0 * member_chip - (column % 2).astype(F32))
    row = (other_core * (columns // 2) + member_chip) * share + (
        group_rank - member_column * share
    )
    lines = cells_ref.shape[0]
    line = lax.broadcasted_iota(I32, (lines, count), 0).astype(F32)
    first_row = start_column * MAIN
    main = jnp.where(rank < MAIN, first_row + rank, -1.0 * MAIN)
    extra = jnp.where(
        (rank >= MAIN) & (rank < SLOTS), first_row + (rank - MAIN) * PARTS, -1.0 * MAIN
    )
    found = [
        jnp.sum(jnp.where(own & (row == line), cell, 0.0), axis=1, keepdims=True)
        for cell in (main, extra)
    ]
    lane = lax.broadcasted_iota(I32, cells_ref.shape, 1)
    cells_ref[...] = jnp.where(lane == 0, found[0], found[1]).astype(I32)


def tables(where, lengths, owners, sizes):
    lines = sizes[0] * sizes[3]
    whole = pl.BlockSpec(memory_space=pltpu.VMEM)

    def body(*refs):
        table_kernel(*refs, sizes=sizes)

    return pl.pallas_call(
        body,
        out_shape=(
            jax.ShapeDtypeStruct((lines, 128), I32),
            jax.ShapeDtypeStruct((8, lengths.shape[0]), I32),
            jax.ShapeDtypeStruct((sizes[1] * sizes[4], 128), I32),
        ),
        in_specs=[pl.BlockSpec(memory_space=pltpu.SMEM), whole, whole],
        out_specs=(whole, whole, whole),
        compiler_params=pltpu.CompilerParams(vmem_limit_bytes=32 * 1024 * 1024),
        cost_estimate=pl.CostEstimate(flops=1000, bytes_accessed=4096, transcendentals=0),
        name="tables",
    )(where, lengths[None, :], owners[None, :])


def slice_kernel(at_ref, gate_ref, up_ref, down_ref, gate_out, up_out, *refs):
    downs, sems = refs[:-1], refs[-1]
    piece = gate_out.shape[1]
    copies = []
    for weight, out in ((gate_ref, gate_out), (up_ref, up_out)):
        for i in range(2):
            rows = pl.ds(pl.multiple_of(at_ref[i] * piece, 128), piece)
            copies.append((weight.at[0, rows, :], out.at[i]))
    for i, outs in enumerate((downs[:1], downs[1:3], downs[3:])):
        columns = pl.ds(pl.multiple_of(at_ref[2 + i] * piece, 128), piece)
        first = 0
        for out in outs:
            copies.append((down_ref.at[0, pl.ds(first, out.shape[0]), columns], out))
            first += out.shape[0]
    copies = [
        pltpu.make_async_copy(source, target, sems.at[i])
        for i, (source, target) in enumerate(copies)
    ]
    for copy in copies:
        copy.start()
    for copy in copies:
        copy.wait()


def weight_slices(at, w_gate, w_up, w_down, dp_count):
    piece = w_gate.shape[1] // dp_count
    away = pl.BlockSpec(memory_space=pltpu.HBM)
    whole = pl.BlockSpec(memory_space=pltpu.VMEM)
    halves = jax.ShapeDtypeStruct((2, piece, w_gate.shape[2]), BF)
    part = jax.ShapeDtypeStruct((w_down.shape[1], piece), BF)
    cut = jax.ShapeDtypeStruct((w_down.shape[1] // 2, piece), BF)
    return pl.pallas_call(
        slice_kernel,
        out_shape=(halves, halves, part, cut, cut, part),
        in_specs=[pl.BlockSpec(memory_space=pltpu.SMEM)] + [away] * 3,
        out_specs=(whole,) * 6,
        scratch_shapes=[pltpu.SemaphoreType.DMA((8,))],
        compiler_params=pltpu.CompilerParams(vmem_limit_bytes=VMEM),
        cost_estimate=pl.CostEstimate(flops=1000, bytes_accessed=4096, transcendentals=0),
        name="weight_slices",
    )(at, w_gate, w_up, w_down)


def attend_kernel(slots_ref, *refs, blocks):
    rows_in = refs[:blocks]
    cos_ref, sin_ref, gain_ref, new_ref, query_ref = refs[blocks : blocks + 5]
    out_ref, rest_ref, keys, query, fresh, held_out, spare, sems, spare_sem = refs[blocks + 5 :]
    number = slots_ref[0, 4]

    def fetch(slot):
        return pltpu.make_async_copy(
            query_ref.at[slots_ref[slot, 2]], query.at[slot], sems.at[slot]
        )

    @pl.loop(0, number)
    def _(slot):
        fetch(slot).start()

    gain = gain_ref[...]
    local_rows = rows_in[0].shape[0] - (MOST - 1) * UNIT
    near_units = rows_in[0].shape[0] // UNIT
    for block, ref in enumerate(rows_in):
        before = near_units * ((block + blocks - 1) % blocks - block)
        for first in range(0, ref.shape[0], UNIT):
            unit = block * near_units + first // UNIT
            if first >= local_rows:
                unit = unit + slots_ref[0, 5] * before
            span = pl.ds(pl.multiple_of(slots_ref[unit, 3] * UNIT, UNIT), UNIT)
            keys[pl.ds(pl.multiple_of(unit * UNIT, UNIT), UNIT), :] = norm_rotate(
                ref[first : first + UNIT, :], cos_ref[span, :], sin_ref[span, :], gain
            )
    fresh[...] = new_ref[...].astype(F32)

    heads = out_ref.shape[0]
    sent = SLOTS
    window = MOST * UNIT
    lanes = window + UNIT
    lane = lax.broadcasted_iota(I32, (heads, lanes), 1)

    def one(slot):
        count = slots_ref[slot, 1]
        own = keys[pl.ds(pl.multiple_of(slots_ref[slot, 0] * UNIT, UNIT), window), :]
        at = pl.ds(count * UNIT, 1)
        new = norm_rotate(
            fresh[pl.ds(slots_ref[slot, 2], 1), :], cos_ref[at, :], sin_ref[at, :], gain
        )
        new = jnp.broadcast_to(new.astype(F32), (UNIT, own.shape[1])).astype(BF)
        held = jnp.concatenate([own, new], axis=0)
        scores = (
            lax.dot_general(
                query[slot], held, (((1,), (1,)), ((), ())), preferred_element_type=F32
            )
            * score_scale
        )
        live = (lane < count * UNIT) | (lane == window)
        scores = jnp.where(live, scores, -jnp.inf)
        weights = jnp.exp(scores - jnp.max(scores, axis=1, keepdims=True))
        total = jnp.sum(weights, axis=1, keepdims=True)
        mixture = jnp.dot(weights.astype(BF), held[:, :LAT], preferred_element_type=F32)
        return mixture / total

    @pl.loop(0, number)
    def _(slot):
        fetch(slot).wait()

    for slot in range(sent):
        value = jnp.where(slot < number, one(slot), 0.0)
        if slot < MAIN:
            held_out[slot, :, :LAT] = value
        for i in range(PARTS if slot >= MAIN else 0):
            held_out[(slot - MAIN) * PARTS + i, :, LAT:] = value[:, i * EXTRA : (i + 1) * EXTRA]

    out_ref[...] = jnp.swapaxes(held_out[...], 0, 1).astype(BF)

    @pl.loop(sent, number)
    def _(slot):
        spare[...] = one(slot).astype(BF)
        copy = pltpu.make_async_copy(spare, rest_ref.at[slot - sent], spare_sem)
        copy.start()
        copy.wait()


def attend(slots, rows, cosine, sine, gain, new_rows, queries, most_slots):
    heads = queries.shape[1]
    blocks = len(rows)
    total_rows = sum(block.shape[0] for block in rows)
    whole = pl.BlockSpec(memory_space=pltpu.VMEM)

    def body(*refs):
        attend_kernel(*refs, blocks=blocks)

    return pl.pallas_call(
        body,
        out_shape=(
            jax.ShapeDtypeStruct((heads, MAIN, LAT + EXTRA), BF),
            jax.ShapeDtypeStruct((most_slots - SLOTS, heads, LAT), BF),
        ),
        in_specs=[pl.BlockSpec(memory_space=pltpu.SMEM)]
        + [whole] * (blocks + 4)
        + [pl.BlockSpec(memory_space=pltpu.HBM)],
        out_specs=(whole, pl.BlockSpec(memory_space=pltpu.HBM)),
        scratch_shapes=[
            pltpu.VMEM((total_rows, queries.shape[2]), BF),
            pltpu.VMEM((most_slots,) + queries.shape[1:], BF),
            pltpu.VMEM(new_rows.shape, F32),
            pltpu.VMEM((MAIN, heads, LAT + EXTRA), F32),
            pltpu.VMEM((heads, LAT), BF),
            pltpu.SemaphoreType.DMA((most_slots,)),
            pltpu.SemaphoreType.DMA,
        ],
        compiler_params=pltpu.CompilerParams(vmem_limit_bytes=VMEM),
        cost_estimate=pl.CostEstimate(
            flops=10**8, bytes_accessed=4 * 10**6, transcendentals=10**5
        ),
        name="attend",
    )(slots, *rows, cosine, sine, gain, new_rows, queries)


def project_kernel(cells_ref, came_ref, more_ref, uv_ref, weight_ref, mine_ref, other_ref):
    requests = cells_ref.shape[0]
    sources, heads, slots, _ = came_ref.shape
    cells = sources * slots
    cell = lax.broadcasted_iota(I32, (requests, cells), 1)

    def pick(at):
        return jnp.where(at == cell, 1.0, 0.0).astype(BF)

    main = pick(cells_ref[:, :1])
    extra = [pick(cells_ref[:, 1:2] + i) for i in range(PARTS)]
    projected = []
    for h in range(heads):
        came = came_ref[:, h].astype(F32).reshape(cells, LAT + EXTRA).astype(BF)
        rows = jnp.dot(main, came[:, :LAT], preferred_element_type=F32)
        rest = [jnp.dot(part, came[:, LAT:], preferred_element_type=F32) for part in extra]
        rows = rows + jnp.concatenate(rest, axis=1) + more_ref[h].astype(F32)
        projected.append(
            jnp.dot(rows.astype(BF), uv_ref[h], preferred_element_type=F32).astype(BF)
        )
    projected = jnp.concatenate(projected, axis=1)
    keep = mine_ref.shape[0]
    step = weight_ref.shape[1] // 4
    for first in range(0, weight_ref.shape[1], step):
        span = slice(first, first + step)
        sums = jnp.dot(projected, weight_ref[:, span], preferred_element_type=F32).astype(BF)
        mine_ref[:, span] = sums[:keep]
        other_ref[:, span] = sums[keep:]


def project(cells, came, more, w_uv, w_out):
    whole = pl.BlockSpec(memory_space=pltpu.VMEM)
    half = jax.ShapeDtypeStruct((cells.shape[0] // 2, w_out.shape[1]), BF)
    return pl.pallas_call(
        project_kernel,
        out_shape=(half, half),
        in_specs=[whole] * 5,
        out_specs=(whole, whole),
        compiler_params=pltpu.CompilerParams(vmem_limit_bytes=SMALL),
        cost_estimate=pl.CostEstimate(
            flops=4 * 10**8, bytes_accessed=6 * 10**6, transcendentals=0
        ),
        name="project",
    )(cells, came, more, w_uv, w_out)


def pair_kernel(mine_ref, other_ref, out_ref):
    chips, share, width = out_ref.shape
    step = width // 4
    for first in range(0, width, step):
        span = slice(first, first + step)
        sums = mine_ref[:, span].astype(F32) + other_ref[:, span].astype(F32)
        for chip in range(chips):
            out_ref[chip, :, span] = sums[chip * share : (chip + 1) * share].astype(BF)


def pair_sum(mine, other, chips):
    whole = pl.BlockSpec(memory_space=pltpu.VMEM)
    return pl.pallas_call(
        pair_kernel,
        out_shape=jax.ShapeDtypeStruct((chips, mine.shape[0] // chips, mine.shape[1]), BF),
        in_specs=[whole] * 2,
        out_specs=whole,
        compiler_params=pltpu.CompilerParams(vmem_limit_bytes=SMALL),
        cost_estimate=pl.CostEstimate(
            flops=4 * 10**5, bytes_accessed=2 * 10**6, transcendentals=0
        ),
        name="pair_sum",
    )(mine, other)


def gate_up_kernel(rows_ref, gate_ref, up_ref, *refs):
    base_ref, out_ref = refs if len(refs) == 2 else (None, refs[0])
    half = gate_ref.shape[2]
    for i, weight_ref in enumerate((gate_ref, up_ref)):
        span = slice(i * half, (i + 1) * half)
        sums = jnp.dot(rows_ref[...], weight_ref[0], preferred_element_type=F32)
        if base_ref is not None:
            sums = sums + base_ref[:, span]
        out_ref[:, span] = sums.astype(out_ref.dtype)


def gate_up(rows, gate, up, quarter, base=None):
    half = gate.shape[2]
    shape = (rows.shape[0], 2 * half)
    whole = pl.BlockSpec(shape, lambda i: (0, 0))
    weight = pl.BlockSpec((1,) + gate.shape[1:], lambda i: (quarter, 0, 0))
    return pl.pallas_call(
        gate_up_kernel,
        grid=(1,),
        out_shape=jax.ShapeDtypeStruct(shape, F32 if base is None else BF),
        in_specs=[pl.BlockSpec(rows.shape, lambda i: (0, 0)), weight, weight]
        + ([] if base is None else [whole]),
        out_specs=whole,
        compiler_params=pltpu.CompilerParams(vmem_limit_bytes=SMALL),
        cost_estimate=pl.CostEstimate(
            flops=5 * 10**8, bytes_accessed=4 * 10**6, transcendentals=0
        ),
        name="gate_up",
    )(rows, gate, up, *(() if base is None else (base,)))


def down_kernel(*refs):
    blocks, weights, out_ref = refs[:4], refs[4:9], refs[9]
    cut = weights[2].shape[0]
    step = out_ref.shape[1] // 2
    for first in range(0, out_ref.shape[1], step):
        span = slice(first, first + step)
        sums = jnp.dot(blocks[0][...], weights[0][:, span], preferred_element_type=F32)
        for rows, weight in (
            (blocks[1][...], weights[1]),
            (blocks[2][:, :cut], weights[2]),
            (blocks[2][:, cut:], weights[3]),
            (blocks[3][...], weights[4]),
        ):
            sums = sums + jnp.dot(rows, weight[:, span], preferred_element_type=F32)
        out_ref[:, span] = sums.astype(BF)


def down_product(blocks, weights):
    whole = pl.BlockSpec(memory_space=pltpu.VMEM)
    return pl.pallas_call(
        down_kernel,
        out_shape=jax.ShapeDtypeStruct((blocks[0].shape[0], weights[0].shape[1]), BF),
        in_specs=[whole] * 9,
        out_specs=whole,
        compiler_params=pltpu.CompilerParams(vmem_limit_bytes=SMALL),
        cost_estimate=pl.CostEstimate(
            flops=10**9, bytes_accessed=5 * 10**6, transcendentals=0
        ),
        name="down_product",
    )(*blocks, *weights)


def shards(
    latent_rows,
    new_rows,
    kv_gain,
    lengths,
    owners,
    queries,
    w_uv,
    w_out,
    resid,
    moe_gain,
    route_ids,
    route_weights,
    w_gate,
    w_up,
    w_down,
):
    dp_count = lax.axis_size("dp")
    columns = lax.axis_size("expert")
    devices = dp_count * columns
    group = lax.axis_index("dp")
    column = lax.axis_index("expert")
    core = column % 2
    pre_rows, width = latent_rows.shape
    half_rope = (width - LAT) // 2
    local_units = pre_rows // UNIT
    block_units = columns * local_units
    gain = kv_gain[None, :]

    border = (MOST - 1) * UNIT
    next_rows = lax.ppermute(
        latent_rows[:border], "expert", [((i + 1) % columns, i) for i in range(columns)]
    )
    near_rows = jnp.concatenate([latent_rows, next_rows], axis=0)
    near_rows, late_group = lax.optimization_barrier((near_rows, group))
    rows = [near_rows] + [shift(near_rows, k, dp_count, "dp") for k in range(1, dp_count)]

    request_total = queries.shape[1]
    most_slots = dp_count * local_units
    near_units = local_units + MOST - 1
    where = jnp.stack([group, column]).astype(I32)
    share = request_total // columns
    slot_table_rows, request_rows, cells = tables(
        where, lengths, owners, (dp_count, columns, local_units, near_units, share)
    )
    cosine, sine = turn_table(half_rope)

    model_width = w_out.shape[1]
    piece = model_width // dp_count
    halves = (0, 1, 1, 0)
    quarters = (0, 2, 3, 1)

    def pair_perm(partner):
        perm = []
        for f in range(dp_count):
            for x in range(columns):
                g = (f - x % 2) % dp_count
                perm.append((f * columns + x, (partner(g) + x % 2) % dp_count * columns + x))
        return perm

    weight_perm = pair_perm(lambda g: g ^ 1)
    token_perm = pair_perm(lambda g: dp_count - 1 - g)
    place = (group - core + dp_count) % dp_count

    def quarter_of(g):
        return jnp.where(g == 0, 0, jnp.where(g == 1, 2, jnp.where(g == 2, 3, 1)))

    my_quarter = quarter_of(place)
    their_quarter = quarter_of(place ^ 1)

    def width_half(weight, first):
        return [
            lax.dynamic_slice_in_dim(weight[0], q * piece, piece, 0) for q in (first, first ^ 1)
        ]

    at = jnp.stack(
        [their_quarter, their_quarter ^ 1]
        + [(late_group - k + dp_count) % dp_count for k in range(1, dp_count)]
    ).astype(I32)
    gate_sent, up_sent, down_near, far_first, far_second, down_last = weight_slices(
        at, w_gate, w_up, w_down, dp_count
    )
    gate_sent, up_sent, slot_table_rows, *rows = lax.optimization_barrier(
        (gate_sent, up_sent, slot_table_rows, *rows)
    )
    gate_came = lax.ppermute(gate_sent, ("dp", "expert"), weight_perm)
    up_came = lax.ppermute(up_sent, ("dp", "expert"), weight_perm)

    attended, attended_rest = attend(
        slot_table_rows, rows, cosine, sine, gain, new_rows[0], queries[0], most_slots
    )
    unit_start, home_rank, group_start, group_rank, start_column = (
        request_rows[i] for i in range(5)
    )
    own = owners == group
    unit_len = lengths // UNIT
    members = jnp.arange(request_total, dtype=I32)

    head_share = w_uv.shape[0]
    chips = columns // 2

    def to_heads(part):
        came = lax.all_to_all(part, "expert", split_axis=0, concat_axis=0, tiled=True)
        return came.reshape((columns, head_share) + part.shape[1:])

    def spill():
        used = jnp.arange(SLOTS, most_slots, dtype=I32) < slot_table_rows[0, 4]
        rest = jnp.where(used[:, None, None], attended_rest, jnp.zeros((), BF))
        came = to_heads(rest.transpose(1, 0, 2))
        count = came.shape[2]
        member_column = group_rank // share
        member_row = (
            (member_column % 2 ^ core) * (chips * share)
            + member_column // 2 * share
            + group_rank % share
        )
        member_cell = jnp.where(home_rank >= SLOTS, start_column * count + home_rank - SLOTS, -1)
        is_row = own[None, :] & (member_row[None, :] == members[:, None])
        cell = jnp.sum(jnp.where(is_row, member_cell[None, :], 0), axis=1)
        pick = (cell[:, None] == jnp.arange(columns * count, dtype=I32)[None, :]).astype(BF)
        return jnp.stack(
            [
                jnp.dot(
                    pick, came[:, h].reshape(columns * count, LAT), preferred_element_type=F32
                ).astype(BF)
                for h in range(head_share)
            ]
        )

    more = lax.cond(
        jnp.max(home_rank) >= SLOTS,
        spill,
        lambda: jnp.zeros((head_share, request_total, LAT), BF),
    )
    by_head = to_heads(attended)
    by_head, gate_came = lax.optimization_barrier((by_head, gate_came))
    mine, other = project(cells, by_head, more, w_uv, w_out)
    mine, other, down_near, down_last = lax.optimization_barrier(
        (mine, other, down_near, down_last)
    )
    down_near = shift(down_near, 1, dp_count, "dp")
    down_last = shift(down_last, 3, dp_count, "dp")

    other = lax.ppermute(other, "expert", [(i, i ^ 1) for i in range(columns)])
    pair_sums = pair_sum(mine, other, chips)
    chip_sums = lax.all_to_all(
        pair_sums,
        "expert",
        split_axis=0,
        concat_axis=0,
        tiled=True,
        axis_index_groups=[[2 * i + c for i in range(chips)] for c in range(2)],
    )
    chip_sums, up_came, far_first = lax.optimization_barrier((chip_sums, up_came, far_first))
    far_first = shift(far_first, 2, dp_count, "dp")
    attention_out = jnp.sum(chip_sums.astype(F32), axis=0)
    residual = resid[0].astype(F32) + attention_out
    normed = (
        residual
        * lax.rsqrt(jnp.mean(residual * residual, axis=1, keepdims=True) + eps)
        * moe_gain[None, :]
    ).astype(BF)

    tokens = resid.shape[1]
    capacity = 2
    expert_ids = jnp.arange(columns, dtype=I32)
    matches = route_ids[0][:, :, None] == expert_ids[None, None, :]
    combine_weights = jnp.sum(jnp.where(matches, route_weights[0][:, :, None], 0.0), axis=1)
    routed = jnp.any(matches, axis=1)
    token_order = jnp.arange(tokens, dtype=I32)
    earlier = token_order[None, :] < token_order[:, None]
    slot_rank = jnp.sum(jnp.where(earlier[:, :, None], routed.astype(I32)[None, :, :], 0), axis=1)
    slot_ids = jnp.arange(capacity, dtype=I32)
    slot_table = routed.T[:, None, :] & (slot_rank.T[:, None, :] == slot_ids[None, :, None])
    table = slot_table.reshape(columns * capacity, tokens)
    even = (jnp.arange(columns * capacity, dtype=I32) // capacity % 2 == 0)[:, None]
    table = jnp.concatenate([table & even, table & ~even], axis=1).astype(BF)
    outgoing = []
    for f in range(dp_count):
        both = jnp.concatenate(
            [
                normed[:, q * piece : (q + 1) * piece]
                for q in (quarters[f], quarters[(f - 1) % dp_count])
            ],
            axis=0,
        )
        outgoing.append(jnp.dot(table, both, preferred_element_type=F32).astype(BF))
    outgoing = jnp.stack(outgoing).reshape(devices, capacity, piece)
    arrived = lax.all_to_all(
        outgoing, ("dp", "expert"), split_axis=0, concat_axis=0, tiled=True
    ).reshape(devices * capacity, piece)

    local_rows = local_units * UNIT
    to_rows = jnp.concatenate(
        [block[:local_rows].reshape(local_units, UNIT, width) for block in rows], axis=0
    ).transpose(1, 0, 2)
    arrived, down_near, far_first, down_last, to_rows = lax.optimization_barrier(
        (arrived, down_near, far_first, down_last, to_rows)
    )
    beside = lax.ppermute(arrived, ("dp", "expert"), token_perm)
    dealt = lax.all_to_all(to_rows, "expert", split_axis=0, concat_axis=0, tiled=True)

    gate_own, up_own = width_half(w_gate, my_quarter), width_half(w_up, my_quarter)
    own_halves = (gate_own, up_own)
    first = [jnp.dot(arrived, weight[0], preferred_element_type=F32) for weight in own_halves]
    given = gate_up(arrived, gate_came, up_came, 0)
    beside, given, far_second, *first = lax.optimization_barrier(
        (beside, given, far_second, *first)
    )
    given = gate_up(beside, gate_came, up_came, 1, given)
    given = lax.ppermute(given, ("dp", "expert"), weight_perm).astype(F32)
    far_second = shift(far_second, 2, dp_count, "dp")
    gate_sum, up_sum = (
        part + jnp.dot(beside, weight[1], preferred_element_type=F32)
        for part, weight in zip(first, own_halves)
    )
    half = gate_sum.shape[1]
    hidden = (
        jax.nn.silu(gate_sum + given[:, :half]) * (up_sum + given[:, half:])
    ).astype(BF)
    blocks = [hidden] + [shift(hidden, k, dp_count, "dp") for k in range(1, dp_count)]
    down_own = lax.dynamic_slice_in_dim(w_down[0], group * piece, piece, 1)
    blocks[0], dealt = lax.optimization_barrier((blocks[0], dealt))
    out = down_product(blocks, [down_own, down_near, far_first, far_second, down_last])
    returned = lax.all_to_all(
        out.reshape(devices, capacity, piece),
        ("dp", "expert"),
        split_axis=0,
        concat_axis=0,
        tiled=True,
    )

    slots = jnp.arange(pre_rows, dtype=I32)
    offset = slots[:, None] - group_start[None, :]
    covers = own[None, :] & (offset >= 0) & (offset < unit_len[None, :])
    slot_offset = jnp.sum(jnp.where(covers, offset, 0), axis=1)
    slot_unit = jnp.sum(jnp.where(covers, offset + unit_start[None, :], 0), axis=1)
    relative = (slot_unit // block_units - group + dp_count) % dp_count
    cache_place = (
        slot_unit % block_units // local_units * most_slots
        + relative * local_units
        + slot_unit % local_units
    )
    places = jnp.arange(columns * most_slots, dtype=I32)
    pick = (cache_place[:, None] == places[None, :]).astype(BF)
    raw_cache = jnp.dot(
        pick, dealt.reshape(columns * most_slots, width), preferred_element_type=F32
    )
    turned = []
    for table_rows in (cosine, sine):
        mine = jnp.asarray(table_rows).reshape(MOST + 1, UNIT, half_rope)
        mine = lax.dynamic_index_in_dim(mine, column, 1, keepdims=False)
        picked = mine[:1]
        for o in range(1, MOST):
            picked = jnp.where(slot_offset[:, None] == o, mine[o : o + 1], picked)
        turned.append(picked)
    cache_local = norm_rotate(raw_cache, *turned, gain)

    slot_weights = jnp.where(slot_table, combine_weights.T[:, None, :], 0.0)
    moe_sum = jnp.einsum(
        "xct,fxcd->tfd",
        slot_weights,
        returned.reshape(dp_count, columns, capacity, piece).astype(F32),
        precision=lax.Precision.HIGHEST,
    ).reshape(tokens, model_width)
    decoded = (residual + moe_sum).astype(BF)
    return (cache_local[None, None], decoded[None])


def solution(mesh):
    return jax.shard_map(
        shards,
        mesh=mesh,
        in_specs=(
            P(("dp", "expert"), None),
            P("dp", None, None),
            P(),
            P(),
            P(),
            P("dp", None, None, None),
            P("expert", None, None),
            P("expert", None),
            P("dp", "expert", None),
            P(),
            P("dp", "expert", None),
            P("dp", "expert", None),
            P("expert", None, "dp"),
            P("expert", None, "dp"),
            P("expert", "dp", None),
        ),
        out_specs=(P("dp", "expert", None, None), P("dp", "expert", None)),
        check_vma=False,
    )
```

```python
import jax
import jax.numpy as jnp
import numpy as np
from jax import lax
from jax.experimental import pallas as pl
from jax.experimental.pallas import tpu as pltpu
from jax.sharding import PartitionSpec as P

LAT = 512
UNIT = 32
MOST = 3
MAIN = 8
SLOTS = 10
PARTS = MAIN // (SLOTS - MAIN)
EXTRA = LAT // PARTS
VMEM = 58 * 1024 * 1024

eps = 1e-06
theta = 10000.0
score_scale = 192.0 ** (-0.5)
BF = jnp.bfloat16
F32 = jnp.float32
I32 = jnp.int32


def turn_table(half_width):
    exponent = -np.arange(half_width, dtype=np.float32) / np.float32(half_width)
    frequency = np.power(np.float32(theta), exponent).astype(np.float32)
    count = (MOST + 1) * UNIT
    angles = np.arange(count, dtype=np.float32)[:, None] * frequency[None, :]
    return np.cos(angles).astype(np.float32), np.sin(angles).astype(np.float32)


def norm_rotate(raw_rows, cosine, sine, kv_gain):
    raw_rows = raw_rows.astype(F32)
    latent = raw_rows[:, :LAT]
    half_width = cosine.shape[1]
    inverse = lax.rsqrt(jnp.mean(latent * latent, axis=1, keepdims=True) + eps)
    latent = latent * inverse * kv_gain
    lower = raw_rows[:, LAT : LAT + half_width]
    upper = raw_rows[:, LAT + half_width :]
    return jnp.concatenate(
        [latent, lower * cosine - upper * sine, upper * cosine + lower * sine], axis=1
    ).astype(BF)


def shift(x, step, size, axis):
    return lax.ppermute(x, axis, [((i + step) % size, i) for i in range(size)])


def table_kernel(where_ref, lengths_ref, owners_ref, slots_ref, rows_ref, cells_ref, *, sizes):
    dp_count, columns, local_units, near_units, share = sizes
    group, column = where_ref[0], where_ref[1]
    group_f, column_f = group.astype(F32), column.astype(F32)
    count = lengths_ref.shape[1]
    units = lengths_ref[...].astype(F32) * (1.0 / UNIT)
    owner = owners_ref[...].astype(F32)
    square = (count, count)
    down = lax.broadcasted_iota(I32, square, 0)
    along = lax.broadcasted_iota(I32, square, 1)
    before = down < along

    def upright(row):
        return jnp.sum(jnp.where(down == along, row, 0.0), axis=1, keepdims=True)

    def whole(x, size):
        return jnp.floor((x + 0.5) * (1.0 / size))

    units_up, owner_up = upright(units), upright(owner)
    start = jnp.sum(jnp.where(before, units_up, 0.0), axis=0, keepdims=True)
    start_source = whole(start, local_units)
    start_block = whole(start_source, columns)
    start_column = start_source - start_block * columns
    home = owner * columns + start_column
    home_up = upright(home)
    rank = jnp.sum(jnp.where(before & (home_up == home), 1.0, 0.0), axis=0, keepdims=True)
    own = owner == group_f
    own_before = before & (owner_up == group_f)
    group_start = jnp.sum(jnp.where(own_before, units_up, 0.0), axis=0, keepdims=True)
    group_rank = jnp.sum(jnp.where(own_before, 1.0, 0.0), axis=0, keepdims=True)

    lines = slots_ref.shape[0]
    line = lax.broadcasted_iota(I32, (lines, count), 0).astype(F32)
    here = home == group_f * columns + column_f
    is_slot = here & (rank == line)
    block = start_block - group_f
    block = jnp.where(block < 0.0, block + dp_count, block)
    place = block * near_units + (start - start_source * local_units)

    def pick(row):
        return jnp.sum(jnp.where(is_slot, row, 0.0), axis=1, keepdims=True)

    near = lax.broadcasted_iota(I32, (lines, 1), 0).astype(F32)
    near_block = whole(near, near_units)
    near_unit = near - near_block * near_units + column_f * local_units
    near_block = near_block + group_f
    near_block = jnp.where(near_block >= dp_count, near_block - dp_count, near_block)
    near_unit = near_unit + near_block * (columns * local_units)
    near_start = jnp.max(jnp.where(start <= near_unit, start, 0.0), axis=1, keepdims=True)
    near_offset = jnp.minimum(near_unit - near_start, MOST - 1.0)
    number = jnp.sum(jnp.where(here, 1.0, 0.0), axis=1, keepdims=True)
    lane = lax.broadcasted_iota(I32, slots_ref.shape, 1)
    packed = jnp.zeros(slots_ref.shape, F32)
    wraps = jnp.where(jnp.full((1, 1), column, I32) == columns - 1, 1.0, 0.0)
    values = (pick(place), pick(units), pick(group_rank), near_offset, number, wraps)
    for i, value in enumerate(values):
        packed = jnp.where(lane == i, value, packed)
    slots_ref[...] = packed.astype(I32)
    rows_ref[...] = jnp.concatenate(
        [start, rank, group_start, group_rank, start_column] + [start] * 3, axis=0
    ).astype(I32)

    member_column = whole(group_rank, share)
    member_chip = whole(member_column, 2)
    other_core = jnp.abs(member_column - 2.0 * member_chip - (column % 2).astype(F32))
    row = (other_core * (columns // 2) + member_chip) * share + (
        group_rank - member_column * share
    )
    lines = cells_ref.shape[0]
    line = lax.broadcasted_iota(I32, (lines, count), 0).astype(F32)
    first_row = start_column * MAIN
    main = jnp.where(rank < MAIN, first_row + rank, -1.0 * MAIN)
    extra = jnp.where(
        (rank >= MAIN) & (rank < SLOTS), first_row + (rank - MAIN) * PARTS, -1.0 * MAIN
    )
    found = [
        jnp.sum(jnp.where(own & (row == line), cell, 0.0), axis=1, keepdims=True)
        for cell in (main, extra)
    ]
    lane = lax.broadcasted_iota(I32, cells_ref.shape, 1)
    cells_ref[...] = jnp.where(lane == 0, found[0], found[1]).astype(I32)


def tables(where, lengths, owners, sizes):
    lines = sizes[0] * sizes[3]
    whole = pl.BlockSpec(memory_space=pltpu.VMEM)

    def body(*refs):
        table_kernel(*refs, sizes=sizes)

    return pl.pallas_call(
        body,
        out_shape=(
            jax.ShapeDtypeStruct((lines, 128), I32),
            jax.ShapeDtypeStruct((8, lengths.shape[0]), I32),
            jax.ShapeDtypeStruct((sizes[1] * sizes[4], 128), I32),
        ),
        in_specs=[pl.BlockSpec(memory_space=pltpu.SMEM), whole, whole],
        out_specs=(whole, whole, whole),
        compiler_params=pltpu.CompilerParams(vmem_limit_bytes=32 * 1024 * 1024),
        cost_estimate=pl.CostEstimate(flops=1000, bytes_accessed=4096, transcendentals=0),
        name="tables",
    )(where, lengths[None, :], owners[None, :])


def slice_kernel(at_ref, gate_ref, up_ref, down_ref, gate_out, up_out, *refs):
    downs, sems = refs[:-1], refs[-1]
    piece = gate_out.shape[1]
    copies = []
    for weight, out in ((gate_ref, gate_out), (up_ref, up_out)):
        for i in range(2):
            rows = pl.ds(pl.multiple_of(at_ref[i] * piece, 128), piece)
            copies.append((weight.at[0, rows, :], out.at[i]))
    for i, outs in enumerate((downs[:1], downs[1:3], downs[3:])):
        columns = pl.ds(pl.multiple_of(at_ref[2 + i] * piece, 128), piece)
        first = 0
        for out in outs:
            copies.append((down_ref.at[0, pl.ds(first, out.shape[0]), columns], out))
            first += out.shape[0]
    copies = [
        pltpu.make_async_copy(source, target, sems.at[i])
        for i, (source, target) in enumerate(copies)
    ]
    for copy in copies:
        copy.start()
    for copy in copies:
        copy.wait()


def weight_slices(at, w_gate, w_up, w_down, dp_count):
    piece = w_gate.shape[1] // dp_count
    away = pl.BlockSpec(memory_space=pltpu.HBM)
    whole = pl.BlockSpec(memory_space=pltpu.VMEM)
    halves = jax.ShapeDtypeStruct((2, piece, w_gate.shape[2]), BF)
    part = jax.ShapeDtypeStruct((w_down.shape[1], piece), BF)
    cut = jax.ShapeDtypeStruct((w_down.shape[1] // 2, piece), BF)
    return pl.pallas_call(
        slice_kernel,
        out_shape=(halves, halves, part, cut, cut, part),
        in_specs=[pl.BlockSpec(memory_space=pltpu.SMEM)] + [away] * 3,
        out_specs=(whole,) * 6,
        scratch_shapes=[pltpu.SemaphoreType.DMA((8,))],
        compiler_params=pltpu.CompilerParams(vmem_limit_bytes=VMEM),
        cost_estimate=pl.CostEstimate(flops=1000, bytes_accessed=4096, transcendentals=0),
        name="weight_slices",
    )(at, w_gate, w_up, w_down)


def attend_kernel(slots_ref, *refs, blocks):
    rows_in = refs[:blocks]
    cos_ref, sin_ref, gain_ref, new_ref, query_ref = refs[blocks : blocks + 5]
    out_ref, rest_ref, keys, query, fresh, held_out, spare, sems, spare_sem = refs[blocks + 5 :]
    number = slots_ref[0, 4]

    def fetch(slot):
        return pltpu.make_async_copy(
            query_ref.at[slots_ref[slot, 2]], query.at[slot], sems.at[slot]
        )

    @pl.loop(0, number)
    def _(slot):
        fetch(slot).start()

    gain = gain_ref[...]
    local_rows = rows_in[0].shape[0] - (MOST - 1) * UNIT
    near_units = rows_in[0].shape[0] // UNIT
    for block, ref in enumerate(rows_in):
        before = near_units * ((block + blocks - 1) % blocks - block)
        for first in range(0, ref.shape[0], UNIT):
            unit = block * near_units + first // UNIT
            if first >= local_rows:
                unit = unit + slots_ref[0, 5] * before
            span = pl.ds(pl.multiple_of(slots_ref[unit, 3] * UNIT, UNIT), UNIT)
            keys[pl.ds(pl.multiple_of(unit * UNIT, UNIT), UNIT), :] = norm_rotate(
                ref[first : first + UNIT, :], cos_ref[span, :], sin_ref[span, :], gain
            )
    fresh[...] = new_ref[...].astype(F32)

    heads = out_ref.shape[0]
    sent = SLOTS
    window = MOST * UNIT
    lanes = window + UNIT
    lane = lax.broadcasted_iota(I32, (heads, lanes), 1)

    def one(slot):
        count = slots_ref[slot, 1]
        own = keys[pl.ds(pl.multiple_of(slots_ref[slot, 0] * UNIT, UNIT), window), :]
        at = pl.ds(count * UNIT, 1)
        new = norm_rotate(
            fresh[pl.ds(slots_ref[slot, 2], 1), :], cos_ref[at, :], sin_ref[at, :], gain
        )
        new = jnp.broadcast_to(new.astype(F32), (UNIT, own.shape[1])).astype(BF)
        held = jnp.concatenate([own, new], axis=0)
        scores = (
            lax.dot_general(
                query[slot], held, (((1,), (1,)), ((), ())), preferred_element_type=F32
            )
            * score_scale
        )
        live = (lane < count * UNIT) | (lane == window)
        scores = jnp.where(live, scores, -jnp.inf)
        weights = jnp.exp(scores - jnp.max(scores, axis=1, keepdims=True))
        total = jnp.sum(weights, axis=1, keepdims=True)
        mixture = jnp.dot(weights.astype(BF), held[:, :LAT], preferred_element_type=F32)
        return mixture / total

    @pl.loop(0, number)
    def _(slot):
        fetch(slot).wait()

    for slot in range(sent):
        value = jnp.where(slot < number, one(slot), 0.0)
        if slot < MAIN:
            held_out[slot, :, :LAT] = value
        for i in range(PARTS if slot >= MAIN else 0):
            held_out[(slot - MAIN) * PARTS + i, :, LAT:] = value[:, i * EXTRA : (i + 1) * EXTRA]

    out_ref[...] = jnp.swapaxes(held_out[...], 0, 1).astype(BF)

    @pl.loop(sent, number)
    def _(slot):
        spare[...] = one(slot).astype(BF)
        copy = pltpu.make_async_copy(spare, rest_ref.at[slot - sent], spare_sem)
        copy.start()
        copy.wait()


def attend(slots, rows, cosine, sine, gain, new_rows, queries, most_slots):
    heads = queries.shape[1]
    blocks = len(rows)
    total_rows = sum(block.shape[0] for block in rows)
    whole = pl.BlockSpec(memory_space=pltpu.VMEM)

    def body(*refs):
        attend_kernel(*refs, blocks=blocks)

    return pl.pallas_call(
        body,
        out_shape=(
            jax.ShapeDtypeStruct((heads, MAIN, LAT + EXTRA), BF),
            jax.ShapeDtypeStruct((most_slots - SLOTS, heads, LAT), BF),
        ),
        in_specs=[pl.BlockSpec(memory_space=pltpu.SMEM)]
        + [whole] * (blocks + 4)
        + [pl.BlockSpec(memory_space=pltpu.HBM)],
        out_specs=(whole, pl.BlockSpec(memory_space=pltpu.HBM)),
        scratch_shapes=[
            pltpu.VMEM((total_rows, queries.shape[2]), BF),
            pltpu.VMEM((most_slots,) + queries.shape[1:], BF),
            pltpu.VMEM(new_rows.shape, F32),
            pltpu.VMEM((MAIN, heads, LAT + EXTRA), F32),
            pltpu.VMEM((heads, LAT), BF),
            pltpu.SemaphoreType.DMA((most_slots,)),
            pltpu.SemaphoreType.DMA,
        ],
        compiler_params=pltpu.CompilerParams(vmem_limit_bytes=VMEM),
        cost_estimate=pl.CostEstimate(
            flops=10**8, bytes_accessed=4 * 10**6, transcendentals=10**5
        ),
        name="attend",
    )(slots, *rows, cosine, sine, gain, new_rows, queries)


def project_kernel(
    cells_ref, came_ref, more_ref, uv_ref, weight_ref, mine_ref, other_ref, weight, sems
):
    step = weight.shape[1] // 4
    spans = [slice(i * step, (i + 1) * step) for i in range(4)]
    copies = [
        pltpu.make_async_copy(weight_ref.at[:, span], weight.at[:, span], sems.at[i])
        for i, span in enumerate(spans)
    ]
    for copy in copies:
        copy.start()
    requests = cells_ref.shape[0]
    sources, heads, slots, _ = came_ref.shape
    cells = sources * slots
    cell = lax.broadcasted_iota(I32, (requests, cells), 1)

    def pick(at):
        return jnp.where(at == cell, 1.0, 0.0).astype(BF)

    main = pick(cells_ref[:, :1])
    extra = [pick(cells_ref[:, 1:2] + i) for i in range(PARTS)]
    projected = []
    for h in range(heads):
        came = came_ref[:, h].astype(F32).reshape(cells, LAT + EXTRA).astype(BF)
        rows = jnp.dot(main, came[:, :LAT], preferred_element_type=F32)
        rest = [jnp.dot(part, came[:, LAT:], preferred_element_type=F32) for part in extra]
        rows = rows + jnp.concatenate(rest, axis=1) + more_ref[h].astype(F32)
        projected.append(
            jnp.dot(rows.astype(BF), uv_ref[h], preferred_element_type=F32).astype(BF)
        )
    projected = jnp.concatenate(projected, axis=1)
    keep = mine_ref.shape[0]
    for span, copy in zip(spans, copies):
        copy.wait()
        sums = jnp.dot(projected, weight[:, span], preferred_element_type=F32).astype(BF)
        mine_ref[:, span] = sums[:keep]
        other_ref[:, span] = sums[keep:]


def project(cells, came, more, w_uv, w_out):
    whole = pl.BlockSpec(memory_space=pltpu.VMEM)
    half = jax.ShapeDtypeStruct((cells.shape[0] // 2, w_out.shape[1]), BF)
    return pl.pallas_call(
        project_kernel,
        out_shape=(half, half),
        in_specs=[whole] * 4 + [pl.BlockSpec(memory_space=pltpu.HBM)],
        out_specs=(whole, whole),
        scratch_shapes=[pltpu.VMEM(w_out.shape, BF), pltpu.SemaphoreType.DMA((4,))],
        compiler_params=pltpu.CompilerParams(vmem_limit_bytes=32 * 1024 * 1024),
        cost_estimate=pl.CostEstimate(
            flops=4 * 10**8, bytes_accessed=6 * 10**6, transcendentals=0
        ),
        name="project",
    )(cells, came, more, w_uv, w_out)


def pair_kernel(mine_ref, other_ref, out_ref):
    chips, share, width = out_ref.shape
    step = width // 4
    for first in range(0, width, step):
        span = slice(first, first + step)
        sums = mine_ref[:, span].astype(F32) + other_ref[:, span].astype(F32)
        for chip in range(chips):
            out_ref[chip, :, span] = sums[chip * share : (chip + 1) * share].astype(BF)


def pair_sum(mine, other, chips):
    whole = pl.BlockSpec(memory_space=pltpu.VMEM)
    return pl.pallas_call(
        pair_kernel,
        out_shape=jax.ShapeDtypeStruct((chips, mine.shape[0] // chips, mine.shape[1]), BF),
        in_specs=[whole] * 2,
        out_specs=whole,
        compiler_params=pltpu.CompilerParams(vmem_limit_bytes=32 * 1024 * 1024),
        cost_estimate=pl.CostEstimate(
            flops=4 * 10**5, bytes_accessed=2 * 10**6, transcendentals=0
        ),
        name="pair_sum",
    )(mine, other)


def down_kernel(*refs):
    blocks, weights, out_ref = refs[:4], refs[4:9], refs[9]
    cut = weights[2].shape[0]
    step = out_ref.shape[1] // 2
    for first in range(0, out_ref.shape[1], step):
        span = slice(first, first + step)
        sums = jnp.dot(blocks[0][...], weights[0][:, span], preferred_element_type=F32)
        for rows, weight in (
            (blocks[1][...], weights[1]),
            (blocks[2][:, :cut], weights[2]),
            (blocks[2][:, cut:], weights[3]),
            (blocks[3][...], weights[4]),
        ):
            sums = sums + jnp.dot(rows, weight[:, span], preferred_element_type=F32)
        out_ref[:, span] = sums.astype(BF)


def down_product(blocks, weights):
    whole = pl.BlockSpec(memory_space=pltpu.VMEM)
    return pl.pallas_call(
        down_kernel,
        out_shape=jax.ShapeDtypeStruct((blocks[0].shape[0], weights[0].shape[1]), BF),
        in_specs=[whole] * 9,
        out_specs=whole,
        compiler_params=pltpu.CompilerParams(vmem_limit_bytes=VMEM),
        cost_estimate=pl.CostEstimate(
            flops=10**9, bytes_accessed=5 * 10**6, transcendentals=0
        ),
        name="down_product",
    )(*blocks, *weights)


def shards(
    latent_rows,
    new_rows,
    kv_gain,
    lengths,
    owners,
    queries,
    w_uv,
    w_out,
    resid,
    moe_gain,
    route_ids,
    route_weights,
    w_gate,
    w_up,
    w_down,
):
    dp_count = lax.axis_size("dp")
    columns = lax.axis_size("expert")
    devices = dp_count * columns
    group = lax.axis_index("dp")
    column = lax.axis_index("expert")
    core = column % 2
    pre_rows, width = latent_rows.shape
    half_rope = (width - LAT) // 2
    local_units = pre_rows // UNIT
    block_units = columns * local_units
    gain = kv_gain[None, :]

    border = (MOST - 1) * UNIT
    next_rows = lax.ppermute(
        latent_rows[:border], "expert", [((i + 1) % columns, i) for i in range(columns)]
    )
    near_rows = jnp.concatenate([latent_rows, next_rows], axis=0)
    near_rows, late_group = lax.optimization_barrier((near_rows, group))
    rows = [near_rows] + [shift(near_rows, k, dp_count, "dp") for k in range(1, dp_count)]

    request_total = queries.shape[1]
    most_slots = dp_count * local_units
    near_units = local_units + MOST - 1
    where = jnp.stack([group, column]).astype(I32)
    share = request_total // columns
    slot_table_rows, request_rows, cells = tables(
        where, lengths, owners, (dp_count, columns, local_units, near_units, share)
    )
    cosine, sine = turn_table(half_rope)

    model_width = w_out.shape[1]
    piece = model_width // dp_count
    halves = (0, 1, 1, 0)
    quarters = (0, 2, 3, 1)

    def pair_perm(partner):
        perm = []
        for f in range(dp_count):
            for x in range(columns):
                g = (f - x % 2) % dp_count
                perm.append((f * columns + x, (partner(g) + x % 2) % dp_count * columns + x))
        return perm

    weight_perm = pair_perm(lambda g: g ^ 1)
    token_perm = pair_perm(lambda g: dp_count - 1 - g)
    place = (group - core + dp_count) % dp_count

    def quarter_of(g):
        return jnp.where(g == 0, 0, jnp.where(g == 1, 2, jnp.where(g == 2, 3, 1)))

    my_quarter = quarter_of(place)
    their_quarter = quarter_of(place ^ 1)

    def width_half(weight, first):
        return [
            lax.dynamic_slice_in_dim(weight[0], q * piece, piece, 0) for q in (first, first ^ 1)
        ]

    at = jnp.stack(
        [their_quarter, their_quarter ^ 1]
        + [(late_group - k + dp_count) % dp_count for k in range(1, dp_count)]
    ).astype(I32)
    gate_sent, up_sent, down_near, far_first, far_second, down_last = weight_slices(
        at, w_gate, w_up, w_down, dp_count
    )
    gate_sent, up_sent, slot_table_rows, *rows = lax.optimization_barrier(
        (gate_sent, up_sent, slot_table_rows, *rows)
    )
    gate_came = lax.ppermute(gate_sent, ("dp", "expert"), weight_perm)
    up_came = lax.ppermute(up_sent, ("dp", "expert"), weight_perm)

    attended, attended_rest = attend(
        slot_table_rows, rows, cosine, sine, gain, new_rows[0], queries[0], most_slots
    )
    unit_start, home_rank, group_start, group_rank, start_column = (
        request_rows[i] for i in range(5)
    )
    own = owners == group
    unit_len = lengths // UNIT
    members = jnp.arange(request_total, dtype=I32)

    head_share = w_uv.shape[0]
    chips = columns // 2

    def to_heads(part):
        came = lax.all_to_all(part, "expert", split_axis=0, concat_axis=0, tiled=True)
        return came.reshape((columns, head_share) + part.shape[1:])

    def spill():
        used = jnp.arange(SLOTS, most_slots, dtype=I32) < slot_table_rows[0, 4]
        rest = jnp.where(used[:, None, None], attended_rest, jnp.zeros((), BF))
        came = to_heads(rest.transpose(1, 0, 2))
        count = came.shape[2]
        member_column = group_rank // share
        member_row = (
            (member_column % 2 ^ core) * (chips * share)
            + member_column // 2 * share
            + group_rank % share
        )
        member_cell = jnp.where(home_rank >= SLOTS, start_column * count + home_rank - SLOTS, -1)
        is_row = own[None, :] & (member_row[None, :] == members[:, None])
        cell = jnp.sum(jnp.where(is_row, member_cell[None, :], 0), axis=1)
        pick = (cell[:, None] == jnp.arange(columns * count, dtype=I32)[None, :]).astype(BF)
        return jnp.stack(
            [
                jnp.dot(
                    pick, came[:, h].reshape(columns * count, LAT), preferred_element_type=F32
                ).astype(BF)
                for h in range(head_share)
            ]
        )

    more = lax.cond(
        jnp.max(home_rank) >= SLOTS,
        spill,
        lambda: jnp.zeros((head_share, request_total, LAT), BF),
    )
    by_head = to_heads(attended)
    by_head, gate_came = lax.optimization_barrier((by_head, gate_came))
    mine, other = project(cells, by_head, more, w_uv, w_out)
    mine, other, down_near, down_last = lax.optimization_barrier(
        (mine, other, down_near, down_last)
    )
    down_near = shift(down_near, 1, dp_count, "dp")
    down_last = shift(down_last, 3, dp_count, "dp")

    other = lax.ppermute(other, "expert", [(i, i ^ 1) for i in range(columns)])
    pair_sums = pair_sum(mine, other, chips)
    chip_sums = lax.all_to_all(
        pair_sums,
        "expert",
        split_axis=0,
        concat_axis=0,
        tiled=True,
        axis_index_groups=[[2 * i + c for i in range(chips)] for c in range(2)],
    )
    chip_sums, up_came, far_first = lax.optimization_barrier((chip_sums, up_came, far_first))
    far_first = shift(far_first, 2, dp_count, "dp")
    attention_out = jnp.sum(chip_sums.astype(F32), axis=0)
    residual = resid[0].astype(F32) + attention_out
    normed = (
        residual
        * lax.rsqrt(jnp.mean(residual * residual, axis=1, keepdims=True) + eps)
        * moe_gain[None, :]
    ).astype(BF)

    tokens = resid.shape[1]
    capacity = 2
    expert_ids = jnp.arange(columns, dtype=I32)
    matches = route_ids[0][:, :, None] == expert_ids[None, None, :]
    combine_weights = jnp.sum(jnp.where(matches, route_weights[0][:, :, None], 0.0), axis=1)
    routed = jnp.any(matches, axis=1)
    token_order = jnp.arange(tokens, dtype=I32)
    earlier = token_order[None, :] < token_order[:, None]
    slot_rank = jnp.sum(jnp.where(earlier[:, :, None], routed.astype(I32)[None, :, :], 0), axis=1)
    slot_ids = jnp.arange(capacity, dtype=I32)
    slot_table = routed.T[:, None, :] & (slot_rank.T[:, None, :] == slot_ids[None, :, None])
    table = slot_table.reshape(columns * capacity, tokens)
    even = (jnp.arange(columns * capacity, dtype=I32) // capacity % 2 == 0)[:, None]
    table = jnp.concatenate([table & even, table & ~even], axis=1).astype(BF)
    outgoing = []
    for f in range(dp_count):
        both = jnp.concatenate(
            [
                normed[:, q * piece : (q + 1) * piece]
                for q in (quarters[f], quarters[(f - 1) % dp_count])
            ],
            axis=0,
        )
        outgoing.append(jnp.dot(table, both, preferred_element_type=F32).astype(BF))
    outgoing = jnp.stack(outgoing).reshape(devices, capacity, piece)
    arrived = lax.all_to_all(
        outgoing, ("dp", "expert"), split_axis=0, concat_axis=0, tiled=True
    ).reshape(devices * capacity, piece)

    local_rows = local_units * UNIT
    to_rows = jnp.concatenate(
        [block[:local_rows].reshape(local_units, UNIT, width) for block in rows], axis=0
    ).transpose(1, 0, 2)
    arrived, down_near, far_first, down_last, to_rows = lax.optimization_barrier(
        (arrived, down_near, far_first, down_last, to_rows)
    )
    beside = lax.ppermute(arrived, ("dp", "expert"), token_perm)
    dealt = lax.all_to_all(to_rows, "expert", split_axis=0, concat_axis=0, tiled=True)

    gate_own, up_own = width_half(w_gate, my_quarter), width_half(w_up, my_quarter)
    weights = (gate_came, up_came, gate_own, up_own)
    first = [jnp.dot(arrived, weight[0], preferred_element_type=F32) for weight in weights]
    beside, far_second, *first = lax.optimization_barrier((beside, far_second, *first))
    gate_given, up_given, gate_sum, up_sum = (
        part + jnp.dot(beside, weight[1], preferred_element_type=F32)
        for part, weight in zip(first, weights)
    )
    given = jnp.concatenate([gate_given, up_given], axis=1).astype(BF)
    given = lax.ppermute(given, ("dp", "expert"), weight_perm).astype(F32)
    far_second = shift(far_second, 2, dp_count, "dp")
    half = gate_sum.shape[1]
    hidden = (
        jax.nn.silu(gate_sum + given[:, :half]) * (up_sum + given[:, half:])
    ).astype(BF)
    blocks = [hidden] + [shift(hidden, k, dp_count, "dp") for k in range(1, dp_count)]
    down_own = lax.dynamic_slice_in_dim(w_down[0], group * piece, piece, 1)
    blocks[0], dealt = lax.optimization_barrier((blocks[0], dealt))
    out = down_product(blocks, [down_own, down_near, far_first, far_second, down_last])
    returned = lax.all_to_all(
        out.reshape(devices, capacity, piece),
        ("dp", "expert"),
        split_axis=0,
        concat_axis=0,
        tiled=True,
    )

    slots = jnp.arange(pre_rows, dtype=I32)
    offset = slots[:, None] - group_start[None, :]
    covers = own[None, :] & (offset >= 0) & (offset < unit_len[None, :])
    slot_offset = jnp.sum(jnp.where(covers, offset, 0), axis=1)
    slot_unit = jnp.sum(jnp.where(covers, offset + unit_start[None, :], 0), axis=1)
    relative = (slot_unit // block_units - group + dp_count) % dp_count
    cache_place = (
        slot_unit % block_units // local_units * most_slots
        + relative * local_units
        + slot_unit % local_units
    )
    places = jnp.arange(columns * most_slots, dtype=I32)
    pick = (cache_place[:, None] == places[None, :]).astype(BF)
    raw_cache = jnp.dot(
        pick, dealt.reshape(columns * most_slots, width), preferred_element_type=F32
    )
    turned = []
    for table_rows in (cosine, sine):
        mine = jnp.asarray(table_rows).reshape(MOST + 1, UNIT, half_rope)
        mine = lax.dynamic_index_in_dim(mine, column, 1, keepdims=False)
        picked = mine[:1]
        for o in range(1, MOST):
            picked = jnp.where(slot_offset[:, None] == o, mine[o : o + 1], picked)
        turned.append(picked)
    cache_local = norm_rotate(raw_cache, *turned, gain)

    slot_weights = jnp.where(slot_table, combine_weights.T[:, None, :], 0.0)
    moe_sum = jnp.einsum(
        "xct,fxcd->tfd",
        slot_weights,
        returned.reshape(dp_count, columns, capacity, piece).astype(F32),
        precision=lax.Precision.HIGHEST,
    ).reshape(tokens, model_width)
    decoded = (residual + moe_sum).astype(BF)
    return (cache_local[None, None], decoded[None])


def solution(mesh):
    return jax.shard_map(
        shards,
        mesh=mesh,
        in_specs=(
            P(("dp", "expert"), None),
            P("dp", None, None),
            P(),
            P(),
            P(),
            P("dp", None, None, None),
            P("expert", None, None),
            P("expert", None),
            P("dp", "expert", None),
            P(),
            P("dp", "expert", None),
            P("dp", "expert", None),
            P("expert", None, "dp"),
            P("expert", None, "dp"),
            P("expert", "dp", None),
        ),
        out_specs=(P("dp", "expert", None, None), P("dp", "expert", None)),
        check_vma=False,
    )
```

```python
import jax
import jax.numpy as jnp
import numpy as np
from jax import lax
from jax.experimental import pallas as pl
from jax.experimental.pallas import tpu as pltpu
from jax.sharding import PartitionSpec as P

LAT = 512
UNIT = 32
MOST = 3
MAIN = 8
SLOTS = 10
PARTS = MAIN // (SLOTS - MAIN)
EXTRA = LAT // PARTS
VMEM = 58 * 1024 * 1024

eps = 1e-06
theta = 10000.0
score_scale = 192.0 ** (-0.5)
BF = jnp.bfloat16
F32 = jnp.float32
I32 = jnp.int32


def turn_table(half_width):
    exponent = -np.arange(half_width, dtype=np.float32) / np.float32(half_width)
    frequency = np.power(np.float32(theta), exponent).astype(np.float32)
    count = (MOST + 1) * UNIT
    angles = np.arange(count, dtype=np.float32)[:, None] * frequency[None, :]
    return np.cos(angles).astype(np.float32), np.sin(angles).astype(np.float32)


def norm_rotate(raw_rows, cosine, sine, kv_gain):
    raw_rows = raw_rows.astype(F32)
    latent = raw_rows[:, :LAT]
    half_width = cosine.shape[1]
    inverse = lax.rsqrt(jnp.mean(latent * latent, axis=1, keepdims=True) + eps)
    latent = latent * inverse * kv_gain
    lower = raw_rows[:, LAT : LAT + half_width]
    upper = raw_rows[:, LAT + half_width :]
    return jnp.concatenate(
        [latent, lower * cosine - upper * sine, upper * cosine + lower * sine], axis=1
    ).astype(BF)


def shift(x, step, size, axis):
    return lax.ppermute(x, axis, [((i + step) % size, i) for i in range(size)])


def table_kernel(where_ref, lengths_ref, owners_ref, slots_ref, rows_ref, cells_ref, *, sizes):
    dp_count, columns, local_units, near_units, share = sizes
    group, column = where_ref[0], where_ref[1]
    group_f, column_f = group.astype(F32), column.astype(F32)
    count = lengths_ref.shape[1]
    units = lengths_ref[...].astype(F32) * (1.0 / UNIT)
    owner = owners_ref[...].astype(F32)
    square = (count, count)
    down = lax.broadcasted_iota(I32, square, 0)
    along = lax.broadcasted_iota(I32, square, 1)
    before = down < along

    def upright(row):
        return jnp.sum(jnp.where(down == along, row, 0.0), axis=1, keepdims=True)

    def whole(x, size):
        return jnp.floor((x + 0.5) * (1.0 / size))

    units_up, owner_up = upright(units), upright(owner)
    start = jnp.sum(jnp.where(before, units_up, 0.0), axis=0, keepdims=True)
    start_source = whole(start, local_units)
    start_block = whole(start_source, columns)
    start_column = start_source - start_block * columns
    home = owner * columns + start_column
    home_up = upright(home)
    rank = jnp.sum(jnp.where(before & (home_up == home), 1.0, 0.0), axis=0, keepdims=True)
    own = owner == group_f
    own_before = before & (owner_up == group_f)
    group_start = jnp.sum(jnp.where(own_before, units_up, 0.0), axis=0, keepdims=True)
    group_rank = jnp.sum(jnp.where(own_before, 1.0, 0.0), axis=0, keepdims=True)

    lines = slots_ref.shape[0]
    line = lax.broadcasted_iota(I32, (lines, count), 0).astype(F32)
    here = home == group_f * columns + column_f
    is_slot = here & (rank == line)
    block = start_block - group_f
    block = jnp.where(block < 0.0, block + dp_count, block)
    place = block * near_units + (start - start_source * local_units)

    def pick(row):
        return jnp.sum(jnp.where(is_slot, row, 0.0), axis=1, keepdims=True)

    near = lax.broadcasted_iota(I32, (lines, 1), 0).astype(F32)
    near_block = whole(near, near_units)
    near_unit = near - near_block * near_units + column_f * local_units
    near_block = near_block + group_f
    near_block = jnp.where(near_block >= dp_count, near_block - dp_count, near_block)
    near_unit = near_unit + near_block * (columns * local_units)
    near_start = jnp.max(jnp.where(start <= near_unit, start, 0.0), axis=1, keepdims=True)
    near_offset = jnp.minimum(near_unit - near_start, MOST - 1.0)
    number = jnp.sum(jnp.where(here, 1.0, 0.0), axis=1, keepdims=True)
    lane = lax.broadcasted_iota(I32, slots_ref.shape, 1)
    packed = jnp.zeros(slots_ref.shape, F32)
    wraps = jnp.where(jnp.full((1, 1), column, I32) == columns - 1, 1.0, 0.0)
    values = (pick(place), pick(units), pick(group_rank), near_offset, number, wraps)
    for i, value in enumerate(values):
        packed = jnp.where(lane == i, value, packed)
    slots_ref[...] = packed.astype(I32)
    rows_ref[...] = jnp.concatenate(
        [start, rank, group_start, group_rank, start_column] + [start] * 3, axis=0
    ).astype(I32)

    member_column = whole(group_rank, share)
    member_chip = whole(member_column, 2)
    other_core = jnp.abs(member_column - 2.0 * member_chip - (column % 2).astype(F32))
    row = (other_core * (columns // 2) + member_chip) * share + (
        group_rank - member_column * share
    )
    lines = cells_ref.shape[0]
    line = lax.broadcasted_iota(I32, (lines, count), 0).astype(F32)
    first_row = start_column * MAIN
    main = jnp.where(rank < MAIN, first_row + rank, -1.0 * MAIN)
    extra = jnp.where(
        (rank >= MAIN) & (rank < SLOTS), first_row + (rank - MAIN) * PARTS, -1.0 * MAIN
    )
    found = [
        jnp.sum(jnp.where(own & (row == line), cell, 0.0), axis=1, keepdims=True)
        for cell in (main, extra)
    ]
    lane = lax.broadcasted_iota(I32, cells_ref.shape, 1)
    cells_ref[...] = jnp.where(lane == 0, found[0], found[1]).astype(I32)


def tables(where, lengths, owners, sizes):
    lines = sizes[0] * sizes[3]
    whole = pl.BlockSpec(memory_space=pltpu.VMEM)

    def body(*refs):
        table_kernel(*refs, sizes=sizes)

    return pl.pallas_call(
        body,
        out_shape=(
            jax.ShapeDtypeStruct((lines, 128), I32),
            jax.ShapeDtypeStruct((8, lengths.shape[0]), I32),
            jax.ShapeDtypeStruct((sizes[1] * sizes[4], 128), I32),
        ),
        in_specs=[pl.BlockSpec(memory_space=pltpu.SMEM), whole, whole],
        out_specs=(whole, whole, whole),
        compiler_params=pltpu.CompilerParams(vmem_limit_bytes=32 * 1024 * 1024),
        cost_estimate=pl.CostEstimate(flops=1000, bytes_accessed=4096, transcendentals=0),
        name="tables",
    )(where, lengths[None, :], owners[None, :])


def slice_kernel(at_ref, gate_ref, up_ref, down_ref, gate_out, up_out, *refs):
    downs, sems = refs[:-1], refs[-1]
    piece = gate_out.shape[1]
    copies = []
    for weight, out in ((gate_ref, gate_out), (up_ref, up_out)):
        for i in range(2):
            rows = pl.ds(pl.multiple_of(at_ref[i] * piece, 128), piece)
            copies.append((weight.at[0, rows, :], out.at[i]))
    for i, outs in enumerate((downs[:1], downs[1:3], downs[3:])):
        columns = pl.ds(pl.multiple_of(at_ref[2 + i] * piece, 128), piece)
        first = 0
        for out in outs:
            copies.append((down_ref.at[0, pl.ds(first, out.shape[0]), columns], out))
            first += out.shape[0]
    copies = [
        pltpu.make_async_copy(source, target, sems.at[i])
        for i, (source, target) in enumerate(copies)
    ]
    for copy in copies:
        copy.start()
    for copy in copies:
        copy.wait()


def weight_slices(at, w_gate, w_up, w_down, dp_count):
    piece = w_gate.shape[1] // dp_count
    away = pl.BlockSpec(memory_space=pltpu.HBM)
    whole = pl.BlockSpec(memory_space=pltpu.VMEM)
    halves = jax.ShapeDtypeStruct((2, piece, w_gate.shape[2]), BF)
    part = jax.ShapeDtypeStruct((w_down.shape[1], piece), BF)
    cut = jax.ShapeDtypeStruct((w_down.shape[1] // 2, piece), BF)
    return pl.pallas_call(
        slice_kernel,
        out_shape=(halves, halves, part, cut, cut, part),
        in_specs=[pl.BlockSpec(memory_space=pltpu.SMEM)] + [away] * 3,
        out_specs=(whole,) * 6,
        scratch_shapes=[pltpu.SemaphoreType.DMA((8,))],
        compiler_params=pltpu.CompilerParams(vmem_limit_bytes=VMEM),
        cost_estimate=pl.CostEstimate(flops=1000, bytes_accessed=4096, transcendentals=0),
        name="weight_slices",
    )(at, w_gate, w_up, w_down)


def attend_kernel(slots_ref, *refs, blocks):
    rows_in = refs[:blocks]
    cos_ref, sin_ref, gain_ref, new_ref, query_ref = refs[blocks : blocks + 5]
    out_ref, rest_ref, keys, query, fresh, held_out, spare, sems, spare_sem = refs[blocks + 5 :]
    number = slots_ref[0, 4]

    def fetch(slot):
        return pltpu.make_async_copy(
            query_ref.at[slots_ref[slot, 2]], query.at[slot], sems.at[slot]
        )

    @pl.loop(0, number)
    def _(slot):
        fetch(slot).start()

    gain = gain_ref[...]
    local_rows = rows_in[0].shape[0] - (MOST - 1) * UNIT
    near_units = rows_in[0].shape[0] // UNIT
    for block, ref in enumerate(rows_in):
        before = near_units * ((block + blocks - 1) % blocks - block)
        for first in range(0, ref.shape[0], UNIT):
            unit = block * near_units + first // UNIT
            if first >= local_rows:
                unit = unit + slots_ref[0, 5] * before
            span = pl.ds(pl.multiple_of(slots_ref[unit, 3] * UNIT, UNIT), UNIT)
            keys[pl.ds(pl.multiple_of(unit * UNIT, UNIT), UNIT), :] = norm_rotate(
                ref[first : first + UNIT, :], cos_ref[span, :], sin_ref[span, :], gain
            )
    fresh[...] = new_ref[...].astype(F32)

    heads = out_ref.shape[0]
    sent = SLOTS
    window = MOST * UNIT
    lanes = window + UNIT
    lane = lax.broadcasted_iota(I32, (heads, lanes), 1)

    def one(slot):
        count = slots_ref[slot, 1]
        own = keys[pl.ds(pl.multiple_of(slots_ref[slot, 0] * UNIT, UNIT), window), :]
        at = pl.ds(count * UNIT, 1)
        new = norm_rotate(
            fresh[pl.ds(slots_ref[slot, 2], 1), :], cos_ref[at, :], sin_ref[at, :], gain
        )
        new = jnp.broadcast_to(new.astype(F32), (UNIT, own.shape[1])).astype(BF)
        held = jnp.concatenate([own, new], axis=0)
        scores = (
            lax.dot_general(
                query[slot], held, (((1,), (1,)), ((), ())), preferred_element_type=F32
            )
            * score_scale
        )
        live = (lane < count * UNIT) | (lane == window)
        scores = jnp.where(live, scores, -jnp.inf)
        weights = jnp.exp(scores - jnp.max(scores, axis=1, keepdims=True))
        total = jnp.sum(weights, axis=1, keepdims=True)
        mixture = jnp.dot(weights.astype(BF), held[:, :LAT], preferred_element_type=F32)
        return mixture / total

    @pl.loop(0, number)
    def _(slot):
        fetch(slot).wait()

    for slot in range(sent):
        value = jnp.where(slot < number, one(slot), 0.0)
        if slot < MAIN:
            held_out[slot, :, :LAT] = value
        for i in range(PARTS if slot >= MAIN else 0):
            held_out[(slot - MAIN) * PARTS + i, :, LAT:] = value[:, i * EXTRA : (i + 1) * EXTRA]

    out_ref[...] = jnp.swapaxes(held_out[...], 0, 1).astype(BF)

    @pl.loop(sent, number)
    def _(slot):
        spare[...] = one(slot).astype(BF)
        copy = pltpu.make_async_copy(spare, rest_ref.at[slot - sent], spare_sem)
        copy.start()
        copy.wait()


def attend(slots, rows, cosine, sine, gain, new_rows, queries, most_slots):
    heads = queries.shape[1]
    blocks = len(rows)
    total_rows = sum(block.shape[0] for block in rows)
    whole = pl.BlockSpec(memory_space=pltpu.VMEM)

    def body(*refs):
        attend_kernel(*refs, blocks=blocks)

    return pl.pallas_call(
        body,
        out_shape=(
            jax.ShapeDtypeStruct((heads, MAIN, LAT + EXTRA), BF),
            jax.ShapeDtypeStruct((most_slots - SLOTS, heads, LAT), BF),
        ),
        in_specs=[pl.BlockSpec(memory_space=pltpu.SMEM)]
        + [whole] * (blocks + 4)
        + [pl.BlockSpec(memory_space=pltpu.HBM)],
        out_specs=(whole, pl.BlockSpec(memory_space=pltpu.HBM)),
        scratch_shapes=[
            pltpu.VMEM((total_rows, queries.shape[2]), BF),
            pltpu.VMEM((most_slots,) + queries.shape[1:], BF),
            pltpu.VMEM(new_rows.shape, F32),
            pltpu.VMEM((MAIN, heads, LAT + EXTRA), F32),
            pltpu.VMEM((heads, LAT), BF),
            pltpu.SemaphoreType.DMA((most_slots,)),
            pltpu.SemaphoreType.DMA,
        ],
        compiler_params=pltpu.CompilerParams(vmem_limit_bytes=VMEM),
        cost_estimate=pl.CostEstimate(
            flops=10**8, bytes_accessed=4 * 10**6, transcendentals=10**5
        ),
        name="attend",
    )(slots, *rows, cosine, sine, gain, new_rows, queries)


def project_kernel(
    cells_ref, came_ref, more_ref, uv_ref, weight_ref, mine_ref, other_ref, weight, sems
):
    step = weight.shape[1] // 4
    spans = [slice(i * step, (i + 1) * step) for i in range(4)]
    copies = [
        pltpu.make_async_copy(weight_ref.at[:, span], weight.at[:, span], sems.at[i])
        for i, span in enumerate(spans)
    ]
    for copy in copies:
        copy.start()
    requests = cells_ref.shape[0]
    sources, heads, slots, _ = came_ref.shape
    cells = sources * slots
    cell = lax.broadcasted_iota(I32, (requests, cells), 1)

    def pick(at):
        return jnp.where(at == cell, 1.0, 0.0).astype(BF)

    main = pick(cells_ref[:, :1])
    extra = [pick(cells_ref[:, 1:2] + i) for i in range(PARTS)]
    projected = []
    for h in range(heads):
        came = came_ref[:, h].astype(F32).reshape(cells, LAT + EXTRA).astype(BF)
        rows = jnp.dot(main, came[:, :LAT], preferred_element_type=F32)
        rest = [jnp.dot(part, came[:, LAT:], preferred_element_type=F32) for part in extra]
        rows = rows + jnp.concatenate(rest, axis=1) + more_ref[h].astype(F32)
        projected.append(
            jnp.dot(rows.astype(BF), uv_ref[h], preferred_element_type=F32).astype(BF)
        )
    projected = jnp.concatenate(projected, axis=1)
    keep = mine_ref.shape[0]
    for span, copy in zip(spans, copies):
        copy.wait()
        sums = jnp.dot(projected, weight[:, span], preferred_element_type=F32).astype(BF)
        mine_ref[:, span] = sums[:keep]
        other_ref[:, span] = sums[keep:]


def project(cells, came, more, w_uv, w_out):
    whole = pl.BlockSpec(memory_space=pltpu.VMEM)
    half = jax.ShapeDtypeStruct((cells.shape[0] // 2, w_out.shape[1]), BF)
    return pl.pallas_call(
        project_kernel,
        out_shape=(half, half),
        in_specs=[whole] * 4 + [pl.BlockSpec(memory_space=pltpu.HBM)],
        out_specs=(whole, whole),
        scratch_shapes=[pltpu.VMEM(w_out.shape, BF), pltpu.SemaphoreType.DMA((4,))],
        compiler_params=pltpu.CompilerParams(vmem_limit_bytes=32 * 1024 * 1024),
        cost_estimate=pl.CostEstimate(
            flops=4 * 10**8, bytes_accessed=6 * 10**6, transcendentals=0
        ),
        name="project",
    )(cells, came, more, w_uv, w_out)


def pair_kernel(mine_ref, other_ref, out_ref):
    chips, share, width = out_ref.shape
    step = width // 4
    for first in range(0, width, step):
        span = slice(first, first + step)
        sums = mine_ref[:, span].astype(F32) + other_ref[:, span].astype(F32)
        for chip in range(chips):
            out_ref[chip, :, span] = sums[chip * share : (chip + 1) * share].astype(BF)


def pair_sum(mine, other, chips):
    whole = pl.BlockSpec(memory_space=pltpu.VMEM)
    return pl.pallas_call(
        pair_kernel,
        out_shape=jax.ShapeDtypeStruct((chips, mine.shape[0] // chips, mine.shape[1]), BF),
        in_specs=[whole] * 2,
        out_specs=whole,
        compiler_params=pltpu.CompilerParams(vmem_limit_bytes=32 * 1024 * 1024),
        cost_estimate=pl.CostEstimate(
            flops=4 * 10**5, bytes_accessed=2 * 10**6, transcendentals=0
        ),
        name="pair_sum",
    )(mine, other)


def shards(
    latent_rows,
    new_rows,
    kv_gain,
    lengths,
    owners,
    queries,
    w_uv,
    w_out,
    resid,
    moe_gain,
    route_ids,
    route_weights,
    w_gate,
    w_up,
    w_down,
):
    dp_count = lax.axis_size("dp")
    columns = lax.axis_size("expert")
    devices = dp_count * columns
    group = lax.axis_index("dp")
    column = lax.axis_index("expert")
    core = column % 2
    pre_rows, width = latent_rows.shape
    half_rope = (width - LAT) // 2
    local_units = pre_rows // UNIT
    block_units = columns * local_units
    gain = kv_gain[None, :]

    border = (MOST - 1) * UNIT
    next_rows = lax.ppermute(
        latent_rows[:border], "expert", [((i + 1) % columns, i) for i in range(columns)]
    )
    near_rows = jnp.concatenate([latent_rows, next_rows], axis=0)
    near_rows, late_group = lax.optimization_barrier((near_rows, group))
    rows = [near_rows] + [shift(near_rows, k, dp_count, "dp") for k in range(1, dp_count)]

    request_total = queries.shape[1]
    most_slots = dp_count * local_units
    near_units = local_units + MOST - 1
    where = jnp.stack([group, column]).astype(I32)
    share = request_total // columns
    slot_table_rows, request_rows, cells = tables(
        where, lengths, owners, (dp_count, columns, local_units, near_units, share)
    )
    cosine, sine = turn_table(half_rope)

    model_width = w_out.shape[1]
    piece = model_width // dp_count
    halves = (0, 1, 1, 0)
    quarters = (0, 2, 3, 1)

    def pair_perm(partner):
        perm = []
        for f in range(dp_count):
            for x in range(columns):
                g = (f - x % 2) % dp_count
                perm.append((f * columns + x, (partner(g) + x % 2) % dp_count * columns + x))
        return perm

    weight_perm = pair_perm(lambda g: g ^ 1)
    token_perm = pair_perm(lambda g: dp_count - 1 - g)
    place = (group - core + dp_count) % dp_count

    def quarter_of(g):
        return jnp.where(g == 0, 0, jnp.where(g == 1, 2, jnp.where(g == 2, 3, 1)))

    my_quarter = quarter_of(place)
    their_quarter = quarter_of(place ^ 1)

    def width_half(weight, first):
        return [
            lax.dynamic_slice_in_dim(weight[0], q * piece, piece, 0) for q in (first, first ^ 1)
        ]

    at = jnp.stack(
        [their_quarter, their_quarter ^ 1]
        + [(late_group - k + dp_count) % dp_count for k in range(1, dp_count)]
    ).astype(I32)
    gate_sent, up_sent, down_near, far_first, far_second, down_last = weight_slices(
        at, w_gate, w_up, w_down, dp_count
    )
    gate_sent, up_sent, slot_table_rows, *rows = lax.optimization_barrier(
        (gate_sent, up_sent, slot_table_rows, *rows)
    )
    gate_came = lax.ppermute(gate_sent, ("dp", "expert"), weight_perm)
    up_came = lax.ppermute(up_sent, ("dp", "expert"), weight_perm)

    attended, attended_rest = attend(
        slot_table_rows, rows, cosine, sine, gain, new_rows[0], queries[0], most_slots
    )
    unit_start, home_rank, group_start, group_rank, start_column = (
        request_rows[i] for i in range(5)
    )
    own = owners == group
    unit_len = lengths // UNIT
    members = jnp.arange(request_total, dtype=I32)

    head_share = w_uv.shape[0]
    chips = columns // 2

    def to_heads(part):
        came = lax.all_to_all(part, "expert", split_axis=0, concat_axis=0, tiled=True)
        return came.reshape((columns, head_share) + part.shape[1:])

    def spill():
        used = jnp.arange(SLOTS, most_slots, dtype=I32) < slot_table_rows[0, 4]
        rest = jnp.where(used[:, None, None], attended_rest, jnp.zeros((), BF))
        came = to_heads(rest.transpose(1, 0, 2))
        count = came.shape[2]
        member_column = group_rank // share
        member_row = (
            (member_column % 2 ^ core) * (chips * share)
            + member_column // 2 * share
            + group_rank % share
        )
        member_cell = jnp.where(home_rank >= SLOTS, start_column * count + home_rank - SLOTS, -1)
        is_row = own[None, :] & (member_row[None, :] == members[:, None])
        cell = jnp.sum(jnp.where(is_row, member_cell[None, :], 0), axis=1)
        pick = (cell[:, None] == jnp.arange(columns * count, dtype=I32)[None, :]).astype(BF)
        return jnp.stack(
            [
                jnp.dot(
                    pick, came[:, h].reshape(columns * count, LAT), preferred_element_type=F32
                ).astype(BF)
                for h in range(head_share)
            ]
        )

    more = lax.cond(
        jnp.max(home_rank) >= SLOTS,
        spill,
        lambda: jnp.zeros((head_share, request_total, LAT), BF),
    )
    by_head = to_heads(attended)
    by_head, gate_came = lax.optimization_barrier((by_head, gate_came))
    mine, other = project(cells, by_head, more, w_uv, w_out)
    mine, other, down_near, down_last = lax.optimization_barrier(
        (mine, other, down_near, down_last)
    )
    down_near = shift(down_near, 1, dp_count, "dp")
    down_last = shift(down_last, 3, dp_count, "dp")

    other = lax.ppermute(other, "expert", [(i, i ^ 1) for i in range(columns)])
    pair_sums = pair_sum(mine, other, chips)
    chip_sums = lax.all_to_all(
        pair_sums,
        "expert",
        split_axis=0,
        concat_axis=0,
        tiled=True,
        axis_index_groups=[[2 * i + c for i in range(chips)] for c in range(2)],
    )
    chip_sums, up_came, far_first = lax.optimization_barrier((chip_sums, up_came, far_first))
    far_first = shift(far_first, 2, dp_count, "dp")
    attention_out = jnp.sum(chip_sums.astype(F32), axis=0)
    residual = resid[0].astype(F32) + attention_out
    normed = (
        residual
        * lax.rsqrt(jnp.mean(residual * residual, axis=1, keepdims=True) + eps)
        * moe_gain[None, :]
    ).astype(BF)

    tokens = resid.shape[1]
    capacity = 2
    expert_ids = jnp.arange(columns, dtype=I32)
    matches = route_ids[0][:, :, None] == expert_ids[None, None, :]
    combine_weights = jnp.sum(jnp.where(matches, route_weights[0][:, :, None], 0.0), axis=1)
    routed = jnp.any(matches, axis=1)
    token_order = jnp.arange(tokens, dtype=I32)
    earlier = token_order[None, :] < token_order[:, None]
    slot_rank = jnp.sum(jnp.where(earlier[:, :, None], routed.astype(I32)[None, :, :], 0), axis=1)
    slot_ids = jnp.arange(capacity, dtype=I32)
    slot_table = routed.T[:, None, :] & (slot_rank.T[:, None, :] == slot_ids[None, :, None])
    table = slot_table.reshape(columns * capacity, tokens)
    even = (jnp.arange(columns * capacity, dtype=I32) // capacity % 2 == 0)[:, None]
    table = jnp.concatenate([table & even, table & ~even], axis=1).astype(BF)
    outgoing = []
    for f in range(dp_count):
        both = jnp.concatenate(
            [
                normed[:, q * piece : (q + 1) * piece]
                for q in (quarters[f], quarters[(f - 1) % dp_count])
            ],
            axis=0,
        )
        outgoing.append(jnp.dot(table, both, preferred_element_type=F32).astype(BF))
    outgoing = jnp.stack(outgoing).reshape(devices, capacity, piece)
    arrived = lax.all_to_all(
        outgoing, ("dp", "expert"), split_axis=0, concat_axis=0, tiled=True
    ).reshape(devices * capacity, piece)

    local_rows = local_units * UNIT
    to_rows = jnp.concatenate(
        [block[:local_rows].reshape(local_units, UNIT, width) for block in rows], axis=0
    ).transpose(1, 0, 2)
    arrived, down_near, far_first, down_last, to_rows = lax.optimization_barrier(
        (arrived, down_near, far_first, down_last, to_rows)
    )
    beside = lax.ppermute(arrived, ("dp", "expert"), token_perm)
    dealt = lax.all_to_all(to_rows, "expert", split_axis=0, concat_axis=0, tiled=True)

    gate_own, up_own = width_half(w_gate, my_quarter), width_half(w_up, my_quarter)
    weights = (gate_came, up_came, gate_own, up_own)
    first = [jnp.dot(arrived, weight[0], preferred_element_type=F32) for weight in weights]
    beside, far_second, *first = lax.optimization_barrier((beside, far_second, *first))
    gate_given, up_given, gate_sum, up_sum = (
        part + jnp.dot(beside, weight[1], preferred_element_type=F32)
        for part, weight in zip(first, weights)
    )
    given = jnp.concatenate([gate_given, up_given], axis=1).astype(BF)
    given = lax.ppermute(given, ("dp", "expert"), weight_perm).astype(F32)
    far_second = shift(far_second, 2, dp_count, "dp")
    half = gate_sum.shape[1]
    hidden = (
        jax.nn.silu(gate_sum + given[:, :half]) * (up_sum + given[:, half:])
    ).astype(BF)
    near, far, last = (shift(hidden, k, dp_count, "dp") for k in range(1, dp_count))
    cut = far_first.shape[0]
    hidden_all = jnp.concatenate([hidden, near, last, far[:, :cut]], axis=1)
    hidden_all, dealt = lax.optimization_barrier((hidden_all, dealt))
    down_own = lax.dynamic_slice_in_dim(w_down[0], group * piece, piece, 1)
    downs = jnp.concatenate([down_own, down_near, down_last, far_first], axis=0)
    out = jnp.dot(hidden_all, downs, preferred_element_type=F32)
    out = out + jnp.dot(far[:, cut:], far_second, preferred_element_type=F32)
    returned = lax.all_to_all(
        out.astype(BF).reshape(devices, capacity, piece),
        ("dp", "expert"),
        split_axis=0,
        concat_axis=0,
        tiled=True,
    )

    slots = jnp.arange(pre_rows, dtype=I32)
    offset = slots[:, None] - group_start[None, :]
    covers = own[None, :] & (offset >= 0) & (offset < unit_len[None, :])
    slot_offset = jnp.sum(jnp.where(covers, offset, 0), axis=1)
    slot_unit = jnp.sum(jnp.where(covers, offset + unit_start[None, :], 0), axis=1)
    relative = (slot_unit // block_units - group + dp_count) % dp_count
    cache_place = (
        slot_unit % block_units // local_units * most_slots
        + relative * local_units
        + slot_unit % local_units
    )
    places = jnp.arange(columns * most_slots, dtype=I32)
    pick = (cache_place[:, None] == places[None, :]).astype(BF)
    raw_cache = jnp.dot(
        pick, dealt.reshape(columns * most_slots, width), preferred_element_type=F32
    )
    turned = []
    for table_rows in (cosine, sine):
        mine = jnp.asarray(table_rows).reshape(MOST + 1, UNIT, half_rope)
        mine = lax.dynamic_index_in_dim(mine, column, 1, keepdims=False)
        picked = mine[:1]
        for o in range(1, MOST):
            picked = jnp.where(slot_offset[:, None] == o, mine[o : o + 1], picked)
        turned.append(picked)
    cache_local = norm_rotate(raw_cache, *turned, gain)

    slot_weights = jnp.where(slot_table, combine_weights.T[:, None, :], 0.0)
    moe_sum = jnp.einsum(
        "xct,fxcd->tfd",
        slot_weights,
        returned.reshape(dp_count, columns, capacity, piece).astype(F32),
        precision=lax.Precision.HIGHEST,
    ).reshape(tokens, model_width)
    decoded = (residual + moe_sum).astype(BF)
    return (cache_local[None, None], decoded[None])


def solution(mesh):
    return jax.shard_map(
        shards,
        mesh=mesh,
        in_specs=(
            P(("dp", "expert"), None),
            P("dp", None, None),
            P(),
            P(),
            P(),
            P("dp", None, None, None),
            P("expert", None, None),
            P("expert", None),
            P("dp", "expert", None),
            P(),
            P("dp", "expert", None),
            P("dp", "expert", None),
            P("expert", None, "dp"),
            P("expert", None, "dp"),
            P("expert", "dp", None),
        ),
        out_specs=(P("dp", "expert", None, None), P("dp", "expert", None)),
        check_vma=False,
    )
```
